128 devices in a mesh: blk: 128 (over y, x, z, core).
Axes of the slice: x: 4, y: 4, z: 4, core: 2. Of those that a mesh axis runs over, the one named last changes fastest.
Arguments:
- old_phase: float32 [2048, 32768], P('blk'), may hold values from -1 to 1
- old_solute: float32 [2048, 32768], P('blk'), may hold values from -0.45 to 0.45
- old_mobility: float32 [2048, 32768], P('blk'), may hold values from 0.25 to 1
- new_global_slot: int32 [2048], P('blk'), may hold values from -1 to 1023, as said below
- neighbors: int32 [1024, 6], P('blk'), may hold values from -1 to 1023, as said below
Outputs:
- phase: float32 [1024, 32768], P('blk')
- solute: float32 [1024, 32768], P('blk')
The draws below stay inside these ranges and needn't reach their ends.
Inputs may be any that keep to these rules, and one draw needn't show every extreme that they name: Each device's old slots hold its blocks first and -1 after them; the blocks taken in device order and slot order get the consecutive numbers 0 to 1023. The block in an old slot of device p goes to device new_global_slot // 8, at most 2 devices away; in every draw some block moves exactly 2 devices down and some exactly 2 up, some device holds 16 blocks and some none. `neighbors`: the relation is symmetric: if b is the +x (+y, +z) neighbour of a, then a is the -x (-y, -z) neighbour of b. The x neighbours of a block of device p lie on devices p - 1 and p + 1 (every block has both except on the first and last device, where that side is -1); y and z neighbours lie on the block's own device, with -1 at the ends along y and none along z (a block may be its own z neighbour). The layers of blocks line up: if b is the -x (+x) neighbour of a, then the y and z neighbours of b are the -x (+x) neighbours of the y and z neighbours of a, and -1 where those are -1.
All inputs are finite; a program needn't handle non-finite values.
Results may differ from the reference program's by a relative error of at most 0.00014.
Values sent between devices are 32-bit elements; how exact they have to be, the bound alone decides.
No kernel may reach another device: no remote copies, remote signals or barrier semaphores. Data moves between devices by JAX's collectives and lax.ppermute only.
A program may use at most 128 MiB of HBM per device.

```python
import math
import jax
import jax.numpy as jnp
from jax import lax

BLOCK_EDGE_CELLS = 32
BLOCK_CELLS = 32768
FACE_CELLS = 1024
CAP = 8
SPREAD = 2
STEPS = 3
ACTIVE_BLOCKS = 1024
NOLD = 2048
N_BLK = 128


def draw_old_phase(key, part):
    cell_ids = jnp.arange(BLOCK_CELLS)
    xs = (cell_ids // FACE_CELLS).astype(jnp.float32)
    ys = (cell_ids // BLOCK_EDGE_CELLS % BLOCK_EDGE_CELLS).astype(jnp.float32)
    zs = (cell_ids % BLOCK_EDGE_CELLS).astype(jnp.float32)
    middle = (BLOCK_EDGE_CELLS - 1) / 2.0
    inverse_width = 1.0 / (math.sqrt(2.0) * BLOCK_EDGE_CELLS / 8.0)
    rough = jax.random.uniform(jax.random.fold_in(key, 31), (NOLD, BLOCK_CELLS), jnp.float32, -1.0, 1.0)
    azimuth = jax.random.uniform(jax.random.fold_in(key, 34), (NOLD, 1), jnp.float32, 0.0, 2.0 * math.pi)
    polar = jax.random.uniform(jax.random.fold_in(key, 35), (NOLD, 1), jnp.float32, 0.0, math.pi)
    shift_along = jax.random.uniform(jax.random.fold_in(key, 36), (NOLD, 1), jnp.float32, -BLOCK_EDGE_CELLS / 4.0, BLOCK_EDGE_CELLS / 4.0)
    normal_x = jnp.cos(azimuth) * jnp.sin(polar)
    normal_y = jnp.sin(azimuth) * jnp.sin(polar)
    normal_z = jnp.cos(polar)
    distance = normal_x * (xs[None, :] - middle) + normal_y * (ys[None, :] - middle) + normal_z * (zs[None, :] - middle) - shift_along
    phase = 0.92 * jnp.tanh(distance * inverse_width) + 0.08 * rough
    return phase.astype(jnp.float32)


def draw_new_global_slot(key, part):
    groups = N_BLK // (2 * SPREAD)
    depth = jax.random.randint(jax.random.fold_in(key, 1), (groups, SPREAD), 0, CAP + 1)
    flips = jax.random.randint(jax.random.fold_in(key, 2), (groups,), 0, 2)
    first = jax.random.randint(jax.random.fold_in(key, 3), (), 0, groups - 1)
    second = groups - 1
    group_ids = jnp.arange(groups)
    forced = (group_ids == first) | (group_ids == second)
    depth = jnp.where(forced[:, None], CAP, depth)
    flips = jnp.where(group_ids == first, 0, jnp.where(group_ids == second, 1, flips))
    signs = 1 - 2 * flips
    lower = CAP - signs[:, None] * depth
    upper = CAP + signs[:, None] * depth[:, ::-1]
    counts = jnp.concatenate([lower, upper], axis=1).reshape(N_BLK)
    starts = jnp.cumsum(counts) - counts
    slot_ids = jnp.arange(2 * CAP)
    result = jnp.where(slot_ids[None, :] < counts[:, None], starts[:, None] + slot_ids[None, :], -1)
    return result.reshape(NOLD).astype(jnp.int32)


def device_perms(key):
    return jax.vmap(lambda sub: jax.random.permutation(sub, CAP))(jax.random.split(key, N_BLK))


def draw_neighbors(key, part):
    columns = max(1, min(2, CAP // 2))
    rows_y = CAP // columns
    dev_ids = jnp.arange(N_BLK)[:, None]
    position = device_perms(jax.random.fold_in(key, 11))
    inverse = jnp.argsort(position, axis=1)
    prev_inverse = jnp.concatenate([inverse[:1], inverse[:-1]], axis=0)
    next_inverse = jnp.concatenate([inverse[1:], inverse[-1:]], axis=0)
    row_pos = position // columns
    col_pos = position % columns
    minus_x = jnp.where(dev_ids > 0, (dev_ids - 1) * CAP + jnp.take_along_axis(prev_inverse, position, axis=1), -1)
    plus_x = jnp.where(dev_ids < N_BLK - 1, (dev_ids + 1) * CAP + jnp.take_along_axis(next_inverse, position, axis=1), -1)
    here = dev_ids * CAP
    minus_y = jnp.where(row_pos > 0, here + jnp.take_along_axis(inverse, jnp.clip(position - columns, 0, CAP - 1), axis=1), -1)
    plus_y = jnp.where(row_pos < rows_y - 1, here + jnp.take_along_axis(inverse, jnp.clip(position + columns, 0, CAP - 1), axis=1), -1)
    minus_z = here + jnp.take_along_axis(inverse, row_pos * columns + (col_pos + columns - 1) % columns, axis=1)
    plus_z = here + jnp.take_along_axis(inverse, row_pos * columns + (col_pos + 1) % columns, axis=1)
    lookup_table = jnp.stack([minus_x, plus_x, minus_y, plus_y, minus_z, plus_z], axis=-1)
    return lookup_table.reshape(ACTIVE_BLOCKS, 6).astype(jnp.int32)


def shard_levels(own_key, shape, pieces, least, largest):
    factor_of, own = 1.0, jax.random.fold_in(own_key, 6)
    for dim, blocks in pieces:
        heights = jnp.exp(jax.random.uniform(jax.random.fold_in(own, dim), (blocks,), jnp.float32, least / len(pieces), largest / len(pieces)))
        factor_of = factor_of * jnp.repeat(heights, shape[dim] // blocks).reshape([-1 if axis == dim else 1 for axis in range(len(shape))])
    return factor_of


def noise(own_key, extent, width, limit, pieces=(), held_as=jnp.bfloat16):
    factor_of = shard_levels(own_key, extent, pieces, -0.22, 0.18) if pieces else 1.0
    array = jax.random.normal(own_key, extent, jnp.float32) * width * factor_of
    return jnp.minimum(jnp.maximum(array, -limit), limit).astype(held_as)


def setup_inputs(seed: int = 0) -> dict:
    key_of = jax.random.split(jax.random.key(seed), 6)
    return {
        "old_phase": draw_old_phase(jax.random.fold_in(key_of[5], 71), 0),
        "old_solute": noise(key_of[1], (NOLD, BLOCK_CELLS), 0.15, 0.45, ((0, 128),), jnp.float32),
        "old_mobility": jnp.clip(jnp.exp(math.log(1.0) - 1.3862944 * jax.random.uniform(key_of[2], (NOLD, BLOCK_CELLS), jnp.float32) ** shard_levels(key_of[2], (NOLD, BLOCK_CELLS), ((0, 128),), -0.2, 0.2)), 0.25, 1.0),
        "new_global_slot": draw_new_global_slot(jax.random.fold_in(key_of[5], 71), 0),
        "neighbors": draw_neighbors(jax.random.fold_in(key_of[5], 71), 0),
    }


time_step = 0.15
coupling = 1.5


def block_faces(field_arrays):
    edge = field_arrays.shape[2]
    low_x = field_arrays[:, :, 0, :]
    high_x = field_arrays[:, :, edge - 1, :]
    low_y = field_arrays[:, :, :, :edge]
    high_y = field_arrays[:, :, :, -edge:]
    low_z = field_arrays[:, :, :, 0::edge]
    high_z = field_arrays[:, :, :, edge - 1::edge]
    return low_x, high_x, low_y, high_y, low_z, high_z


def pick_face(other, own, index):
    valid = index >= 0
    taken = jnp.take(other, jnp.maximum(index, 0), axis=0)
    return jnp.where(valid.reshape((-1,) + (1,) * (own.ndim - 1)), taken, own)


def laplacian(field_arrays, ghosts):
    minus_x, plus_x, minus_y, plus_y, minus_z, plus_z = ghosts
    edge = field_arrays.shape[2]
    flat_ids = jnp.arange(field_arrays.shape[3], dtype=jnp.int32)
    y_ids = flat_ids // edge
    z_ids = flat_ids % edge
    prev_x = jnp.concatenate([minus_x[:, :, None, :], field_arrays[:, :, :-1, :]], axis=2)
    next_x = jnp.concatenate([field_arrays[:, :, 1:, :], plus_x[:, :, None, :]], axis=2)
    zero_row = jnp.zeros(field_arrays.shape[:3] + (edge,), jnp.float32)
    zero_one = jnp.zeros(field_arrays.shape[:3] + (1,), jnp.float32)
    prev_y = jnp.where(y_ids == 0, jnp.tile(minus_y, (1, 1, 1, edge)),
                       jnp.concatenate([zero_row, field_arrays[..., :-edge]], axis=-1))
    next_y = jnp.where(y_ids == edge - 1, jnp.tile(plus_y, (1, 1, 1, edge)),
                       jnp.concatenate([field_arrays[..., edge:], zero_row], axis=-1))
    prev_z = jnp.where(z_ids == 0, jnp.repeat(minus_z, edge, axis=-1),
                       jnp.concatenate([zero_one, field_arrays[..., :-1]], axis=-1))
    next_z = jnp.where(z_ids == edge - 1, jnp.repeat(plus_z, edge, axis=-1),
                       jnp.concatenate([field_arrays[..., 1:], zero_one], axis=-1))
    return (prev_x + next_x) + (prev_y + next_y) + (prev_z + next_z) - 6.0 * field_arrays


def advance(field_arrays, mobility, ghosts):
    lapl = laplacian(field_arrays, ghosts)
    phi = field_arrays[:, 0]
    conc = field_arrays[:, 1]
    wetting = 1.0 - phi * phi
    drive = lapl[:, 0] + phi - phi * phi * phi - coupling * conc * wetting * wetting
    new_phi = phi + time_step * mobility * drive
    new_conc = conc + time_step * lapl[:, 1] + 0.5 * (new_phi - phi)
    return jnp.stack([new_phi, new_conc], axis=1)


def reference(old_phase, old_solute, old_mobility, new_global_slot, neighbors):
    stacked_fields = jnp.stack([old_phase, old_solute, old_mobility], axis=1)
    target_slot = jnp.where(new_global_slot >= 0, new_global_slot, ACTIVE_BLOCKS).astype(jnp.int32)
    placed_blocks = jnp.zeros((ACTIVE_BLOCKS, 3, BLOCK_CELLS), jnp.float32).at[target_slot].set(stacked_fields, mode="drop")
    placed_blocks = placed_blocks.reshape(ACTIVE_BLOCKS, 3, BLOCK_EDGE_CELLS, FACE_CELLS)
    field_arrays = placed_blocks[:, :2]
    mobility = placed_blocks[:, 2]
    for step in range(STEPS):
        low_x, high_x, low_y, high_y, low_z, high_z = block_faces(field_arrays)
        ghosts = (pick_face(high_x, low_x, neighbors[:, 0]), pick_face(low_x, high_x, neighbors[:, 1]),
                  pick_face(high_y, low_y, neighbors[:, 2]), pick_face(low_y, high_y, neighbors[:, 3]),
                  pick_face(high_z, low_z, neighbors[:, 4]), pick_face(low_z, high_z, neighbors[:, 5]))
        grouped = jax.tree.map(lambda a: a.reshape((N_BLK, CAP) + a.shape[1:]), (field_arrays, mobility, ghosts))
        result = lax.map(lambda t: advance(t[0], t[1], t[2]), grouped)
        field_arrays = result.reshape(field_arrays.shape)
    return field_arrays[:, 0].reshape(ACTIVE_BLOCKS, BLOCK_CELLS), field_arrays[:, 1].reshape(ACTIVE_BLOCKS, BLOCK_CELLS)
```

```python
import functools

import jax
import jax.numpy as jnp
from jax import lax
from jax.experimental import pallas as pl
from jax.experimental.pallas import tpu as pltpu
from jax.sharding import PartitionSpec as P

EDGE = 32
FACE = EDGE * EDGE
CELLS = EDGE * FACE
CAP = 8
OLD = 16
FIELDS = 3
HALO = 3
CHUNK_PLANES = 4
CHUNK = CHUNK_PLANES * FACE
CHUNKS = EDGE // CHUNK_PLANES
LANES = 128
EXT = EDGE + 2 * HALO

time_step = 0.15
coupling = 1.5


def windows(slot_ref, here):
    first = slot_ref[0]
    count = jnp.int32(0)
    for i in range(OLD):
        count += (slot_ref[i] >= 0).astype(jnp.int32)
    amount = jnp.bitwise_and(first, CAP - 1)
    row = lax.broadcasted_iota(jnp.int32, (CAP, LANES), 0)

    def masks(k):
        index = row + ((here + k) * CAP - first)
        low = (index >= 0) & (index < CAP) & (index < count)
        high = (index >= CAP) & (index < count)
        return low, high

    return amount, masks


def picked(masks, low_rows, high_rows):
    low, high = masks
    return jnp.where(low, low_rows, jnp.where(high, high_rows, 0.0))


def side_of(here):
    return jnp.where(jnp.bitwise_and(here, 1) == 0, -1, 1)


def pack_kernel(here_ref, slot_ref, phi_ref, conc_ref, mob_ref, far_ref, merge_ref, final_ref):
    here = here_ref[0]
    side = side_of(here)
    amount, masks = windows(slot_ref, here)
    far, merge, final = masks(2 * side), masks(side), masks(-side)
    for f, ref in enumerate((phi_ref, conc_ref, mob_ref)):
        for v in range(CHUNK // LANES):
            lanes = pl.ds(v * LANES, LANES)
            low_rows = pltpu.roll(ref[0:CAP, lanes], amount, 0)
            high_rows = pltpu.roll(ref[CAP:OLD, lanes], amount, 0)
            far_ref[f, :, lanes] = picked(far, low_rows, high_rows)
            merge_ref[f, :, lanes] = picked(merge, low_rows, high_rows)
            final_ref[f, :, lanes] = picked(final, low_rows, high_rows)


def relay_kernel(here_ref, slot_ref, phi_ref, conc_ref, mob_ref, merge_ref, edge_ref, rest_ref):
    here = here_ref[0]
    side = side_of(here)
    amount, masks = windows(slot_ref, here)
    back = masks(-2 * side)
    i = pl.program_id(0)
    outer = (i == 0) | (i == CHUNKS - 1)

    def fill(out_ref):
        for f, ref in enumerate((phi_ref, conc_ref, mob_ref)):
            for v in range(CHUNK // LANES):
                lanes = pl.ds(v * LANES, LANES)
                low_rows = pltpu.roll(ref[0:CAP, lanes], amount, 0)
                high_rows = pltpu.roll(ref[CAP:OLD, lanes], amount, 0)
                out_ref[f, :, lanes] = picked(back, low_rows, high_rows) + merge_ref[f, :, lanes]

    @pl.when(outer)
    def _():
        fill(edge_ref)

    @pl.when(jnp.logical_not(outer))
    def _():
        fill(rest_ref)


def gather_kernel(here_ref, slot_ref, phi_ref, conc_ref, mob_ref, final_ref, far_ref, edge_ref, sum_ref, low_ref, high_ref):
    here = here_ref[0]
    amount, masks = windows(slot_ref, here)
    own = masks(0)
    i = pl.program_id(0)

    def placed(f, ref, lanes):
        low_rows = pltpu.roll(ref[0:CAP, lanes], amount, 0)
        high_rows = pltpu.roll(ref[CAP:OLD, lanes], amount, 0)
        return picked(own, low_rows, high_rows) + final_ref[f, :, lanes] + far_ref[f, :, lanes]

    def fill(with_edge, face_ref, start):
        for f, ref in enumerate((phi_ref, conc_ref, mob_ref)):
            for v in range(CHUNK // LANES):
                lanes = pl.ds(v * LANES, LANES)
                value = placed(f, ref, lanes)
                if with_edge:
                    value = value + edge_ref[f, :, lanes]
                    at = v * LANES - start
                    if 0 <= at < HALO * FACE:
                        face_ref[f, :, pl.ds(at, LANES)] = value
                sum_ref[f, :, lanes] = value

    @pl.when(i == 0)
    def _():
        fill(True, low_ref, 0)

    @pl.when(i == CHUNKS - 1)
    def _():
        fill(True, high_ref, (CHUNK_PLANES - HALO) * FACE)

    @pl.when((i > 0) & (i < CHUNKS - 1))
    def _():
        fill(False, None, 0)


def step_kernel(here_ref, sum_ref, rest_ref, below_ref, above_ref, nbr_ref, phase_ref, solute_ref, phi0, conc0, mob, phi1, conc1, phi2, conc2):
    here = here_ref[0]
    base = here * CAP
    vregs = FACE // LANES
    lane = lax.broadcasted_iota(jnp.int32, (CAP, LANES), 1)
    z = jnp.bitwise_and(lane, EDGE - 1)
    z_first, z_last = z == 0, z == EDGE - 1
    y_first, y_last = lane < EDGE, lane >= LANES - EDGE
    nbr = nbr_ref[...]

    def column(c, start):
        wide = jnp.broadcast_to(nbr[:, c : c + 1], (CAP, LANES))
        valid = wide >= 0
        return jnp.where(valid, wide - start, 0), valid

    below_x, has_below_x = column(0, base - CAP)
    above_x, has_above_x = column(1, base + CAP)
    below_y, has_below_y = column(2, base)
    above_y, has_above_y = column(3, base)
    below_z, _ = column(4, base)
    above_z, _ = column(5, base)
    down_z = jnp.bitwise_or(lane - z, jnp.bitwise_and(z + EDGE - 1, EDGE - 1))
    up_z = jnp.bitwise_or(lane - z, jnp.bitwise_and(z + 1, EDGE - 1))

    def rows(x, index):
        return jnp.take_along_axis(x, index, axis=0, mode="promise_in_bounds")

    def turned(x, index):
        return jnp.take_along_axis(x, index, axis=1, mode="promise_in_bounds")

    start_states = (phi0, conc0, mob)
    first_rest, last_rest = CHUNK_PLANES, EDGE - CHUNK_PLANES

    def place(x, add):
        for f, ref in enumerate(start_states):
            for v in range(vregs):
                lanes = pl.ds(pl.multiple_of(x * FACE + v * LANES, LANES), LANES)
                value = sum_ref[f, :, lanes]
                if add:
                    part = pl.ds(pl.multiple_of((x - first_rest) * FACE + v * LANES, LANES), LANES)
                    value = value + rest_ref[f, :, part]
                ref[x + HALO, :, pl.ds(v * LANES, LANES)] = value

    for x in (*range(first_rest), *range(last_rest, EDGE)):
        place(x, False)

    @pl.loop(first_rest, last_rest)
    def _(x):
        place(x, True)

    for f, ref in enumerate(start_states):
        for d in range(HALO):
            for v in range(vregs):
                lanes = pl.ds(v * LANES, LANES)
                part = pl.ds(d * FACE + v * LANES, LANES)
                mirror_low = ref[2 * HALO - 1 - d, :, lanes]
                ref[d, :, lanes] = jnp.where(has_below_x, rows(below_ref[f, :, part], below_x), mirror_low)
                mirror_high = ref[EDGE + HALO - 1 - d, :, lanes]
                ref[EDGE + HALO + d, :, lanes] = jnp.where(has_above_x, rows(above_ref[f, :, part], above_x), mirror_high)

    def laplacian(ref, x):
        centre = [ref[x, :, pl.ds(v * LANES, LANES)] for v in range(vregs)]
        lower = [pltpu.roll(c, EDGE, 1) for c in centre]
        upper = [pltpu.roll(c, LANES - EDGE, 1) for c in centre]
        out = []
        for v in range(vregs):
            c = centre[v]
            lanes = pl.ds(v * LANES, LANES)
            if v:
                from_lower = lower[v - 1]
            else:
                from_lower = jnp.where(has_below_y, rows(lower[-1], below_y), c)
            if v < vregs - 1:
                from_upper = upper[v + 1]
            else:
                from_upper = jnp.where(has_above_y, rows(upper[0], above_y), c)
            prev_y = jnp.where(y_first, from_lower, lower[v])
            next_y = jnp.where(y_last, from_upper, upper[v])
            prev_z = turned(jnp.where(z_last, rows(c, below_z), c), down_z)
            next_z = turned(jnp.where(z_first, rows(c, above_z), c), up_z)
            total = (ref[x - 1, :, lanes] + ref[x + 1, :, lanes]) + (prev_y + next_y) + (prev_z + next_z)
            out.append(total - 6.0 * c)
        return out, centre

    def advance(phi_ref, conc_ref, x, store):
        lapl_phi, phis = laplacian(phi_ref, x)
        lapl_conc, concs = laplacian(conc_ref, x)
        for v in range(vregs):
            phi, conc = phis[v], concs[v]
            square = phi * phi
            wetting = 1.0 - square
            drive = lapl_phi[v] + phi - square * phi - coupling * conc * wetting * wetting
            change = time_step * mob[x, :, pl.ds(v * LANES, LANES)] * drive
            store(v, phi + change, conc + time_step * lapl_conc[v] + 0.5 * change)

    def into(phi_ref, conc_ref, x):
        def store(v, phi, conc):
            lanes = pl.ds(v * LANES, LANES)
            phi_ref[x, :, lanes] = phi
            conc_ref[x, :, lanes] = conc

        return store

    def out(x):
        def store(v, phi, conc):
            lanes = pl.ds(pl.multiple_of((x - HALO) * FACE + v * LANES, LANES), LANES)
            phase_ref[:, lanes] = phi
            solute_ref[:, lanes] = conc

        return store

    @pl.loop(1, EXT - 1)
    def _(x):
        advance(phi0, conc0, x, into(phi1, conc1, x))

    @pl.loop(2, EXT - 2)
    def _(x):
        advance(phi1, conc1, x, into(phi2, conc2, x))

    @pl.loop(HALO, EXT - HALO)
    def _(x):
        advance(phi2, conc2, x, out(x))


SMEM = pl.BlockSpec(memory_space=pltpu.SMEM)
VMEM = pl.BlockSpec(memory_space=pltpu.VMEM)
PARAMS = pltpu.CompilerParams(vmem_limit_bytes=32 * 2**20)


def shaped(planes):
    return jax.ShapeDtypeStruct((FIELDS, CAP, planes * FACE), jnp.float32)


def cost(flops, moved):
    return pl.CostEstimate(flops=flops, bytes_accessed=moved, transcendentals=0)


OLD_SPEC = pl.BlockSpec((OLD, CHUNK), lambda i: (0, i))
CHUNK_SPEC = pl.BlockSpec((FIELDS, CAP, CHUNK), lambda i: (0, 0, i))
EDGE_SPEC = pl.BlockSpec((FIELDS, CAP, CHUNK), lambda i: (0, 0, jnp.where(i == CHUNKS - 1, 1, 0)))
REST_SPEC = pl.BlockSpec((FIELDS, CAP, CHUNK), lambda i: (0, 0, jnp.clip(i - 1, 0, CHUNKS - 3)))
FACE_SPEC = pl.BlockSpec((FIELDS, CAP, HALO * FACE), lambda i: (0, 0, 0))
MB = 2**20


def on_device(old_phase, old_solute, old_mobility, new_global_slot, neighbors):
    count = lax.axis_size("blk")
    here = lax.axis_index("blk").astype(jnp.int32).reshape(1)
    olds = (old_phase, old_solute, old_mobility)
    devices = range(count)

    def sent(block, route):
        return lax.ppermute(block, "blk", [(p, q) for p, q in route if 0 <= q < count])

    def outward(p):
        return -2 if p % 2 == 0 else 2

    far_send, merge_send, final_send = pl.pallas_call(
        pack_kernel,
        grid=(CHUNKS,),
        in_specs=[SMEM, SMEM] + [OLD_SPEC] * 3,
        out_specs=[CHUNK_SPEC] * 3,
        out_shape=[shaped(EDGE)] * 3,
        compiler_params=PARAMS,
        cost_estimate=cost(10**6, 15 * MB),
        name="pack",
    )(here, new_global_slot, *olds)

    merge_got = sent(merge_send, [(p, p ^ 1) for p in devices])
    far_got = sent(far_send, [(p, p + outward(p)) for p in devices])
    final_got = sent(final_send, [(p, p ^ 1) for p in devices])

    edge_send, rest_send = pl.pallas_call(
        relay_kernel,
        grid=(CHUNKS,),
        in_specs=[SMEM, SMEM] + [OLD_SPEC] * 3 + [CHUNK_SPEC],
        out_specs=[EDGE_SPEC, REST_SPEC],
        out_shape=[shaped(2 * CHUNK_PLANES), shaped(EDGE - 2 * CHUNK_PLANES)],
        compiler_params=PARAMS,
        cost_estimate=cost(10**6, 12 * MB),
        name="relay",
    )(here, new_global_slot, *olds, merge_got)
    edge_got = sent(edge_send, [(p, p - outward(p)) for p in devices])
    rest_got = sent(rest_send, [(p, p - outward(p)) for p in devices])

    partial_sum, low, high = pl.pallas_call(
        gather_kernel,
        grid=(CHUNKS,),
        in_specs=[SMEM, SMEM] + [OLD_SPEC] * 3 + [CHUNK_SPEC, CHUNK_SPEC, EDGE_SPEC],
        out_specs=[CHUNK_SPEC, FACE_SPEC, FACE_SPEC],
        out_shape=[shaped(EDGE), shaped(HALO), shaped(HALO)],
        compiler_params=PARAMS,
        cost_estimate=cost(10**6, 15 * MB),
        name="gather",
    )(here, new_global_slot, *olds, final_got, far_got, edge_got)
    below = sent(high, [(p, p + 1) for p in devices])
    above = sent(low, [(p, p - 1) for p in devices])

    state = pltpu.VMEM((EXT, CAP, FACE), jnp.float32)
    phase, solute = pl.pallas_call(
        step_kernel,
        in_specs=[SMEM] + [VMEM] * 5,
        out_specs=[VMEM] * 2,
        out_shape=[jax.ShapeDtypeStruct((CAP, CELLS), jnp.float32)] * 2,
        scratch_shapes=[state] * 7,
        compiler_params=PARAMS,
        cost_estimate=cost(40 * 10**6, 8 * MB),
        name="substeps",
    )(here, partial_sum, rest_got, below, above, neighbors)
    return phase, solute


def solution(mesh):
    placed = (P("blk", None), P("blk", None), P("blk", None), P("blk"), P("blk", None))
    return jax.shard_map(
        on_device,
        mesh=mesh,
        in_specs=placed,
        out_specs=(P("blk", None), P("blk", None)),
        check_vma=False,
    )
```

```python
import functools

import jax
import jax.numpy as jnp
from jax import lax
from jax.experimental import pallas as pl
from jax.experimental.pallas import tpu as pltpu
from jax.sharding import PartitionSpec as P

EDGE = 32
FACE = EDGE * EDGE
CELLS = EDGE * FACE
CAP = 8
OLD = 16
FIELDS = 3
HALO = 3
CHUNK_PLANES = 4
CHUNK = CHUNK_PLANES * FACE
CHUNKS = EDGE // CHUNK_PLANES
LANES = 128
EXT = EDGE + 2 * HALO
MID = 16
LATE = EDGE - 2 * CHUNK_PLANES - MID
MID_CHUNKS = MID // CHUNK_PLANES
LATE_CHUNKS = LATE // CHUNK_PLANES
VREGS = FACE // LANES

time_step = 0.15
coupling = 1.5


def windows(slot_ref, here):
    first = slot_ref[0]
    count = jnp.int32(0)
    for i in range(OLD):
        count += (slot_ref[i] >= 0).astype(jnp.int32)
    amount = jnp.bitwise_and(first, CAP - 1)
    row = lax.broadcasted_iota(jnp.int32, (CAP, LANES), 0)

    def masks(k):
        index = row + ((here + k) * CAP - first)
        low = (index >= 0) & (index < CAP) & (index < count)
        high = (index >= CAP) & (index < count)
        return low, high

    return amount, masks


def picked(masks, low_rows, high_rows):
    low, high = masks
    return jnp.where(low, low_rows, jnp.where(high, high_rows, 0.0))


def side_of(here):
    return jnp.where(jnp.bitwise_and(here, 1) == 0, -1, 1)


def vregs_of(planes):
    return [pl.ds(v * LANES, LANES) for v in range(planes * VREGS)]


def aligned(ref, lanes, amount):
    return pltpu.roll(ref[0:CAP, lanes], amount, 0), pltpu.roll(ref[CAP:OLD, lanes], amount, 0)


def load_slots(slot_hbm, slot_ref, sem):
    copy = pltpu.make_async_copy(slot_hbm, slot_ref, sem)
    copy.start()
    copy.wait()


def chunk_at(i):
    return jnp.where(i == 0, 0, jnp.where(i == 1, CHUNKS - 1, i - 1))


def into_parts(i, fill, *refs):
    edge_ref, mid_ref, late_ref = refs
    pl.when(i < 2)(lambda: fill(edge_ref))
    pl.when((i >= 2) & (i < 2 + MID_CHUNKS))(lambda: fill(mid_ref))
    pl.when(i >= 2 + MID_CHUNKS)(lambda: fill(late_ref))


def pack_kernel(here_ref, slot_hbm, phi_hbm, conc_hbm, mob_hbm, pair_hbm, far_hbm, late_hbm, slot_ref, sem):
    load_slots(slot_hbm, slot_ref, sem)
    here = here_ref[0]
    side = side_of(here)
    amount, masks = windows(slot_ref, here)
    far, merge, final = masks(2 * side), masks(side), masks(-side)

    def body(phi_ref, conc_ref, mob_ref, pair_ref, far_ref, late_ref):
        def fill(out_ref):
            for f, ref in enumerate((phi_ref, conc_ref, mob_ref)):
                for lanes in vregs_of(CHUNK_PLANES):
                    rows = aligned(ref, lanes, amount)
                    pair_ref[f, :, lanes] = picked(merge, *rows)
                    pair_ref[FIELDS + f, :, lanes] = picked(final, *rows)
                    out_ref[f, :, lanes] = picked(far, *rows)

        i = pl.program_id(0)
        pl.when(i < 2 + MID_CHUNKS)(lambda: fill(far_ref))
        pl.when(i >= 2 + MID_CHUNKS)(lambda: fill(late_ref))

    pltpu.emit_pipeline(
        body,
        grid=(CHUNKS,),
        in_specs=[pl.BlockSpec((OLD, CHUNK), lambda i: (0, chunk_at(i)))] * 3,
        out_specs=[
            pl.BlockSpec((2 * FIELDS, CAP, CHUNK), lambda i: (0, 0, chunk_at(i))),
            pl.BlockSpec((FIELDS, CAP, CHUNK), lambda i: (0, 0, jnp.minimum(i, 1 + MID_CHUNKS))),
            LATE_SPEC,
        ],
    )(phi_hbm, conc_hbm, mob_hbm, pair_hbm, far_hbm, late_hbm)


def relay_kernel(here_ref, slot_ref, phi_ref, conc_ref, mob_ref, merge_ref, *out_refs):
    here = here_ref[0]
    amount, masks = windows(slot_ref, here)
    back = masks(-2 * side_of(here))

    def fill(out_ref):
        for f, ref in enumerate((phi_ref, conc_ref, mob_ref)):
            for lanes in vregs_of(CHUNK_PLANES):
                out_ref[f, :, lanes] = picked(back, *aligned(ref, lanes, amount)) + merge_ref[f, :, lanes]

    into_parts(pl.program_id(0), fill, *out_refs)


def stay_kernel(here_ref, slot_ref, phi_ref, conc_ref, mob_ref, final_ref, *out_refs):
    here = here_ref[0]
    amount, masks = windows(slot_ref, here)
    own = masks(0)

    def fill(out_ref):
        for f, ref in enumerate((phi_ref, conc_ref, mob_ref)):
            for lanes in vregs_of(CHUNK_PLANES):
                out_ref[f, :, lanes] = picked(own, *aligned(ref, lanes, amount)) + final_ref[f, :, lanes]

    into_parts(pl.program_id(0), fill, *out_refs)


def face_kernel(stay_ref, far_ref, back_ref, edge_ref, low_ref, high_ref):
    first_high = (2 * CHUNK_PLANES - HALO) * FACE
    for f in range(FIELDS):
        for v in range(2 * CHUNK_PLANES * VREGS):
            lanes = pl.ds(v * LANES, LANES)
            value = stay_ref[f, :, lanes] + far_ref[f, :, lanes] + back_ref[f, :, lanes]
            edge_ref[f, :, lanes] = value
            at = v * LANES
            if at < HALO * FACE:
                low_ref[f, :, lanes] = value
            if at >= first_high:
                high_ref[f, :, pl.ds(at - first_high, LANES)] = value


class Stencil:
    def __init__(self, here, nbr):
        base = here * CAP
        self.nbr = nbr
        lane = lax.broadcasted_iota(jnp.int32, (CAP, LANES), 1)
        z = jnp.bitwise_and(lane, EDGE - 1)
        self.z_first, self.z_last = z == 0, z == EDGE - 1
        self.y_first, self.y_last = lane < EDGE, lane >= LANES - EDGE
        self.below_x, self.has_below_x = self.column(0, base - CAP)
        self.above_x, self.has_above_x = self.column(1, base + CAP)
        self.below_y, self.has_below_y = self.column(2, base)
        self.above_y, self.has_above_y = self.column(3, base)
        self.below_z, _ = self.column(4, base)
        self.above_z, _ = self.column(5, base)

    def column(self, c, start):
        wide = jnp.broadcast_to(self.nbr[:, c : c + 1], (CAP, LANES))
        valid = wide >= 0
        return jnp.where(valid, wide - start, 0), valid

    @staticmethod
    def rows(x, index):
        return jnp.take_along_axis(x, index, axis=0, mode="promise_in_bounds")

    def laplacian(self, ref, x):
        centre = [ref[x, :, pl.ds(v * LANES, LANES)] for v in range(VREGS)]
        lower = [pltpu.roll(c, EDGE, 1) for c in centre]
        upper = [pltpu.roll(c, LANES - EDGE, 1) for c in centre]
        out = []
        for v in range(VREGS):
            c = centre[v]
            lanes = pl.ds(v * LANES, LANES)
            if v:
                from_lower = lower[v - 1]
            else:
                from_lower = jnp.where(self.has_below_y, self.rows(lower[-1], self.below_y), c)
            if v < VREGS - 1:
                from_upper = upper[v + 1]
            else:
                from_upper = jnp.where(self.has_above_y, self.rows(upper[0], self.above_y), c)
            prev_y = jnp.where(self.y_first, from_lower, lower[v])
            next_y = jnp.where(self.y_last, from_upper, upper[v])
            prev_z = jnp.where(self.z_first, pltpu.roll(self.rows(c, self.below_z), LANES - EDGE + 1, 1), pltpu.roll(c, 1, 1))
            next_z = jnp.where(self.z_last, pltpu.roll(self.rows(c, self.above_z), EDGE - 1, 1), pltpu.roll(c, LANES - 1, 1))
            total = (ref[x - 1, :, lanes] + ref[x + 1, :, lanes]) + (prev_y + next_y) + (prev_z + next_z)
            out.append(total - 6.0 * c)
        return out, centre

    def advance(self, phi_ref, conc_ref, mob_ref, x, store):
        lapl_phi, phis = self.laplacian(phi_ref, x)
        lapl_conc, concs = self.laplacian(conc_ref, x)
        for v in range(VREGS):
            phi, conc = phis[v], concs[v]
            square = phi * phi
            wetting = 1.0 - square
            drive = lapl_phi[v] + phi - square * phi - coupling * conc * wetting * wetting
            change = time_step * mob_ref[x, :, pl.ds(v * LANES, LANES)] * drive
            store(v, phi + change, conc + time_step * lapl_conc[v] + 0.5 * change)

    def sweep(self, first, last, unroll, source, mob_ref, target, shift=None):
        phi_ref, conc_ref = source
        phi_out, conc_out = target

        def one(x):
            def store(v, phi, conc):
                if shift is None:
                    where = (x, slice(None), pl.ds(v * LANES, LANES))
                else:
                    where = (slice(None), pl.ds(pl.multiple_of((x - shift) * FACE + v * LANES, LANES), LANES))
                phi_out[where] = phi
                conc_out[where] = conc

            self.advance(phi_ref, conc_ref, mob_ref, x, store)

        whole = first + (last - first) // unroll * unroll
        if whole > first:

            @pl.loop(0, (whole - first) // unroll)
            def _(i):
                for u in range(unroll):
                    one(first + i * unroll + u)

        for x in range(whole, last):
            one(x)


def place(states, planes, at, *parts):
    for f, ref in enumerate(states):

        @pl.loop(0, planes)
        def _(x):
            for v in range(VREGS):
                lanes = pl.ds(pl.multiple_of(x * FACE + v * LANES, LANES), LANES)
                value = parts[0][f, :, lanes]
                for part in parts[1:]:
                    value = value + part[f, :, lanes]
                ref[x + at, :, pl.ds(v * LANES, LANES)] = value


MID_AT = HALO + CHUNK_PLANES
LATE_AT = MID_AT + MID
TOP_AT = LATE_AT + LATE


def early_kernel(
    here_ref, edge_ref, stay_ref, far_ref, back_ref, below_ref, above_ref, nbr_ref,
    phase_ref, solute_ref, kept0_ref, kept1_ref, kept2_ref,
    phi0, conc0, mob, phi1, conc1, phi2, conc2,
):
    st = Stencil(here_ref[0], nbr_ref[...])
    states = (phi0, conc0, mob)
    for f, ref in enumerate(states):
        for d in range(2 * CHUNK_PLANES):
            at = HALO + d if d < CHUNK_PLANES else TOP_AT + d - CHUNK_PLANES
            for v in range(VREGS):
                ref[at, :, pl.ds(v * LANES, LANES)] = edge_ref[f, :, pl.ds(d * FACE + v * LANES, LANES)]
    place(states, MID, MID_AT, stay_ref, far_ref.at[:, :, pl.ds(2 * CHUNK, MID * FACE)], back_ref)
    for f, ref in enumerate(states):
        for d in range(HALO):
            for v in range(VREGS):
                lanes = pl.ds(v * LANES, LANES)
                part = pl.ds(d * FACE + v * LANES, LANES)
                mirror_low = ref[2 * HALO - 1 - d, :, lanes]
                ref[d, :, lanes] = jnp.where(st.has_below_x, st.rows(below_ref[f, :, part], st.below_x), mirror_low)
                mirror_high = ref[EDGE + HALO - 1 - d, :, lanes]
                ref[EDGE + HALO + d, :, lanes] = jnp.where(st.has_above_x, st.rows(above_ref[f, :, part], st.above_x), mirror_high)
    st.sweep(1, LATE_AT - 1, 4, (phi0, conc0), mob, (phi1, conc1))
    st.sweep(TOP_AT + 1, EXT - 1, 5, (phi0, conc0), mob, (phi1, conc1))
    st.sweep(2, LATE_AT - 2, 4, (phi1, conc1), mob, (phi2, conc2))
    st.sweep(TOP_AT + 2, EXT - 2, 3, (phi1, conc1), mob, (phi2, conc2))
    st.sweep(HALO, LATE_AT - 3, 4, (phi2, conc2), mob, (phase_ref, solute_ref), HALO)
    st.sweep(TOP_AT + 3, EXT - 3, 1, (phi2, conc2), mob, (phase_ref, solute_ref), HALO)
    for f, ref in enumerate(states):
        for n, x in enumerate((*range(LATE_AT - 3, LATE_AT), *range(TOP_AT, TOP_AT + 3))):
            kept0_ref[f, n] = ref[x]
    for f, ref in enumerate((phi1, conc1)):
        for n, x in enumerate((LATE_AT - 3, LATE_AT - 2, TOP_AT + 1, TOP_AT + 2)):
            kept1_ref[f, n] = ref[x]
    for f, ref in enumerate((phi2, conc2)):
        for n, x in enumerate((LATE_AT - 4, LATE_AT - 3, TOP_AT + 2, TOP_AT + 3)):
            kept2_ref[f, n] = ref[x]


BACK = LATE_AT - 4
LATE_PLANES = TOP_AT + 4 - BACK
OUT_FIRST = LATE_AT - 3
OUT_PLANES = TOP_AT + 3 - OUT_FIRST


def late_kernel(
    here_ref, stay_ref, far_ref, back_ref, nbr_ref, kept0_ref, kept1_ref, kept2_ref, _phase_in, _solute_in,
    phase_hbm, solute_hbm,
    phi0, conc0, mob, phi1, conc1, phi2, conc2, phase_ref, solute_ref, sems,
):
    st = Stencil(here_ref[0], nbr_ref[...])
    states = (phi0, conc0, mob)
    first, last = LATE_AT - BACK, TOP_AT - BACK
    for f, ref in enumerate(states):
        for n, x in enumerate((*range(first - 3, first), *range(last, last + 3))):
            ref[x] = kept0_ref[f, n]
    for f, ref in enumerate((phi1, conc1)):
        for n, x in enumerate((first - 3, first - 2, last + 1, last + 2)):
            ref[x] = kept1_ref[f, n]
    for f, ref in enumerate((phi2, conc2)):
        for n, x in enumerate((first - 4, first - 3, last + 2, last + 3)):
            ref[x] = kept2_ref[f, n]
    place(states, LATE, first, stay_ref, far_ref, back_ref)
    st.sweep(first - 1, last + 1, 5, (phi0, conc0), mob, (phi1, conc1))
    st.sweep(first - 2, last + 2, 4, (phi1, conc1), mob, (phi2, conc2))
    st.sweep(first - 3, last + 3, 7, (phi2, conc2), mob, (phase_ref, solute_ref), first - 3)
    copies = []
    for n, (ref, hbm) in enumerate(((phase_ref, phase_hbm), (solute_ref, solute_hbm))):
        lanes = pl.ds((OUT_FIRST - HALO) * FACE, OUT_PLANES * FACE)
        copies.append(pltpu.make_async_copy(ref, hbm.at[:, lanes], sems.at[n]))
    for copy in copies:
        copy.start()
    for copy in copies:
        copy.wait()


SMEM = pl.BlockSpec(memory_space=pltpu.SMEM)
VMEM = pl.BlockSpec(memory_space=pltpu.VMEM)
HBM = pl.BlockSpec(memory_space=pltpu.HBM)
ANY = pl.BlockSpec(memory_space=pl.ANY)
PARAMS = pltpu.CompilerParams(vmem_limit_bytes=32 * 2**20)


def shaped(planes, fields=FIELDS):
    return jax.ShapeDtypeStruct((fields, CAP, planes * FACE), jnp.float32)


def cost(moved, flops=10**6):
    return pl.CostEstimate(flops=flops, bytes_accessed=moved, transcendentals=0)


OLD_SPEC = pl.BlockSpec((OLD, CHUNK), lambda i: (0, chunk_at(i)))
EDGE_SPEC = pl.BlockSpec((FIELDS, CAP, CHUNK), lambda i: (0, 0, jnp.minimum(i, 1)))
MID_SPEC = pl.BlockSpec((FIELDS, CAP, CHUNK), lambda i: (0, 0, jnp.clip(i - 2, 0, MID_CHUNKS - 1)))
LATE_SPEC = pl.BlockSpec((FIELDS, CAP, CHUNK), lambda i: (0, 0, jnp.clip(i - 2 - MID_CHUNKS, 0, LATE_CHUNKS - 1)))
MERGE_SPEC = pl.BlockSpec((FIELDS, CAP, CHUNK), lambda i: (0, 0, chunk_at(i)))
FINAL_SPEC = pl.BlockSpec((FIELDS, CAP, CHUNK), lambda i: (1, 0, chunk_at(i)))
EDGES = pl.BlockSpec((FIELDS, CAP, 2 * CHUNK), lambda i: (0, 0, 0))
FACES = pl.BlockSpec((FIELDS, CAP, HALO * FACE), lambda i: (0, 0, 0))
MB = 2**20


def on_device(old_phase, old_solute, old_mobility, new_global_slot, neighbors):
    count = lax.axis_size("blk")
    here = lax.axis_index("blk").astype(jnp.int32).reshape(1)
    olds = tuple(pltpu.with_memory_space_constraint(x, pltpu.HBM) for x in (old_phase, old_solute, old_mobility))
    devices = range(count)

    def sent(block, route):
        return lax.ppermute(block, "blk", [(p, q) for p, q in route if 0 <= q < count])

    def outward(p):
        return -2 if p % 2 == 0 else 2

    partner = [(p, p ^ 1) for p in devices]
    far_route = [(p, p + outward(p)) for p in devices]
    back_route = [(p, p - outward(p)) for p in devices]

    def after(block, *others):
        return lax.optimization_barrier((block, *others))[0]

    slots_hbm = pltpu.with_memory_space_constraint(new_global_slot, pltpu.HBM)
    slot_scratch = [pltpu.SMEM((OLD,), jnp.int32), pltpu.SemaphoreType.DMA]
    pair, far_first, far_late = pl.pallas_call(
        pack_kernel,
        in_specs=[SMEM, HBM, HBM, HBM, HBM],
        out_specs=[ANY] * 3,
        out_shape=[shaped(EDGE, 2 * FIELDS), shaped(2 * CHUNK_PLANES + MID), shaped(LATE)],
        scratch_shapes=slot_scratch,
        compiler_params=PARAMS,
        cost_estimate=cost(15 * MB),
        name="pack",
    )(here, slots_hbm, *olds)
    far_first_got = sent(far_first, far_route)
    pair_got = sent(pair, partner)

    three_parts = [shaped(2 * CHUNK_PLANES), shaped(MID), shaped(LATE)]
    back_edge, back_mid, back_late = pl.pallas_call(
        relay_kernel,
        grid=(CHUNKS,),
        in_specs=[SMEM, SMEM] + [OLD_SPEC] * 3 + [MERGE_SPEC],
        out_specs=[EDGE_SPEC, MID_SPEC, LATE_SPEC],
        out_shape=three_parts,
        compiler_params=PARAMS,
        cost_estimate=cost(12 * MB),
        name="relay",
    )(here, new_global_slot, *olds, pair_got)
    back_edge_got = sent(back_edge, back_route)
    back_mid_got = sent(after(back_mid, back_edge_got), back_route)

    stay_edge, stay_mid, stay_late = pl.pallas_call(
        stay_kernel,
        grid=(CHUNKS,),
        in_specs=[SMEM, SMEM] + [OLD_SPEC] * 3 + [FINAL_SPEC],
        out_specs=[EDGE_SPEC, MID_SPEC, LATE_SPEC],
        out_shape=three_parts,
        compiler_params=PARAMS,
        cost_estimate=cost(12 * MB),
        name="stay",
    )(here, new_global_slot, *olds, pair_got)

    edge, low, high = pl.pallas_call(
        face_kernel,
        grid=(1,),
        in_specs=[EDGES] * 3,
        out_specs=[EDGES, FACES, FACES],
        out_shape=[shaped(2 * CHUNK_PLANES), shaped(HALO), shaped(HALO)],
        compiler_params=PARAMS,
        cost_estimate=cost(3 * MB),
        name="faces",
    )(stay_edge, far_first_got, back_edge_got)
    below = sent(high, [(p, p + 1) for p in devices])
    above = sent(low, [(p, p - 1) for p in devices])
    far_late_got = sent(after(far_late, low), far_route)
    back_late_got = sent(after(back_late, back_mid_got, below, above), back_route)

    state = pltpu.VMEM((EXT, CAP, FACE), jnp.float32)
    whole = jax.ShapeDtypeStruct((CAP, CELLS), jnp.float32)

    def kept(fields, planes):
        return jax.ShapeDtypeStruct((fields, planes, CAP, FACE), jnp.float32)

    phase, solute, kept0, kept1, kept2 = pl.pallas_call(
        early_kernel,
        in_specs=[SMEM] + [VMEM] * 7,
        out_specs=[VMEM] * 5,
        out_shape=[whole, whole, kept(3, 6), kept(2, 4), kept(2, 4)],
        scratch_shapes=[state] * 7,
        compiler_params=PARAMS,
        cost_estimate=cost(20 * MB),
        name="early_steps",
    )(here, edge, stay_mid, far_first_got, back_mid_got, below, above, neighbors)

    state = pltpu.VMEM((LATE_PLANES, CAP, FACE), jnp.float32)
    rows_out = pltpu.VMEM((CAP, OUT_PLANES * FACE), jnp.float32)
    phase, solute = pl.pallas_call(
        late_kernel,
        in_specs=[SMEM] + [VMEM] * 7 + [HBM] * 2,
        out_specs=[HBM] * 2,
        out_shape=[whole, whole],
        scratch_shapes=[state] * 7 + [rows_out] * 2 + [pltpu.SemaphoreType.DMA((2,))],
        input_output_aliases={8: 0, 9: 1},
        compiler_params=PARAMS,
        cost_estimate=cost(8 * MB),
        name="late_steps",
    )(here, stay_late, far_late_got, back_late_got, neighbors, kept0, kept1, kept2, phase, solute)
    return phase, solute


def solution(mesh):
    placed = (P("blk", None), P("blk", None), P("blk", None), P("blk"), P("blk", None))
    return jax.shard_map(
        on_device,
        mesh=mesh,
        in_specs=placed,
        out_specs=(P("blk", None), P("blk", None)),
        check_vma=False,
    )
```

```python
import functools

import jax
import jax.numpy as jnp
from jax import lax
from jax.experimental import pallas as pl
from jax.experimental.pallas import tpu as pltpu
from jax.sharding import PartitionSpec as P

EDGE = 32
FACE = EDGE * EDGE
CELLS = EDGE * FACE
CAP = 8
OLD = 16
FIELDS = 3
HALO = 3
CHUNK_PLANES = 4
CHUNK = CHUNK_PLANES * FACE
CHUNKS = EDGE // CHUNK_PLANES
LANES = 128
EXT = EDGE + 2 * HALO
MID = 16
LATE = EDGE - 2 * CHUNK_PLANES - MID
MID_CHUNKS = MID // CHUNK_PLANES
LATE_CHUNKS = LATE // CHUNK_PLANES
VREGS = FACE // LANES

time_step = 0.15
coupling = 1.5


def windows(slot_ref, here):
    first = slot_ref[0]
    count = jnp.int32(0)
    for i in range(OLD):
        count += (slot_ref[i] >= 0).astype(jnp.int32)
    amount = jnp.bitwise_and(first, CAP - 1)
    row = lax.broadcasted_iota(jnp.int32, (CAP, LANES), 0)

    def masks(k):
        index = row + ((here + k) * CAP - first)
        low = (index >= 0) & (index < CAP) & (index < count)
        high = (index >= CAP) & (index < count)
        return low, high

    return amount, masks


def picked(masks, low_rows, high_rows):
    low, high = masks
    return jnp.where(low, low_rows, jnp.where(high, high_rows, 0.0))


def side_of(here):
    return jnp.where(jnp.bitwise_and(here, 1) == 0, -1, 1)


def aligned(ref, lanes, amount):
    return pltpu.roll(ref[0:CAP, lanes], amount, 0), pltpu.roll(ref[CAP:OLD, lanes], amount, 0)


def chunk_at(i):
    return jnp.where(i == 0, 0, jnp.where(i == 1, CHUNKS - 1, i - 1))


def lanes_at(start, v):
    return pl.ds(pl.multiple_of(start + v * LANES, LANES), LANES)


def pack_kernel(
    here_ref, slot_hbm, phi_hbm, conc_hbm, mob_hbm,
    phi_ref, conc_ref, mob_ref, merge_ref, final_ref, far_ref, late_ref,
    slot_ref, slot_sem, sems,
):
    olds = tuple(zip((phi_hbm, conc_hbm, mob_hbm), (phi_ref, conc_ref, mob_ref)))

    def copies(i):
        lanes = pl.ds(pl.multiple_of(chunk_at(i) * CHUNK, CHUNK), CHUNK)
        return [pltpu.make_async_copy(hbm.at[:, lanes], ref.at[:, lanes], sems.at[i, f]) for f, (hbm, ref) in enumerate(olds)]

    slot_copy = pltpu.make_async_copy(slot_hbm, slot_ref, slot_sem)
    slot_copy.start()

    @pl.loop(0, CHUNKS)
    def _(i):
        for copy in copies(i):
            copy.start()

    slot_copy.wait()
    here = here_ref[0]
    side = side_of(here)
    amount, masks = windows(slot_ref, here)
    far, merge, final = masks(2 * side), masks(side), masks(-side)

    def fill(i, out_ref, out_start):
        start = chunk_at(i) * CHUNK
        for f, (_, ref) in enumerate(olds):
            for v in range(CHUNK // LANES):
                lanes = lanes_at(start, v)
                rows = aligned(ref, lanes, amount)
                merge_ref[f, :, lanes] = picked(merge, *rows)
                final_ref[f, :, lanes] = picked(final, *rows)
                out_ref[f, :, lanes_at(out_start, v)] = picked(far, *rows)

    first_steps = 2 + MID_CHUNKS

    @pl.loop(0, first_steps)
    def _(i):
        for copy in copies(i):
            copy.wait()
        fill(i, far_ref, i * CHUNK)

    @pl.loop(first_steps, CHUNKS)
    def _(i):
        for copy in copies(i):
            copy.wait()
        fill(i, late_ref, (i - first_steps) * CHUNK)


def add_rows(masks, amount, old_refs, add_ref, part_refs):
    edge_ref, mid_ref, late_ref = part_refs
    high = CHUNK_PLANES + MID + LATE
    for out_ref, out_plane, plane, count in (
        (edge_ref, 0, 0, CHUNK_PLANES),
        (edge_ref, CHUNK_PLANES, high, CHUNK_PLANES),
        (mid_ref, 0, CHUNK_PLANES, MID),
        (late_ref, 0, CHUNK_PLANES + MID, LATE),
    ):

        @pl.loop(0, count // 2)
        def _(i):
            for f, ref in enumerate(old_refs):
                for v in range(2 * VREGS):
                    lanes = lanes_at((plane + 2 * i) * FACE, v)
                    value = picked(masks, *aligned(ref, lanes, amount)) + add_ref[f, :, lanes]
                    out_ref[f, :, lanes_at((out_plane + 2 * i) * FACE, v)] = value


def relay_kernel(here_ref, slot_ref, phi_ref, conc_ref, mob_ref, merge_ref, *part_refs):
    here = here_ref[0]
    amount, masks = windows(slot_ref, here)
    add_rows(masks(-2 * side_of(here)), amount, (phi_ref, conc_ref, mob_ref), merge_ref, part_refs)


def stay_kernel(here_ref, slot_ref, phi_ref, conc_ref, mob_ref, final_ref, *part_refs):
    here = here_ref[0]
    amount, masks = windows(slot_ref, here)
    add_rows(masks(0), amount, (phi_ref, conc_ref, mob_ref), final_ref, part_refs)


def face_kernel(stay_ref, far_ref, back_ref, edge_ref, low_ref, high_ref):
    first_high = (2 * CHUNK_PLANES - HALO) * FACE
    for f in range(FIELDS):
        for v in range(2 * CHUNK_PLANES * VREGS):
            lanes = pl.ds(v * LANES, LANES)
            value = stay_ref[f, :, lanes] + far_ref[f, :, lanes] + back_ref[f, :, lanes]
            edge_ref[f, :, lanes] = value
            at = v * LANES
            if at < HALO * FACE:
                low_ref[f, :, lanes] = value
            if at >= first_high:
                high_ref[f, :, pl.ds(at - first_high, LANES)] = value


class Stencil:
    def __init__(self, here, nbr):
        base = here * CAP
        self.nbr = nbr
        lane = lax.broadcasted_iota(jnp.int32, (CAP, LANES), 1)
        z = jnp.bitwise_and(lane, EDGE - 1)
        self.z_first, self.z_last = z == 0, z == EDGE - 1
        self.y_first, self.y_last = lane < EDGE, lane >= LANES - EDGE
        self.below_x, self.has_below_x = self.column(0, base - CAP)
        self.above_x, self.has_above_x = self.column(1, base + CAP)
        self.below_y, self.has_below_y = self.column(2, base)
        self.above_y, self.has_above_y = self.column(3, base)
        self.below_z, _ = self.column(4, base)
        self.above_z, _ = self.column(5, base)

    def column(self, c, start):
        wide = jnp.broadcast_to(self.nbr[:, c : c + 1], (CAP, LANES))
        valid = wide >= 0
        return jnp.where(valid, wide - start, 0), valid

    @staticmethod
    def rows(x, index):
        return jnp.take_along_axis(x, index, axis=0, mode="promise_in_bounds")

    def laplacian(self, ref, x):
        centre = [ref[x, :, pl.ds(v * LANES, LANES)] for v in range(VREGS)]
        lower = [pltpu.roll(c, EDGE, 1) for c in centre]
        upper = [pltpu.roll(c, LANES - EDGE, 1) for c in centre]
        out = []
        for v in range(VREGS):
            c = centre[v]
            lanes = pl.ds(v * LANES, LANES)
            if v:
                from_lower = lower[v - 1]
            else:
                from_lower = jnp.where(self.has_below_y, self.rows(lower[-1], self.below_y), c)
            if v < VREGS - 1:
                from_upper = upper[v + 1]
            else:
                from_upper = jnp.where(self.has_above_y, self.rows(upper[0], self.above_y), c)
            prev_y = jnp.where(self.y_first, from_lower, lower[v])
            next_y = jnp.where(self.y_last, from_upper, upper[v])
            prev_z = jnp.where(self.z_first, pltpu.roll(self.rows(c, self.below_z), LANES - EDGE + 1, 1), pltpu.roll(c, 1, 1))
            next_z = jnp.where(self.z_last, pltpu.roll(self.rows(c, self.above_z), EDGE - 1, 1), pltpu.roll(c, LANES - 1, 1))
            total = (ref[x - 1, :, lanes] + ref[x + 1, :, lanes]) + (prev_y + next_y) + (prev_z + next_z)
            out.append(total - 6.0 * c)
        return out, centre

    def advance(self, phi_ref, conc_ref, mob_ref, x, store):
        lapl_phi, phis = self.laplacian(phi_ref, x)
        lapl_conc, concs = self.laplacian(conc_ref, x)
        for v in range(VREGS):
            phi, conc = phis[v], concs[v]
            square = phi * phi
            wetting = 1.0 - square
            drive = lapl_phi[v] + phi - square * phi - coupling * conc * wetting * wetting
            change = time_step * mob_ref[x, :, pl.ds(v * LANES, LANES)] * drive
            store(v, phi + change, conc + time_step * lapl_conc[v] + 0.5 * change)

    def sweep(self, first, last, unroll, source, mob_ref, target, shift=None):
        phi_ref, conc_ref = source
        phi_out, conc_out = target

        def one(x):
            def store(v, phi, conc):
                if shift is None:
                    where = (x, slice(None), pl.ds(v * LANES, LANES))
                else:
                    where = (slice(None), pl.ds(pl.multiple_of((x - shift) * FACE + v * LANES, LANES), LANES))
                phi_out[where] = phi
                conc_out[where] = conc

            self.advance(phi_ref, conc_ref, mob_ref, x, store)

        whole = first + (last - first) // unroll * unroll
        if whole > first:

            @pl.loop(0, (whole - first) // unroll)
            def _(i):
                for u in range(unroll):
                    one(first + i * unroll + u)

        for x in range(whole, last):
            one(x)


def place(states, planes, at, *parts):
    for f, ref in enumerate(states):

        @pl.loop(0, planes)
        def _(x):
            for v in range(VREGS):
                lanes = pl.ds(pl.multiple_of(x * FACE + v * LANES, LANES), LANES)
                value = parts[0][f, :, lanes]
                for part in parts[1:]:
                    value = value + part[f, :, lanes]
                ref[x + at, :, pl.ds(v * LANES, LANES)] = value


MID_AT = HALO + CHUNK_PLANES
LATE_AT = MID_AT + MID
TOP_AT = LATE_AT + LATE


def early_kernel(
    here_ref, edge_ref, stay_ref, far_ref, back_ref, below_ref, above_ref, nbr_ref,
    phase_ref, solute_ref, kept0_ref, kept1_ref, kept2_ref,
    phi0, conc0, mob, phi1, conc1, phi2, conc2,
):
    st = Stencil(here_ref[0], nbr_ref[...])
    states = (phi0, conc0, mob)
    for f, ref in enumerate(states):
        for d in range(2 * CHUNK_PLANES):
            at = HALO + d if d < CHUNK_PLANES else TOP_AT + d - CHUNK_PLANES
            for v in range(VREGS):
                ref[at, :, pl.ds(v * LANES, LANES)] = edge_ref[f, :, pl.ds(d * FACE + v * LANES, LANES)]
    place(states, MID, MID_AT, stay_ref, far_ref.at[:, :, pl.ds(2 * CHUNK, MID * FACE)], back_ref)
    for f, ref in enumerate(states):
        for d in range(HALO):
            for v in range(VREGS):
                lanes = pl.ds(v * LANES, LANES)
                part = pl.ds(d * FACE + v * LANES, LANES)
                mirror_low = ref[2 * HALO - 1 - d, :, lanes]
                ref[d, :, lanes] = jnp.where(st.has_below_x, st.rows(below_ref[f, :, part], st.below_x), mirror_low)
                mirror_high = ref[EDGE + HALO - 1 - d, :, lanes]
                ref[EDGE + HALO + d, :, lanes] = jnp.where(st.has_above_x, st.rows(above_ref[f, :, part], st.above_x), mirror_high)
    st.sweep(1, LATE_AT - 1, 4, (phi0, conc0), mob, (phi1, conc1))
    st.sweep(TOP_AT + 1, EXT - 1, 5, (phi0, conc0), mob, (phi1, conc1))
    st.sweep(2, LATE_AT - 2, 4, (phi1, conc1), mob, (phi2, conc2))
    st.sweep(TOP_AT + 2, EXT - 2, 3, (phi1, conc1), mob, (phi2, conc2))
    st.sweep(HALO, LATE_AT - 3, 4, (phi2, conc2), mob, (phase_ref, solute_ref), HALO)
    st.sweep(TOP_AT + 3, EXT - 3, 1, (phi2, conc2), mob, (phase_ref, solute_ref), HALO)
    for f, ref in enumerate(states):
        for n, x in enumerate((*range(LATE_AT - 3, LATE_AT), *range(TOP_AT, TOP_AT + 3))):
            kept0_ref[f, n] = ref[x]
    for f, ref in enumerate((phi1, conc1)):
        for n, x in enumerate((LATE_AT - 3, LATE_AT - 2, TOP_AT + 1, TOP_AT + 2)):
            kept1_ref[f, n] = ref[x]
    for f, ref in enumerate((phi2, conc2)):
        for n, x in enumerate((LATE_AT - 4, LATE_AT - 3, TOP_AT + 2, TOP_AT + 3)):
            kept2_ref[f, n] = ref[x]


BACK = LATE_AT - 4
LATE_PLANES = TOP_AT + 4 - BACK
OUT_FIRST = LATE_AT - 3
OUT_PLANES = TOP_AT + 3 - OUT_FIRST


def late_kernel(
    here_ref, stay_ref, far_ref, back_ref, nbr_ref, kept0_ref, kept1_ref, kept2_ref, _phase_in, _solute_in,
    phase_hbm, solute_hbm,
    phi0, conc0, mob, phi1, conc1, phi2, conc2, phase_ref, solute_ref, sems,
):
    st = Stencil(here_ref[0], nbr_ref[...])
    states = (phi0, conc0, mob)
    first, last = LATE_AT - BACK, TOP_AT - BACK
    for f, ref in enumerate(states):
        for n, x in enumerate((*range(first - 3, first), *range(last, last + 3))):
            ref[x] = kept0_ref[f, n]
    for f, ref in enumerate((phi1, conc1)):
        for n, x in enumerate((first - 3, first - 2, last + 1, last + 2)):
            ref[x] = kept1_ref[f, n]
    for f, ref in enumerate((phi2, conc2)):
        for n, x in enumerate((first - 4, first - 3, last + 2, last + 3)):
            ref[x] = kept2_ref[f, n]
    place(states, LATE, first, stay_ref, far_ref, back_ref)
    st.sweep(first - 1, last + 1, 5, (phi0, conc0), mob, (phi1, conc1))
    st.sweep(first - 2, last + 2, 4, (phi1, conc1), mob, (phi2, conc2))
    st.sweep(first - 3, last + 3, 7, (phi2, conc2), mob, (phase_ref, solute_ref), first - 3)
    copies = []
    for n, (ref, hbm) in enumerate(((phase_ref, phase_hbm), (solute_ref, solute_hbm))):
        lanes = pl.ds((OUT_FIRST - HALO) * FACE, OUT_PLANES * FACE)
        copies.append(pltpu.make_async_copy(ref, hbm.at[:, lanes], sems.at[n]))
    for copy in copies:
        copy.start()
    for copy in copies:
        copy.wait()


SMEM = pl.BlockSpec(memory_space=pltpu.SMEM)
VMEM = pl.BlockSpec(memory_space=pltpu.VMEM)
HBM = pl.BlockSpec(memory_space=pltpu.HBM)
ANY = pl.BlockSpec(memory_space=pl.ANY)
PARAMS = pltpu.CompilerParams(vmem_limit_bytes=32 * 2**20)


def shaped(planes, fields=FIELDS):
    return jax.ShapeDtypeStruct((fields, CAP, planes * FACE), jnp.float32)


def cost(moved, flops=10**6):
    return pl.CostEstimate(flops=flops, bytes_accessed=moved, transcendentals=0)


MB = 2**20


def on_device(old_phase, old_solute, old_mobility, new_global_slot, neighbors):
    count = lax.axis_size("blk")
    here = lax.axis_index("blk").astype(jnp.int32).reshape(1)
    olds = tuple(pltpu.with_memory_space_constraint(x, pltpu.HBM) for x in (old_phase, old_solute, old_mobility))
    devices = range(count)

    def sent(block, route):
        return lax.ppermute(block, "blk", [(p, q) for p, q in route if 0 <= q < count])

    def outward(p):
        return -2 if p % 2 == 0 else 2

    partner = [(p, p ^ 1) for p in devices]
    far_route = [(p, p + outward(p)) for p in devices]
    back_route = [(p, p - outward(p)) for p in devices]

    def after(block, *others):
        return lax.optimization_barrier((block, *others))[0]

    slots_hbm = pltpu.with_memory_space_constraint(new_global_slot, pltpu.HBM)
    old_shape = jax.ShapeDtypeStruct((OLD, CELLS), jnp.float32)
    *olds, merge, final, far_first, far_late = pl.pallas_call(
        pack_kernel,
        in_specs=[SMEM, HBM, HBM, HBM, HBM],
        out_specs=[VMEM] * 7,
        out_shape=[old_shape] * 3 + [shaped(EDGE)] * 2 + [shaped(2 * CHUNK_PLANES + MID), shaped(LATE)],
        scratch_shapes=[pltpu.SMEM((OLD,), jnp.int32), pltpu.SemaphoreType.DMA, pltpu.SemaphoreType.DMA((CHUNKS, FIELDS))],
        compiler_params=PARAMS,
        cost_estimate=cost(6 * MB),
        name="pack",
    )(here, slots_hbm, *olds)
    far_first_got = sent(far_first, far_route)
    merge_got = sent(merge, partner)
    final_got = sent(final, partner)

    three_parts = [shaped(2 * CHUNK_PLANES), shaped(MID), shaped(LATE)]
    back_edge, back_mid, back_late = pl.pallas_call(
        relay_kernel,
        in_specs=[SMEM, SMEM] + [VMEM] * 4,
        out_specs=[VMEM] * 3,
        out_shape=three_parts,
        compiler_params=PARAMS,
        cost_estimate=cost(6 * MB),
        name="relay",
    )(here, new_global_slot, *olds, merge_got)
    back_edge_got = sent(back_edge, back_route)

    stay_edge, stay_mid, stay_late = pl.pallas_call(
        stay_kernel,
        in_specs=[SMEM, SMEM] + [VMEM] * 4,
        out_specs=[VMEM] * 3,
        out_shape=three_parts,
        compiler_params=PARAMS,
        cost_estimate=cost(6 * MB),
        name="stay",
    )(here, new_global_slot, *olds, final_got)
    back_mid_got = sent(after(back_mid, back_edge_got, stay_edge), back_route)
    far_late_got = sent(after(far_late, far_first_got), far_route)

    edges = pl.BlockSpec((FIELDS, CAP, 2 * CHUNK), lambda i: (0, 0, 0))
    faces = pl.BlockSpec((FIELDS, CAP, HALO * FACE), lambda i: (0, 0, 0))
    edge, low, high = pl.pallas_call(
        face_kernel,
        grid=(1,),
        in_specs=[edges] * 3,
        out_specs=[edges, faces, faces],
        out_shape=[shaped(2 * CHUNK_PLANES), shaped(HALO), shaped(HALO)],
        compiler_params=PARAMS,
        cost_estimate=cost(3 * MB),
        name="faces",
    )(stay_edge, far_first_got, back_edge_got)
    below = sent(high, [(p, p + 1) for p in devices])
    above = sent(low, [(p, p - 1) for p in devices])
    back_late_got = sent(after(back_late, back_mid_got, below, above), back_route)

    state = pltpu.VMEM((EXT, CAP, FACE), jnp.float32)
    whole = jax.ShapeDtypeStruct((CAP, CELLS), jnp.float32)

    def kept(fields, planes):
        return jax.ShapeDtypeStruct((fields, planes, CAP, FACE), jnp.float32)

    phase, solute, kept0, kept1, kept2 = pl.pallas_call(
        early_kernel,
        in_specs=[SMEM] + [VMEM] * 7,
        out_specs=[VMEM] * 5,
        out_shape=[whole, whole, kept(3, 6), kept(2, 4), kept(2, 4)],
        scratch_shapes=[state] * 7,
        compiler_params=PARAMS,
        cost_estimate=cost(20 * MB),
        name="early_steps",
    )(here, edge, stay_mid, far_first_got, back_mid_got, below, above, neighbors)

    state = pltpu.VMEM((LATE_PLANES, CAP, FACE), jnp.float32)
    rows_out = pltpu.VMEM((CAP, OUT_PLANES * FACE), jnp.float32)
    phase, solute = pl.pallas_call(
        late_kernel,
        in_specs=[SMEM] + [VMEM] * 7 + [HBM] * 2,
        out_specs=[HBM] * 2,
        out_shape=[whole, whole],
        scratch_shapes=[state] * 7 + [rows_out] * 2 + [pltpu.SemaphoreType.DMA((2,))],
        input_output_aliases={8: 0, 9: 1},
        compiler_params=PARAMS,
        cost_estimate=cost(8 * MB),
        name="late_steps",
    )(here, stay_late, far_late_got, back_late_got, neighbors, kept0, kept1, kept2, phase, solute)
    return phase, solute


def solution(mesh):
    placed = (P("blk", None), P("blk", None), P("blk", None), P("blk"), P("blk", None))
    return jax.shard_map(
        on_device,
        mesh=mesh,
        in_specs=placed,
        out_specs=(P("blk", None), P("blk", None)),
        check_vma=False,
    )
```

```python
import functools

import jax
import jax.numpy as jnp
from jax import lax
from jax.experimental import pallas as pl
from jax.experimental.pallas import tpu as pltpu
from jax.sharding import PartitionSpec as P

EDGE = 32
FACE = EDGE * EDGE
CELLS = EDGE * FACE
CAP = 8
OLD = 16
FIELDS = 3
HALO = 3
CHUNK_PLANES = 4
CHUNK = CHUNK_PLANES * FACE
CHUNKS = EDGE // CHUNK_PLANES
LANES = 128
EXT = EDGE + 2 * HALO
MID = 16
LATE = EDGE - 2 * CHUNK_PLANES - MID
MID_CHUNKS = MID // CHUNK_PLANES
LATE_CHUNKS = LATE // CHUNK_PLANES
VREGS = FACE // LANES

time_step = 0.15
coupling = 1.5


def windows(slot_ref, here):
    first = slot_ref[0]
    count = jnp.int32(0)
    for i in range(OLD):
        count += (slot_ref[i] >= 0).astype(jnp.int32)
    amount = jnp.bitwise_and(first, CAP - 1)
    row = lax.broadcasted_iota(jnp.int32, (CAP, LANES), 0)

    def masks(k):
        index = row + ((here + k) * CAP - first)
        low = (index >= 0) & (index < CAP) & (index < count)
        high = (index >= CAP) & (index < count)
        return low, high

    return amount, masks


def picked(masks, low_rows, high_rows):
    low, high = masks
    return jnp.where(low, low_rows, jnp.where(high, high_rows, 0.0))


def side_of(here):
    return jnp.where(jnp.bitwise_and(here, 1) == 0, -1, 1)


def aligned(ref, lanes, amount):
    return pltpu.roll(ref[0:CAP, lanes], amount, 0), pltpu.roll(ref[CAP:OLD, lanes], amount, 0)


def chunk_at(i):
    return jnp.where(i == 0, 0, jnp.where(i == 1, CHUNKS - 1, i - 1))


def lanes_at(start, v):
    return pl.ds(pl.multiple_of(start + v * LANES, LANES), LANES)


def pack_kernel(
    here_ref, slot_hbm, phi_hbm, conc_hbm, mob_hbm,
    phi_ref, conc_ref, mob_ref, merge_ref, final_ref, far_ref, late_ref,
    slot_ref, slot_sem, sems,
):
    olds = tuple(zip((phi_hbm, conc_hbm, mob_hbm), (phi_ref, conc_ref, mob_ref)))

    def copies(i):
        lanes = pl.ds(pl.multiple_of(chunk_at(i) * CHUNK, CHUNK), CHUNK)
        return [pltpu.make_async_copy(hbm.at[:, lanes], ref.at[:, lanes], sems.at[i, f]) for f, (hbm, ref) in enumerate(olds)]

    slot_copy = pltpu.make_async_copy(slot_hbm, slot_ref, slot_sem)
    slot_copy.start()

    @pl.loop(0, CHUNKS)
    def _(i):
        for copy in copies(i):
            copy.start()

    slot_copy.wait()
    here = here_ref[0]
    side = side_of(here)
    amount, masks = windows(slot_ref, here)
    far, merge, final = masks(2 * side), masks(side), masks(-side)

    def fill(i, out_ref, out_start):
        start = chunk_at(i) * CHUNK
        for f, (_, ref) in enumerate(olds):
            for v in range(CHUNK // LANES):
                lanes = lanes_at(start, v)
                rows = aligned(ref, lanes, amount)
                merge_ref[f, :, lanes] = picked(merge, *rows)
                final_ref[f, :, lanes] = picked(final, *rows)
                out_ref[f, :, lanes_at(out_start, v)] = picked(far, *rows)

    first_steps = 2 + MID_CHUNKS

    @pl.loop(0, first_steps)
    def _(i):
        for copy in copies(i):
            copy.wait()
        fill(i, far_ref, i * CHUNK)

    @pl.loop(first_steps, CHUNKS)
    def _(i):
        for copy in copies(i):
            copy.wait()
        fill(i, late_ref, (i - first_steps) * CHUNK)


TOP = CHUNK_PLANES + MID + LATE
PARTS = (2 * CHUNK_PLANES, MID, LATE)
HALVES = (2 * CHUNK_PLANES, MID // 2, MID // 2, LATE // 2, LATE // 2)


def add_rows(masks, amount, old_refs, add_ref, part_refs, sizes):
    edge_ref, *rest = part_refs
    spans = [(edge_ref, 0, 0, CHUNK_PLANES), (edge_ref, CHUNK_PLANES, TOP, CHUNK_PLANES)]
    first = CHUNK_PLANES
    for part_ref, size in zip(rest, sizes[1:]):
        spans.append((part_ref, 0, first, size))
        first += size
    for out_ref, out_plane, plane, count in spans:

        @pl.loop(0, count // 2)
        def _(i):
            for f, ref in enumerate(old_refs):
                for v in range(2 * VREGS):
                    lanes = lanes_at((plane + 2 * i) * FACE, v)
                    value = picked(masks, *aligned(ref, lanes, amount)) + add_ref[f, :, lanes]
                    out_ref[f, :, lanes_at((out_plane + 2 * i) * FACE, v)] = value


def relay_kernel(here_ref, slot_ref, phi_ref, conc_ref, mob_ref, merge_ref, *part_refs):
    here = here_ref[0]
    amount, masks = windows(slot_ref, here)
    add_rows(masks(-2 * side_of(here)), amount, (phi_ref, conc_ref, mob_ref), merge_ref, part_refs, HALVES)


def stay_kernel(here_ref, slot_ref, phi_ref, conc_ref, mob_ref, final_ref, *part_refs):
    here = here_ref[0]
    amount, masks = windows(slot_ref, here)
    add_rows(masks(0), amount, (phi_ref, conc_ref, mob_ref), final_ref, part_refs, PARTS)


def face_kernel(stay_ref, far_ref, back_ref, edge_ref, low_ref, high_ref):
    first_high = (2 * CHUNK_PLANES - HALO) * FACE
    for f in range(FIELDS):
        for v in range(2 * CHUNK_PLANES * VREGS):
            lanes = pl.ds(v * LANES, LANES)
            value = stay_ref[f, :, lanes] + far_ref[f, :, lanes] + back_ref[f, :, lanes]
            edge_ref[f, :, lanes] = value
            at = v * LANES
            if at < HALO * FACE:
                low_ref[f, :, lanes] = value
            if at >= first_high:
                high_ref[f, :, pl.ds(at - first_high, LANES)] = value


class Stencil:
    def __init__(self, here, nbr):
        base = here * CAP
        self.nbr = nbr
        lane = lax.broadcasted_iota(jnp.int32, (CAP, LANES), 1)
        z = jnp.bitwise_and(lane, EDGE - 1)
        self.z_first, self.z_last = z == 0, z == EDGE - 1
        self.y_first, self.y_last = lane < EDGE, lane >= LANES - EDGE
        self.below_x, self.has_below_x = self.column(0, base - CAP)
        self.above_x, self.has_above_x = self.column(1, base + CAP)
        self.below_y, self.has_below_y = self.column(2, base)
        self.above_y, self.has_above_y = self.column(3, base)
        self.below_z, _ = self.column(4, base)
        self.above_z, _ = self.column(5, base)

    def column(self, c, start):
        wide = jnp.broadcast_to(self.nbr[:, c : c + 1], (CAP, LANES))
        valid = wide >= 0
        return jnp.where(valid, wide - start, 0), valid

    @staticmethod
    def rows(x, index):
        return jnp.take_along_axis(x, index, axis=0, mode="promise_in_bounds")

    def laplacian(self, ref, x):
        centre = [ref[x, :, pl.ds(v * LANES, LANES)] for v in range(VREGS)]
        lower = [pltpu.roll(c, EDGE, 1) for c in centre]
        upper = [pltpu.roll(c, LANES - EDGE, 1) for c in centre]
        out = []
        for v in range(VREGS):
            c = centre[v]
            lanes = pl.ds(v * LANES, LANES)
            if v:
                from_lower = lower[v - 1]
            else:
                from_lower = jnp.where(self.has_below_y, self.rows(lower[-1], self.below_y), c)
            if v < VREGS - 1:
                from_upper = upper[v + 1]
            else:
                from_upper = jnp.where(self.has_above_y, self.rows(upper[0], self.above_y), c)
            prev_y = jnp.where(self.y_first, from_lower, lower[v])
            next_y = jnp.where(self.y_last, from_upper, upper[v])
            prev_z = jnp.where(self.z_first, pltpu.roll(self.rows(c, self.below_z), LANES - EDGE + 1, 1), pltpu.roll(c, 1, 1))
            next_z = jnp.where(self.z_last, pltpu.roll(self.rows(c, self.above_z), EDGE - 1, 1), pltpu.roll(c, LANES - 1, 1))
            total = (ref[x - 1, :, lanes] + ref[x + 1, :, lanes]) + (prev_y + next_y) + (prev_z + next_z)
            out.append(total - 6.0 * c)
        return out, centre

    def advance(self, phi_ref, conc_ref, mob_ref, x, store):
        lapl_phi, phis = self.laplacian(phi_ref, x)
        lapl_conc, concs = self.laplacian(conc_ref, x)
        for v in range(VREGS):
            phi, conc = phis[v], concs[v]
            square = phi * phi
            wetting = 1.0 - square
            drive = lapl_phi[v] + phi - square * phi - coupling * conc * wetting * wetting
            change = time_step * mob_ref[x, :, pl.ds(v * LANES, LANES)] * drive
            store(v, phi + change, conc + time_step * lapl_conc[v] + 0.5 * change)

    def sweep(self, first, last, unroll, source, mob_ref, target, shift=None):
        phi_ref, conc_ref = source
        phi_out, conc_out = target

        def one(x):
            def store(v, phi, conc):
                if shift is None:
                    where = (x, slice(None), pl.ds(v * LANES, LANES))
                else:
                    where = (slice(None), pl.ds(pl.multiple_of((x - shift) * FACE + v * LANES, LANES), LANES))
                phi_out[where] = phi
                conc_out[where] = conc

            self.advance(phi_ref, conc_ref, mob_ref, x, store)

        whole = first + (last - first) // unroll * unroll
        if whole > first:

            @pl.loop(0, (whole - first) // unroll)
            def _(i):
                for u in range(unroll):
                    one(first + i * unroll + u)

        for x in range(whole, last):
            one(x)


def place(states, planes, at, *parts):
    for f, ref in enumerate(states):

        @pl.loop(0, planes // 2)
        def _(i):
            for u in range(2):
                x = 2 * i + u
                for v in range(VREGS):
                    value = sum(part[f, :, lanes_at((x + first) * FACE, v)] for part, first in parts)
                    ref[x + at, :, pl.ds(v * LANES, LANES)] = value


MID_AT = HALO + CHUNK_PLANES
LATE_AT = MID_AT + MID
TOP_AT = LATE_AT + LATE


def early_kernel(
    here_ref, edge_ref, stay_ref, far_ref, back_low_ref, back_high_ref, below_ref, above_ref, nbr_ref,
    phase_ref, solute_ref, kept0_ref, kept1_ref, kept2_ref,
    phi0, conc0, mob, phi1, conc1, phi2, conc2,
):
    st = Stencil(here_ref[0], nbr_ref[...])
    back_refs = (back_low_ref, back_high_ref)
    states = (phi0, conc0, mob)
    for f, ref in enumerate(states):
        for d in range(2 * CHUNK_PLANES):
            at = HALO + d if d < CHUNK_PLANES else TOP_AT + d - CHUNK_PLANES
            for v in range(VREGS):
                ref[at, :, pl.ds(v * LANES, LANES)] = edge_ref[f, :, pl.ds(d * FACE + v * LANES, LANES)]
    for n, back_ref in enumerate(back_refs):
        done = n * MID // 2
        place(states, MID // 2, MID_AT + done, (stay_ref, done), (far_ref, 2 * CHUNK_PLANES + done), (back_ref, 0))
    for f, ref in enumerate(states):
        for d in range(HALO):
            for v in range(VREGS):
                lanes = pl.ds(v * LANES, LANES)
                part = pl.ds(d * FACE + v * LANES, LANES)
                mirror_low = ref[2 * HALO - 1 - d, :, lanes]
                ref[d, :, lanes] = jnp.where(st.has_below_x, st.rows(below_ref[f, :, part], st.below_x), mirror_low)
                mirror_high = ref[EDGE + HALO - 1 - d, :, lanes]
                ref[EDGE + HALO + d, :, lanes] = jnp.where(st.has_above_x, st.rows(above_ref[f, :, part], st.above_x), mirror_high)
    st.sweep(1, LATE_AT - 1, 4, (phi0, conc0), mob, (phi1, conc1))
    st.sweep(TOP_AT + 1, EXT - 1, 5, (phi0, conc0), mob, (phi1, conc1))
    st.sweep(2, LATE_AT - 2, 4, (phi1, conc1), mob, (phi2, conc2))
    st.sweep(TOP_AT + 2, EXT - 2, 3, (phi1, conc1), mob, (phi2, conc2))
    st.sweep(HALO, LATE_AT - 3, 4, (phi2, conc2), mob, (phase_ref, solute_ref), HALO)
    st.sweep(TOP_AT + 3, EXT - 3, 1, (phi2, conc2), mob, (phase_ref, solute_ref), HALO)
    for f, ref in enumerate(states):
        for n, x in enumerate((*range(LATE_AT - 3, LATE_AT), *range(TOP_AT, TOP_AT + 3))):
            kept0_ref[f, n] = ref[x]
    for f, ref in enumerate((phi1, conc1)):
        for n, x in enumerate((LATE_AT - 3, LATE_AT - 2, TOP_AT + 1, TOP_AT + 2)):
            kept1_ref[f, n] = ref[x]
    for f, ref in enumerate((phi2, conc2)):
        for n, x in enumerate((LATE_AT - 4, LATE_AT - 3, TOP_AT + 2, TOP_AT + 3)):
            kept2_ref[f, n] = ref[x]


BACK = LATE_AT - 4
LATE_PLANES = TOP_AT + 4 - BACK
OUT_FIRST = LATE_AT - 3
OUT_PLANES = TOP_AT + 3 - OUT_FIRST


def late_kernel(
    here_ref, stay_ref, far_ref, back_low_ref, back_high_ref, nbr_ref, kept0_ref, kept1_ref, kept2_ref, _phase_in, _solute_in,
    phase_hbm, solute_hbm,
    phi0, conc0, mob, phi1, conc1, phi2, conc2, phase_ref, solute_ref, sems,
):
    st = Stencil(here_ref[0], nbr_ref[...])
    back_refs = (back_low_ref, back_high_ref)
    states = (phi0, conc0, mob)
    first, last = LATE_AT - BACK, TOP_AT - BACK
    for f, ref in enumerate(states):
        for n, x in enumerate((*range(first - 3, first), *range(last, last + 3))):
            ref[x] = kept0_ref[f, n]
    for f, ref in enumerate((phi1, conc1)):
        for n, x in enumerate((first - 3, first - 2, last + 1, last + 2)):
            ref[x] = kept1_ref[f, n]
    for f, ref in enumerate((phi2, conc2)):
        for n, x in enumerate((first - 4, first - 3, last + 2, last + 3)):
            ref[x] = kept2_ref[f, n]
    for n, back_ref in enumerate(back_refs):
        done = n * LATE // 2
        place(states, LATE // 2, first + done, (stay_ref, done), (far_ref, done), (back_ref, 0))
    st.sweep(first - 1, last + 1, 5, (phi0, conc0), mob, (phi1, conc1))
    st.sweep(first - 2, last + 2, 4, (phi1, conc1), mob, (phi2, conc2))
    st.sweep(first - 3, last + 3, 7, (phi2, conc2), mob, (phase_ref, solute_ref), first - 3)
    copies = []
    for n, (ref, hbm) in enumerate(((phase_ref, phase_hbm), (solute_ref, solute_hbm))):
        lanes = pl.ds((OUT_FIRST - HALO) * FACE, OUT_PLANES * FACE)
        copies.append(pltpu.make_async_copy(ref, hbm.at[:, lanes], sems.at[n]))
    for copy in copies:
        copy.start()
    for copy in copies:
        copy.wait()


SMEM = pl.BlockSpec(memory_space=pltpu.SMEM)
VMEM = pl.BlockSpec(memory_space=pltpu.VMEM)
HBM = pl.BlockSpec(memory_space=pltpu.HBM)
ANY = pl.BlockSpec(memory_space=pl.ANY)
PARAMS = pltpu.CompilerParams(vmem_limit_bytes=32 * 2**20)


def shaped(planes, fields=FIELDS):
    return jax.ShapeDtypeStruct((fields, CAP, planes * FACE), jnp.float32)


def cost(moved, flops=10**6):
    return pl.CostEstimate(flops=flops, bytes_accessed=moved, transcendentals=0)


MB = 2**20


def on_device(old_phase, old_solute, old_mobility, new_global_slot, neighbors):
    count = lax.axis_size("blk")
    here = lax.axis_index("blk").astype(jnp.int32).reshape(1)
    olds = tuple(pltpu.with_memory_space_constraint(x, pltpu.HBM) for x in (old_phase, old_solute, old_mobility))
    devices = range(count)

    def sent(block, route):
        return lax.ppermute(block, "blk", [(p, q) for p, q in route if 0 <= q < count])

    def outward(p):
        return -2 if p % 2 == 0 else 2

    partner = [(p, p ^ 1) for p in devices]
    far_route = [(p, p + outward(p)) for p in devices]
    back_route = [(p, p - outward(p)) for p in devices]

    def after(block, *others):
        return lax.optimization_barrier((block, *others))[0]

    slots_hbm = pltpu.with_memory_space_constraint(new_global_slot, pltpu.HBM)
    old_shape = jax.ShapeDtypeStruct((OLD, CELLS), jnp.float32)
    *olds, merge, final, far_first, far_late = pl.pallas_call(
        pack_kernel,
        in_specs=[SMEM, HBM, HBM, HBM, HBM],
        out_specs=[VMEM] * 7,
        out_shape=[old_shape] * 3 + [shaped(EDGE)] * 2 + [shaped(2 * CHUNK_PLANES + MID), shaped(LATE)],
        scratch_shapes=[pltpu.SMEM((OLD,), jnp.int32), pltpu.SemaphoreType.DMA, pltpu.SemaphoreType.DMA((CHUNKS, FIELDS))],
        compiler_params=PARAMS,
        cost_estimate=cost(6 * MB),
        name="pack",
    )(here, slots_hbm, *olds)
    far_first_got = sent(far_first, far_route)
    merge_got = sent(merge, partner)
    final_got = sent(final, partner)

    back_edge, *back_mid, back_late_low, back_late_high = pl.pallas_call(
        relay_kernel,
        in_specs=[SMEM, SMEM] + [VMEM] * 4,
        out_specs=[VMEM] * len(HALVES),
        out_shape=[shaped(size) for size in HALVES],
        compiler_params=PARAMS,
        cost_estimate=cost(6 * MB),
        name="relay",
    )(here, new_global_slot, *olds, merge_got)
    back_edge_got = sent(back_edge, back_route)

    stay_edge, stay_mid, stay_late = pl.pallas_call(
        stay_kernel,
        in_specs=[SMEM, SMEM] + [VMEM] * 4,
        out_specs=[VMEM] * 3,
        out_shape=[shaped(size) for size in PARTS],
        compiler_params=PARAMS,
        cost_estimate=cost(6 * MB),
        name="stay",
    )(here, new_global_slot, *olds, final_got)
    back_mid_got = [sent(after(half, back_edge_got, stay_edge), back_route) for half in back_mid]
    far_late_got = sent(after(far_late, far_first_got), far_route)

    edges = pl.BlockSpec((FIELDS, CAP, 2 * CHUNK), lambda i: (0, 0, 0))
    faces = pl.BlockSpec((FIELDS, CAP, HALO * FACE), lambda i: (0, 0, 0))
    edge, low, high = pl.pallas_call(
        face_kernel,
        grid=(1,),
        in_specs=[edges] * 3,
        out_specs=[edges, faces, faces],
        out_shape=[shaped(2 * CHUNK_PLANES), shaped(HALO), shaped(HALO)],
        compiler_params=PARAMS,
        cost_estimate=cost(3 * MB),
        name="faces",
    )(stay_edge, far_first_got, back_edge_got)
    below = sent(high, [(p, p + 1) for p in devices])
    above = sent(low, [(p, p - 1) for p in devices])
    back_late = (back_late_low, back_late_high)
    back_late_got = [sent(after(half, *back_mid_got, below, above), back_route) for half in back_late]

    state = pltpu.VMEM((EXT, CAP, FACE), jnp.float32)
    whole = jax.ShapeDtypeStruct((CAP, CELLS), jnp.float32)

    def kept(fields, planes):
        return jax.ShapeDtypeStruct((fields, planes, CAP, FACE), jnp.float32)

    phase, solute, kept0, kept1, kept2 = pl.pallas_call(
        early_kernel,
        in_specs=[SMEM] + [VMEM] * 8,
        out_specs=[VMEM] * 5,
        out_shape=[whole, whole, kept(3, 6), kept(2, 4), kept(2, 4)],
        scratch_shapes=[state] * 7,
        compiler_params=PARAMS,
        cost_estimate=cost(20 * MB),
        name="early_steps",
    )(here, edge, stay_mid, far_first_got, *back_mid_got, below, above, neighbors)

    state = pltpu.VMEM((LATE_PLANES, CAP, FACE), jnp.float32)
    rows_out = pltpu.VMEM((CAP, OUT_PLANES * FACE), jnp.float32)
    phase, solute = pl.pallas_call(
        late_kernel,
        in_specs=[SMEM] + [VMEM] * 8 + [HBM] * 2,
        out_specs=[HBM] * 2,
        out_shape=[whole, whole],
        scratch_shapes=[state] * 7 + [rows_out] * 2 + [pltpu.SemaphoreType.DMA((2,))],
        input_output_aliases={9: 0, 10: 1},
        compiler_params=PARAMS,
        cost_estimate=cost(8 * MB),
        name="late_steps",
    )(here, stay_late, far_late_got, *back_late_got, neighbors, kept0, kept1, kept2, phase, solute)
    return phase, solute


def solution(mesh):
    placed = (P("blk", None), P("blk", None), P("blk", None), P("blk"), P("blk", None))
    return jax.shard_map(
        on_device,
        mesh=mesh,
        in_specs=placed,
        out_specs=(P("blk", None), P("blk", None)),
        check_vma=False,
    )
```

```python
import functools

import jax
import jax.numpy as jnp
from jax import lax
from jax.experimental import pallas as pl
from jax.experimental.pallas import tpu as pltpu
from jax.sharding import PartitionSpec as P

EDGE = 32
FACE = EDGE * EDGE
CELLS = EDGE * FACE
CAP = 8
OLD = 16
FIELDS = 3
HALO = 3
CHUNK_PLANES = 4
CHUNK = CHUNK_PLANES * FACE
CHUNKS = EDGE // CHUNK_PLANES
LANES = 128
EXT = EDGE + 2 * HALO
MID = 20
LATE = EDGE - 2 * CHUNK_PLANES - MID
MID_CHUNKS = MID // CHUNK_PLANES
LATE_CHUNKS = LATE // CHUNK_PLANES
VREGS = FACE // LANES

time_step = 0.15
coupling = 1.5


def windows(slot_ref, here):
    first = slot_ref[0]
    count = jnp.int32(0)
    for i in range(OLD):
        count += (slot_ref[i] >= 0).astype(jnp.int32)
    amount = jnp.bitwise_and(first, CAP - 1)
    row = lax.broadcasted_iota(jnp.int32, (CAP, LANES), 0)

    def masks(k):
        index = row + ((here + k) * CAP - first)
        low = (index >= 0) & (index < CAP) & (index < count)
        high = (index >= CAP) & (index < count)
        return low, high

    return amount, masks


def picked(masks, low_rows, high_rows):
    low, high = masks
    return jnp.where(low, low_rows, jnp.where(high, high_rows, 0.0))


def side_of(here):
    return jnp.where(jnp.bitwise_and(here, 1) == 0, -1, 1)


def aligned(ref, lanes, amount):
    return pltpu.roll(ref[0:CAP, lanes], amount, 0), pltpu.roll(ref[CAP:OLD, lanes], amount, 0)


def chunk_at(i):
    return jnp.where(i == 0, 0, jnp.where(i == 1, CHUNKS - 1, i - 1))


def lanes_at(start, v):
    return pl.ds(pl.multiple_of(start + v * LANES, LANES), LANES)


def pack_kernel(
    here_ref, slot_hbm, phi_hbm, conc_hbm, mob_hbm,
    phi_ref, conc_ref, mob_ref, merge_ref, final_ref, far_ref, late_ref,
    slot_ref, slot_sem, sems,
):
    olds = tuple(zip((phi_hbm, conc_hbm, mob_hbm), (phi_ref, conc_ref, mob_ref)))

    def copies(i):
        lanes = pl.ds(pl.multiple_of(chunk_at(i) * CHUNK, CHUNK), CHUNK)
        return [pltpu.make_async_copy(hbm.at[:, lanes], ref.at[:, lanes], sems.at[i, f]) for f, (hbm, ref) in enumerate(olds)]

    slot_copy = pltpu.make_async_copy(slot_hbm, slot_ref, slot_sem)
    slot_copy.start()

    @pl.loop(0, CHUNKS)
    def _(i):
        for copy in copies(i):
            copy.start()

    slot_copy.wait()
    here = here_ref[0]
    side = side_of(here)
    amount, masks = windows(slot_ref, here)
    far, merge, final = masks(2 * side), masks(side), masks(-side)

    def fill(i, out_ref, out_start):
        start = chunk_at(i) * CHUNK
        for f, (_, ref) in enumerate(olds):
            for v in range(CHUNK // LANES):
                lanes = lanes_at(start, v)
                rows = aligned(ref, lanes, amount)
                merge_ref[f, :, lanes] = picked(merge, *rows)
                final_ref[f, :, lanes] = picked(final, *rows)
                out_ref[f, :, lanes_at(out_start, v)] = picked(far, *rows)

    first_steps = 2 + MID_CHUNKS

    @pl.loop(0, first_steps)
    def _(i):
        for copy in copies(i):
            copy.wait()
        fill(i, far_ref, i * CHUNK)

    @pl.loop(first_steps, CHUNKS)
    def _(i):
        for copy in copies(i):
            copy.wait()
        fill(i, late_ref, (i - first_steps) * CHUNK)


def add_rows(masks, amount, old_refs, add_ref, part_refs):
    edge_ref, mid_ref, late_ref = part_refs
    high = CHUNK_PLANES + MID + LATE
    for out_ref, out_plane, plane, count in (
        (edge_ref, 0, 0, CHUNK_PLANES),
        (edge_ref, CHUNK_PLANES, high, CHUNK_PLANES),
        (mid_ref, 0, CHUNK_PLANES, MID),
        (late_ref, 0, CHUNK_PLANES + MID, LATE),
    ):

        @pl.loop(0, count // 2)
        def _(i):
            for f, ref in enumerate(old_refs):
                for v in range(2 * VREGS):
                    lanes = lanes_at((plane + 2 * i) * FACE, v)
                    value = picked(masks, *aligned(ref, lanes, amount)) + add_ref[f, :, lanes]
                    out_ref[f, :, lanes_at((out_plane + 2 * i) * FACE, v)] = value


def relay_kernel(here_ref, slot_ref, phi_ref, conc_ref, mob_ref, merge_ref, *part_refs):
    here = here_ref[0]
    amount, masks = windows(slot_ref, here)
    add_rows(masks(-2 * side_of(here)), amount, (phi_ref, conc_ref, mob_ref), merge_ref, part_refs)


def stay_kernel(here_ref, slot_ref, phi_ref, conc_ref, mob_ref, final_ref, *part_refs):
    here = here_ref[0]
    amount, masks = windows(slot_ref, here)
    add_rows(masks(0), amount, (phi_ref, conc_ref, mob_ref), final_ref, part_refs)


def face_kernel(stay_ref, far_ref, back_ref, edge_ref, low_ref, high_ref):
    first_high = (2 * CHUNK_PLANES - HALO) * FACE
    for f in range(FIELDS):
        for v in range(2 * CHUNK_PLANES * VREGS):
            lanes = pl.ds(v * LANES, LANES)
            value = stay_ref[f, :, lanes] + far_ref[f, :, lanes] + back_ref[f, :, lanes]
            edge_ref[f, :, lanes] = value
            at = v * LANES
            if at < HALO * FACE:
                low_ref[f, :, lanes] = value
            if at >= first_high:
                high_ref[f, :, pl.ds(at - first_high, LANES)] = value


class Stencil:
    def __init__(self, here, nbr):
        base = here * CAP
        self.nbr = nbr
        lane = lax.broadcasted_iota(jnp.int32, (CAP, LANES), 1)
        z = jnp.bitwise_and(lane, EDGE - 1)
        self.z_first, self.z_last = z == 0, z == EDGE - 1
        self.y_first, self.y_last = lane < EDGE, lane >= LANES - EDGE
        self.below_x, self.has_below_x = self.column(0, base - CAP)
        self.above_x, self.has_above_x = self.column(1, base + CAP)
        self.below_y, self.has_below_y = self.column(2, base)
        self.above_y, self.has_above_y = self.column(3, base)
        self.below_z, _ = self.column(4, base)
        self.above_z, _ = self.column(5, base)

    def column(self, c, start):
        wide = jnp.broadcast_to(self.nbr[:, c : c + 1], (CAP, LANES))
        valid = wide >= 0
        return jnp.where(valid, wide - start, 0), valid

    @staticmethod
    def rows(x, index):
        return jnp.take_along_axis(x, index, axis=0, mode="promise_in_bounds")

    def laplacian(self, ref, x):
        centre = [ref[x, :, pl.ds(v * LANES, LANES)] for v in range(VREGS)]
        lower = [pltpu.roll(c, EDGE, 1) for c in centre]
        upper = [pltpu.roll(c, LANES - EDGE, 1) for c in centre]
        out = []
        for v in range(VREGS):
            c = centre[v]
            lanes = pl.ds(v * LANES, LANES)
            if v:
                from_lower = lower[v - 1]
            else:
                from_lower = jnp.where(self.has_below_y, self.rows(lower[-1], self.below_y), c)
            if v < VREGS - 1:
                from_upper = upper[v + 1]
            else:
                from_upper = jnp.where(self.has_above_y, self.rows(upper[0], self.above_y), c)
            prev_y = jnp.where(self.y_first, from_lower, lower[v])
            next_y = jnp.where(self.y_last, from_upper, upper[v])
            prev_z = jnp.where(self.z_first, pltpu.roll(self.rows(c, self.below_z), LANES - EDGE + 1, 1), pltpu.roll(c, 1, 1))
            next_z = jnp.where(self.z_last, pltpu.roll(self.rows(c, self.above_z), EDGE - 1, 1), pltpu.roll(c, LANES - 1, 1))
            total = (ref[x - 1, :, lanes] + ref[x + 1, :, lanes]) + (prev_y + next_y) + (prev_z + next_z)
            out.append(total - 6.0 * c)
        return out, centre

    def advance(self, phi_ref, conc_ref, mob_ref, x, store):
        lapl_phi, phis = self.laplacian(phi_ref, x)
        lapl_conc, concs = self.laplacian(conc_ref, x)
        for v in range(VREGS):
            phi, conc = phis[v], concs[v]
            square = phi * phi
            wetting = 1.0 - square
            drive = lapl_phi[v] + phi - square * phi - coupling * conc * wetting * wetting
            change = time_step * mob_ref[x, :, pl.ds(v * LANES, LANES)] * drive
            store(v, phi + change, conc + time_step * lapl_conc[v] + 0.5 * change)

    def sweep(self, first, last, unroll, source, mob_ref, target, shift=None):
        phi_ref, conc_ref = source
        phi_out, conc_out = target

        def one(x):
            def store(v, phi, conc):
                if shift is None:
                    where = (x, slice(None), pl.ds(v * LANES, LANES))
                else:
                    where = (slice(None), pl.ds(pl.multiple_of((x - shift) * FACE + v * LANES, LANES), LANES))
                phi_out[where] = phi
                conc_out[where] = conc

            self.advance(phi_ref, conc_ref, mob_ref, x, store)

        whole = first + (last - first) // unroll * unroll
        if whole > first:

            @pl.loop(0, (whole - first) // unroll)
            def _(i):
                for u in range(unroll):
                    one(first + i * unroll + u)

        for x in range(whole, last):
            one(x)


def place(states, planes, at, *parts):
    for f, ref in enumerate(states):

        @pl.loop(0, planes)
        def _(x):
            for v in range(VREGS):
                lanes = pl.ds(pl.multiple_of(x * FACE + v * LANES, LANES), LANES)
                value = parts[0][f, :, lanes]
                for part in parts[1:]:
                    value = value + part[f, :, lanes]
                ref[x + at, :, pl.ds(v * LANES, LANES)] = value


MID_AT = HALO + CHUNK_PLANES
LATE_AT = MID_AT + MID
TOP_AT = LATE_AT + LATE


def early_kernel(
    here_ref, edge_ref, stay_ref, far_ref, back_ref, below_ref, above_ref, nbr_ref,
    phase_ref, solute_ref, kept0_ref, kept1_ref, kept2_ref,
    phi0, conc0, mob, phi1, conc1, phi2, conc2,
):
    st = Stencil(here_ref[0], nbr_ref[...])
    states = (phi0, conc0, mob)
    for f, ref in enumerate(states):
        for d in range(2 * CHUNK_PLANES):
            at = HALO + d if d < CHUNK_PLANES else TOP_AT + d - CHUNK_PLANES
            for v in range(VREGS):
                ref[at, :, pl.ds(v * LANES, LANES)] = edge_ref[f, :, pl.ds(d * FACE + v * LANES, LANES)]
    place(states, MID, MID_AT, stay_ref, far_ref.at[:, :, pl.ds(2 * CHUNK, MID * FACE)], back_ref)
    for f, ref in enumerate(states):
        for d in range(HALO):
            for v in range(VREGS):
                lanes = pl.ds(v * LANES, LANES)
                part = pl.ds(d * FACE + v * LANES, LANES)
                mirror_low = ref[2 * HALO - 1 - d, :, lanes]
                ref[d, :, lanes] = jnp.where(st.has_below_x, st.rows(below_ref[f, :, part], st.below_x), mirror_low)
                mirror_high = ref[EDGE + HALO - 1 - d, :, lanes]
                ref[EDGE + HALO + d, :, lanes] = jnp.where(st.has_above_x, st.rows(above_ref[f, :, part], st.above_x), mirror_high)
    st.sweep(1, LATE_AT - 1, 5, (phi0, conc0), mob, (phi1, conc1))
    st.sweep(TOP_AT + 1, EXT - 1, 5, (phi0, conc0), mob, (phi1, conc1))
    st.sweep(2, LATE_AT - 2, 4, (phi1, conc1), mob, (phi2, conc2))
    st.sweep(TOP_AT + 2, EXT - 2, 3, (phi1, conc1), mob, (phi2, conc2))
    st.sweep(HALO, LATE_AT - 3, 3, (phi2, conc2), mob, (phase_ref, solute_ref), HALO)
    st.sweep(TOP_AT + 3, EXT - 3, 1, (phi2, conc2), mob, (phase_ref, solute_ref), HALO)
    for f, ref in enumerate(states):
        for n, x in enumerate((*range(LATE_AT - 3, LATE_AT), *range(TOP_AT, TOP_AT + 3))):
            kept0_ref[f, n] = ref[x]
    for f, ref in enumerate((phi1, conc1)):
        for n, x in enumerate((LATE_AT - 3, LATE_AT - 2, TOP_AT + 1, TOP_AT + 2)):
            kept1_ref[f, n] = ref[x]
    for f, ref in enumerate((phi2, conc2)):
        for n, x in enumerate((LATE_AT - 4, LATE_AT - 3, TOP_AT + 2, TOP_AT + 3)):
            kept2_ref[f, n] = ref[x]


BACK = LATE_AT - 4
LATE_PLANES = TOP_AT + 4 - BACK
OUT_FIRST = LATE_AT - 3
OUT_PLANES = TOP_AT + 3 - OUT_FIRST


def late_kernel(
    here_ref, stay_ref, far_ref, back_ref, nbr_ref, kept0_ref, kept1_ref, kept2_ref, _phase_in, _solute_in,
    phase_hbm, solute_hbm,
    phi0, conc0, mob, phi1, conc1, phi2, conc2, phase_ref, solute_ref, sems,
):
    st = Stencil(here_ref[0], nbr_ref[...])
    states = (phi0, conc0, mob)
    first, last = LATE_AT - BACK, TOP_AT - BACK
    for f, ref in enumerate(states):
        for n, x in enumerate((*range(first - 3, first), *range(last, last + 3))):
            ref[x] = kept0_ref[f, n]
    for f, ref in enumerate((phi1, conc1)):
        for n, x in enumerate((first - 3, first - 2, last + 1, last + 2)):
            ref[x] = kept1_ref[f, n]
    for f, ref in enumerate((phi2, conc2)):
        for n, x in enumerate((first - 4, first - 3, last + 2, last + 3)):
            ref[x] = kept2_ref[f, n]
    place(states, LATE, first, stay_ref, far_ref, back_ref)
    st.sweep(first - 1, last + 1, 6, (phi0, conc0), mob, (phi1, conc1))
    st.sweep(first - 2, last + 2, 4, (phi1, conc1), mob, (phi2, conc2))
    st.sweep(first - 3, last + 3, 5, (phi2, conc2), mob, (phase_ref, solute_ref), first - 3)
    copies = []
    for n, (ref, hbm) in enumerate(((phase_ref, phase_hbm), (solute_ref, solute_hbm))):
        lanes = pl.ds((OUT_FIRST - HALO) * FACE, OUT_PLANES * FACE)
        copies.append(pltpu.make_async_copy(ref, hbm.at[:, lanes], sems.at[n]))
    for copy in copies:
        copy.start()
    for copy in copies:
        copy.wait()


SMEM = pl.BlockSpec(memory_space=pltpu.SMEM)
VMEM = pl.BlockSpec(memory_space=pltpu.VMEM)
HBM = pl.BlockSpec(memory_space=pltpu.HBM)
ANY = pl.BlockSpec(memory_space=pl.ANY)
PARAMS = pltpu.CompilerParams(vmem_limit_bytes=32 * 2**20)


def shaped(planes, fields=FIELDS):
    return jax.ShapeDtypeStruct((fields, CAP, planes * FACE), jnp.float32)


def cost(moved, flops=10**6):
    return pl.CostEstimate(flops=flops, bytes_accessed=moved, transcendentals=0)


MB = 2**20


def on_device(old_phase, old_solute, old_mobility, new_global_slot, neighbors):
    count = lax.axis_size("blk")
    here = lax.axis_index("blk").astype(jnp.int32).reshape(1)
    olds = tuple(pltpu.with_memory_space_constraint(x, pltpu.HBM) for x in (old_phase, old_solute, old_mobility))
    devices = range(count)

    def sent(block, route):
        return lax.ppermute(block, "blk", [(p, q) for p, q in route if 0 <= q < count])

    def outward(p):
        return -2 if p % 2 == 0 else 2

    partner = [(p, p ^ 1) for p in devices]
    far_route = [(p, p + outward(p)) for p in devices]
    back_route = [(p, p - outward(p)) for p in devices]

    def after(block, *others):
        return lax.optimization_barrier((block, *others))[0]

    slots_hbm = pltpu.with_memory_space_constraint(new_global_slot, pltpu.HBM)
    old_shape = jax.ShapeDtypeStruct((OLD, CELLS), jnp.float32)
    *olds, merge, final, far_first, far_late = pl.pallas_call(
        pack_kernel,
        in_specs=[SMEM, HBM, HBM, HBM, HBM],
        out_specs=[VMEM] * 7,
        out_shape=[old_shape] * 3 + [shaped(EDGE)] * 2 + [shaped(2 * CHUNK_PLANES + MID), shaped(LATE)],
        scratch_shapes=[pltpu.SMEM((OLD,), jnp.int32), pltpu.SemaphoreType.DMA, pltpu.SemaphoreType.DMA((CHUNKS, FIELDS))],
        compiler_params=PARAMS,
        cost_estimate=cost(6 * MB),
        name="pack",
    )(here, slots_hbm, *olds)
    far_first_got = sent(far_first, far_route)
    merge_got = sent(merge, partner)
    final_got = sent(final, partner)

    three_parts = [shaped(2 * CHUNK_PLANES), shaped(MID), shaped(LATE)]
    back_edge, back_mid, back_late = pl.pallas_call(
        relay_kernel,
        in_specs=[SMEM, SMEM] + [VMEM] * 4,
        out_specs=[VMEM] * 3,
        out_shape=three_parts,
        compiler_params=PARAMS,
        cost_estimate=cost(6 * MB),
        name="relay",
    )(here, new_global_slot, *olds, merge_got)
    back_edge_got = sent(back_edge, back_route)

    stay_edge, stay_mid, stay_late = pl.pallas_call(
        stay_kernel,
        in_specs=[SMEM, SMEM] + [VMEM] * 4,
        out_specs=[VMEM] * 3,
        out_shape=three_parts,
        compiler_params=PARAMS,
        cost_estimate=cost(6 * MB),
        name="stay",
    )(here, new_global_slot, *olds, final_got)
    back_mid_got = sent(after(back_mid, back_edge_got, stay_edge), back_route)
    far_late_got = sent(after(far_late, far_first_got), far_route)

    edges = pl.BlockSpec((FIELDS, CAP, 2 * CHUNK), lambda i: (0, 0, 0))
    faces = pl.BlockSpec((FIELDS, CAP, HALO * FACE), lambda i: (0, 0, 0))
    edge, low, high = pl.pallas_call(
        face_kernel,
        grid=(1,),
        in_specs=[edges] * 3,
        out_specs=[edges, faces, faces],
        out_shape=[shaped(2 * CHUNK_PLANES), shaped(HALO), shaped(HALO)],
        compiler_params=PARAMS,
        cost_estimate=cost(3 * MB),
        name="faces",
    )(stay_edge, far_first_got, back_edge_got)
    below = sent(high, [(p, p + 1) for p in devices])
    above = sent(low, [(p, p - 1) for p in devices])
    back_late_got = sent(after(back_late, back_mid_got, below, above), back_route)

    state = pltpu.VMEM((EXT, CAP, FACE), jnp.float32)
    whole = jax.ShapeDtypeStruct((CAP, CELLS), jnp.float32)

    def kept(fields, planes):
        return jax.ShapeDtypeStruct((fields, planes, CAP, FACE), jnp.float32)

    phase, solute, kept0, kept1, kept2 = pl.pallas_call(
        early_kernel,
        in_specs=[SMEM] + [VMEM] * 7,
        out_specs=[VMEM] * 5,
        out_shape=[whole, whole, kept(3, 6), kept(2, 4), kept(2, 4)],
        scratch_shapes=[state] * 7,
        compiler_params=PARAMS,
        cost_estimate=cost(20 * MB),
        name="early_steps",
    )(here, edge, stay_mid, far_first_got, back_mid_got, below, above, neighbors)

    state = pltpu.VMEM((LATE_PLANES, CAP, FACE), jnp.float32)
    rows_out = pltpu.VMEM((CAP, OUT_PLANES * FACE), jnp.float32)
    phase, solute = pl.pallas_call(
        late_kernel,
        in_specs=[SMEM] + [VMEM] * 7 + [HBM] * 2,
        out_specs=[HBM] * 2,
        out_shape=[whole, whole],
        scratch_shapes=[state] * 7 + [rows_out] * 2 + [pltpu.SemaphoreType.DMA((2,))],
        input_output_aliases={8: 0, 9: 1},
        compiler_params=PARAMS,
        cost_estimate=cost(8 * MB),
        name="late_steps",
    )(here, stay_late, far_late_got, back_late_got, neighbors, kept0, kept1, kept2, phase, solute)
    return phase, solute


def solution(mesh):
    placed = (P("blk", None), P("blk", None), P("blk", None), P("blk"), P("blk", None))
    return jax.shard_map(
        on_device,
        mesh=mesh,
        in_specs=placed,
        out_specs=(P("blk", None), P("blk", None)),
        check_vma=False,
    )
```

```python
import functools

import jax
import jax.numpy as jnp
from jax import lax
from jax.experimental import pallas as pl
from jax.experimental.pallas import tpu as pltpu
from jax.sharding import PartitionSpec as P

EDGE = 32
FACE = EDGE * EDGE
CELLS = EDGE * FACE
CAP = 8
OLD = 16
FIELDS = 3
HALO = 3
CHUNK_PLANES = 4
CHUNK = CHUNK_PLANES * FACE
CHUNKS = EDGE // CHUNK_PLANES
LANES = 128
EXT = EDGE + 2 * HALO
REST = EDGE - 2 * CHUNK_PLANES
AHEAD = 20
FIRST_STEPS = 2 + AHEAD // CHUNK_PLANES
VREGS = FACE // LANES

time_step = 0.15
coupling = 1.5


def windows(slot_ref, here):
    first = slot_ref[0]
    count = jnp.int32(0)
    for i in range(OLD):
        count += (slot_ref[i] >= 0).astype(jnp.int32)
    amount = jnp.bitwise_and(first, CAP - 1)
    row = lax.broadcasted_iota(jnp.int32, (CAP, LANES), 0)

    def masks(k):
        index = row + ((here + k) * CAP - first)
        low = (index >= 0) & (index < CAP) & (index < count)
        high = (index >= CAP) & (index < count)
        return low, high

    return amount, masks


def picked(masks, low_rows, high_rows):
    low, high = masks
    return jnp.where(low, low_rows, jnp.where(high, high_rows, 0.0))


def side_of(here):
    return jnp.where(jnp.bitwise_and(here, 1) == 0, -1, 1)


def aligned(ref, lanes, amount):
    return pltpu.roll(ref[0:CAP, lanes], amount, 0), pltpu.roll(ref[CAP:OLD, lanes], amount, 0)


def chunk_at(i):
    return jnp.where(i == 0, 0, jnp.where(i == 1, CHUNKS - 1, i - 1))


def lanes_at(start, v):
    return pl.ds(pl.multiple_of(start + v * LANES, LANES), LANES)


def pack_kernel(
    here_ref, slot_hbm, phi_hbm, conc_hbm, mob_hbm,
    phi_ref, conc_ref, mob_ref, merge_ref, final_ref, far_ref, late_ref,
    slot_ref, slot_sem, sems,
):
    olds = tuple(zip((phi_hbm, conc_hbm, mob_hbm), (phi_ref, conc_ref, mob_ref)))

    def copies(i):
        lanes = pl.ds(pl.multiple_of(chunk_at(i) * CHUNK, CHUNK), CHUNK)
        return [pltpu.make_async_copy(hbm.at[:, lanes], ref.at[:, lanes], sems.at[i, f]) for f, (hbm, ref) in enumerate(olds)]

    slot_copy = pltpu.make_async_copy(slot_hbm, slot_ref, slot_sem)
    slot_copy.start()

    @pl.loop(0, CHUNKS)
    def _(i):
        for copy in copies(i):
            copy.start()

    slot_copy.wait()
    here = here_ref[0]
    side = side_of(here)
    amount, masks = windows(slot_ref, here)
    far, merge, final = masks(2 * side), masks(side), masks(-side)

    def fill(i, out_ref, out_start):
        start = chunk_at(i) * CHUNK
        for f, (_, ref) in enumerate(olds):
            for v in range(CHUNK // LANES):
                lanes = lanes_at(start, v)
                rows = aligned(ref, lanes, amount)
                merge_ref[f, :, lanes] = picked(merge, *rows)
                final_ref[f, :, lanes] = picked(final, *rows)
                out_ref[f, :, lanes_at(out_start, v)] = picked(far, *rows)

    @pl.loop(0, FIRST_STEPS)
    def _(i):
        for copy in copies(i):
            copy.wait()
        fill(i, far_ref, i * CHUNK)

    @pl.loop(FIRST_STEPS, CHUNKS)
    def _(i):
        for copy in copies(i):
            copy.wait()
        fill(i, late_ref, (i - FIRST_STEPS) * CHUNK)


def add_rows(masks, amount, old_refs, add_ref, edge_ref, rest_ref):
    for out_ref, out_plane, plane, count in (
        (edge_ref, 0, 0, CHUNK_PLANES),
        (edge_ref, CHUNK_PLANES, CHUNK_PLANES + REST, CHUNK_PLANES),
        (rest_ref, 0, CHUNK_PLANES, REST),
    ):

        @pl.loop(0, count // 2)
        def _(i):
            for f, ref in enumerate(old_refs):
                for v in range(2 * VREGS):
                    lanes = lanes_at((plane + 2 * i) * FACE, v)
                    value = picked(masks, *aligned(ref, lanes, amount)) + add_ref[f, :, lanes]
                    out_ref[f, :, lanes_at((out_plane + 2 * i) * FACE, v)] = value


def relay_kernel(here_ref, slot_ref, phi_ref, conc_ref, mob_ref, merge_ref, *part_refs):
    here = here_ref[0]
    amount, masks = windows(slot_ref, here)
    add_rows(masks(-2 * side_of(here)), amount, (phi_ref, conc_ref, mob_ref), merge_ref, *part_refs)


def stay_kernel(here_ref, slot_ref, phi_ref, conc_ref, mob_ref, final_ref, *part_refs):
    here = here_ref[0]
    amount, masks = windows(slot_ref, here)
    add_rows(masks(0), amount, (phi_ref, conc_ref, mob_ref), final_ref, *part_refs)


def face_kernel(stay_ref, far_ref, back_ref, edge_ref, low_ref, high_ref):
    first_high = (2 * CHUNK_PLANES - HALO) * FACE
    for f in range(FIELDS):
        for v in range(2 * CHUNK_PLANES * VREGS):
            lanes = pl.ds(v * LANES, LANES)
            value = stay_ref[f, :, lanes] + far_ref[f, :, lanes] + back_ref[f, :, lanes]
            edge_ref[f, :, lanes] = value
            at = v * LANES
            if at < HALO * FACE:
                low_ref[f, :, lanes] = value
            if at >= first_high:
                high_ref[f, :, pl.ds(at - first_high, LANES)] = value


class Stencil:
    def __init__(self, here, nbr):
        base = here * CAP
        self.nbr = nbr
        lane = lax.broadcasted_iota(jnp.int32, (CAP, LANES), 1)
        z = jnp.bitwise_and(lane, EDGE - 1)
        self.z_first, self.z_last = z == 0, z == EDGE - 1
        self.y_first, self.y_last = lane < EDGE, lane >= LANES - EDGE
        self.below_x, self.has_below_x = self.column(0, base - CAP)
        self.above_x, self.has_above_x = self.column(1, base + CAP)
        self.below_y, self.has_below_y = self.column(2, base)
        self.above_y, self.has_above_y = self.column(3, base)
        self.below_z, _ = self.column(4, base)
        self.above_z, _ = self.column(5, base)

    def column(self, c, start):
        wide = jnp.broadcast_to(self.nbr[:, c : c + 1], (CAP, LANES))
        valid = wide >= 0
        return jnp.where(valid, wide - start, 0), valid

    @staticmethod
    def rows(x, index):
        return jnp.take_along_axis(x, index, axis=0, mode="promise_in_bounds")

    def laplacian(self, ref, x):
        centre = [ref[x, :, pl.ds(v * LANES, LANES)] for v in range(VREGS)]
        lower = [pltpu.roll(c, EDGE, 1) for c in centre]
        upper = [pltpu.roll(c, LANES - EDGE, 1) for c in centre]
        out = []
        for v in range(VREGS):
            c = centre[v]
            lanes = pl.ds(v * LANES, LANES)
            if v:
                from_lower = lower[v - 1]
            else:
                from_lower = jnp.where(self.has_below_y, self.rows(lower[-1], self.below_y), c)
            if v < VREGS - 1:
                from_upper = upper[v + 1]
            else:
                from_upper = jnp.where(self.has_above_y, self.rows(upper[0], self.above_y), c)
            prev_y = jnp.where(self.y_first, from_lower, lower[v])
            next_y = jnp.where(self.y_last, from_upper, upper[v])
            prev_z = jnp.where(self.z_first, pltpu.roll(self.rows(c, self.below_z), LANES - EDGE + 1, 1), pltpu.roll(c, 1, 1))
            next_z = jnp.where(self.z_last, pltpu.roll(self.rows(c, self.above_z), EDGE - 1, 1), pltpu.roll(c, LANES - 1, 1))
            total = (ref[x - 1, :, lanes] + ref[x + 1, :, lanes]) + (prev_y + next_y) + (prev_z + next_z)
            out.append(total - 6.0 * c)
        return out, centre

    def advance(self, phi_ref, conc_ref, mob_ref, x, store):
        lapl_phi, phis = self.laplacian(phi_ref, x)
        lapl_conc, concs = self.laplacian(conc_ref, x)
        for v in range(VREGS):
            phi, conc = phis[v], concs[v]
            square = phi * phi
            wetting = 1.0 - square
            drive = lapl_phi[v] + phi - square * phi - coupling * conc * wetting * wetting
            change = time_step * mob_ref[x, :, pl.ds(v * LANES, LANES)] * drive
            store(v, phi + change, conc + time_step * lapl_conc[v] + 0.5 * change)

    def sweep(self, first, last, unroll, source, mob_ref, target, shift=None):
        phi_ref, conc_ref = source
        phi_out, conc_out = target

        def one(x):
            def store(v, phi, conc):
                if shift is None:
                    where = (x, slice(None), pl.ds(v * LANES, LANES))
                else:
                    where = (slice(None), pl.ds(pl.multiple_of((x - shift) * FACE + v * LANES, LANES), LANES))
                phi_out[where] = phi
                conc_out[where] = conc

            self.advance(phi_ref, conc_ref, mob_ref, x, store)

        whole = first + (last - first) // unroll * unroll
        if whole > first:

            @pl.loop(0, (whole - first) // unroll)
            def _(i):
                for u in range(unroll):
                    one(first + i * unroll + u)

        for x in range(whole, last):
            one(x)


def place(states, planes, at, *parts):
    for f, ref in enumerate(states):

        @pl.loop(0, planes // 2)
        def _(i):
            for u in range(2):
                x = 2 * i + u
                for v in range(VREGS):
                    value = sum(part[f, :, lanes_at((x + first) * FACE, v)] for part, first in parts)
                    ref[x + at, :, pl.ds(v * LANES, LANES)] = value


REST_AT = HALO + CHUNK_PLANES
TOP_AT = REST_AT + REST


def edge_kernel(
    here_ref, edge_ref, below_ref, above_ref, nbr_ref,
    phase_ref, solute_ref, kept0_ref, kept1_ref, kept2_ref,
    phi0, conc0, mob, phi1, conc1, phi2, conc2,
):
    st = Stencil(here_ref[0], nbr_ref[...])
    states = (phi0, conc0, mob)
    for f, ref in enumerate(states):
        for d in range(2 * CHUNK_PLANES):
            at = HALO + d if d < CHUNK_PLANES else TOP_AT + d - CHUNK_PLANES
            for v in range(VREGS):
                ref[at, :, pl.ds(v * LANES, LANES)] = edge_ref[f, :, pl.ds(d * FACE + v * LANES, LANES)]
        for d in range(HALO):
            for v in range(VREGS):
                lanes = pl.ds(v * LANES, LANES)
                part = pl.ds(d * FACE + v * LANES, LANES)
                mirror_low = ref[2 * HALO - 1 - d, :, lanes]
                ref[d, :, lanes] = jnp.where(st.has_below_x, st.rows(below_ref[f, :, part], st.below_x), mirror_low)
                mirror_high = ref[EDGE + HALO - 1 - d, :, lanes]
                ref[EDGE + HALO + d, :, lanes] = jnp.where(st.has_above_x, st.rows(above_ref[f, :, part], st.above_x), mirror_high)
    for first, last in ((1, REST_AT - 1), (TOP_AT + 1, EXT - 1)):
        st.sweep(first, last, 5, (phi0, conc0), mob, (phi1, conc1))
        st.sweep(first + 1, last - 1, 3, (phi1, conc1), mob, (phi2, conc2))
        st.sweep(first + 2, last - 2, 1, (phi2, conc2), mob, (phase_ref, solute_ref), HALO)
    for f, ref in enumerate(states):
        for n, x in enumerate((*range(REST_AT - 3, REST_AT), *range(TOP_AT, TOP_AT + 3))):
            kept0_ref[f, n] = ref[x]
    for f, ref in enumerate((phi1, conc1)):
        for n, x in enumerate((REST_AT - 3, REST_AT - 2, TOP_AT + 1, TOP_AT + 2)):
            kept1_ref[f, n] = ref[x]
    for f, ref in enumerate((phi2, conc2)):
        for n, x in enumerate((REST_AT - 4, REST_AT - 3, TOP_AT + 2, TOP_AT + 3)):
            kept2_ref[f, n] = ref[x]


BACK = REST_AT - 4
MAIN_PLANES = TOP_AT + 4 - BACK
OUT_FIRST = REST_AT - 3
OUT_PLANES = TOP_AT + 3 - OUT_FIRST
PIECE = 6
PIECES = OUT_PLANES // PIECE


def main_kernel(
    here_ref, stay_ref, far_ref, far_late_ref, back_ref, nbr_ref, kept0_ref, kept1_ref, kept2_ref, _phase_in, _solute_in,
    phase_hbm, solute_hbm,
    phi0, conc0, mob, phi1, conc1, phi2, conc2, phase_ref, solute_ref, sems,
):
    st = Stencil(here_ref[0], nbr_ref[...])
    states = (phi0, conc0, mob)
    first, last = REST_AT - BACK, TOP_AT - BACK
    for f, ref in enumerate(states):
        for n, x in enumerate((*range(first - 3, first), *range(last, last + 3))):
            ref[x] = kept0_ref[f, n]
    for f, ref in enumerate((phi1, conc1)):
        for n, x in enumerate((first - 3, first - 2, last + 1, last + 2)):
            ref[x] = kept1_ref[f, n]
    for f, ref in enumerate((phi2, conc2)):
        for n, x in enumerate((first - 4, first - 3, last + 2, last + 3)):
            ref[x] = kept2_ref[f, n]
    place(states, AHEAD, first, (stay_ref, 0), (far_ref, 2 * CHUNK_PLANES), (back_ref, 0))
    place(states, REST - AHEAD, first + AHEAD, (stay_ref, AHEAD), (far_late_ref, 0), (back_ref, AHEAD))
    st.sweep(first - 1, last + 1, 5, (phi0, conc0), mob, (phi1, conc1))
    st.sweep(first - 2, last + 2, 4, (phi1, conc1), mob, (phi2, conc2))
    start = first - 3
    copies = []
    for piece in range(PIECES):
        at = start + piece * PIECE
        st.sweep(at, at + PIECE, PIECE, (phi2, conc2), mob, (phase_ref, solute_ref), start)
        source = pl.ds(piece * PIECE * FACE, PIECE * FACE)
        target = pl.ds((OUT_FIRST - HALO + piece * PIECE) * FACE, PIECE * FACE)
        for n, (ref, hbm) in enumerate(((phase_ref, phase_hbm), (solute_ref, solute_hbm))):
            copies.append(pltpu.make_async_copy(ref.at[:, source], hbm.at[:, target], sems.at[piece, n]))
            copies[-1].start()
    for copy in copies:
        copy.wait()


SMEM = pl.BlockSpec(memory_space=pltpu.SMEM)
VMEM = pl.BlockSpec(memory_space=pltpu.VMEM)
HBM = pl.BlockSpec(memory_space=pltpu.HBM)
ANY = pl.BlockSpec(memory_space=pl.ANY)
PARAMS = pltpu.CompilerParams(vmem_limit_bytes=32 * 2**20)


def shaped(planes, fields=FIELDS):
    return jax.ShapeDtypeStruct((fields, CAP, planes * FACE), jnp.float32)


def cost(moved, flops=10**6):
    return pl.CostEstimate(flops=flops, bytes_accessed=moved, transcendentals=0)


MB = 2**20


def on_device(old_phase, old_solute, old_mobility, new_global_slot, neighbors):
    count = lax.axis_size("blk")
    here = lax.axis_index("blk").astype(jnp.int32).reshape(1)
    olds = tuple(pltpu.with_memory_space_constraint(x, pltpu.HBM) for x in (old_phase, old_solute, old_mobility))
    devices = range(count)

    def sent(block, route):
        return lax.ppermute(block, "blk", [(p, q) for p, q in route if 0 <= q < count])

    def outward(p):
        return -2 if p % 2 == 0 else 2

    partner = [(p, p ^ 1) for p in devices]
    far_route = [(p, p + outward(p)) for p in devices]
    back_route = [(p, p - outward(p)) for p in devices]

    def after(block, *others):
        return lax.optimization_barrier((block, *others))[0]

    slots_hbm = pltpu.with_memory_space_constraint(new_global_slot, pltpu.HBM)
    old_shape = jax.ShapeDtypeStruct((OLD, CELLS), jnp.float32)
    *olds, merge, final, far_first, far_late = pl.pallas_call(
        pack_kernel,
        in_specs=[SMEM, HBM, HBM, HBM, HBM],
        out_specs=[VMEM] * 7,
        out_shape=[old_shape] * 3 + [shaped(EDGE)] * 2 + [shaped(2 * CHUNK_PLANES + AHEAD), shaped(REST - AHEAD)],
        scratch_shapes=[pltpu.SMEM((OLD,), jnp.int32), pltpu.SemaphoreType.DMA, pltpu.SemaphoreType.DMA((CHUNKS, FIELDS))],
        compiler_params=PARAMS,
        cost_estimate=cost(6 * MB),
        name="pack",
    )(here, slots_hbm, *olds)
    far_first_got = sent(far_first, far_route)
    merge_got = sent(merge, partner)
    final_got = sent(final, partner)

    two_parts = [shaped(2 * CHUNK_PLANES), shaped(REST)]
    back_edge, back_rest = pl.pallas_call(
        relay_kernel,
        in_specs=[SMEM, SMEM] + [VMEM] * 4,
        out_specs=[VMEM] * 2,
        out_shape=two_parts,
        compiler_params=PARAMS,
        cost_estimate=cost(6 * MB),
        name="relay",
    )(here, new_global_slot, *olds, merge_got)
    back_edge_got = sent(back_edge, back_route)

    stay_edge, stay_rest = pl.pallas_call(
        stay_kernel,
        in_specs=[SMEM, SMEM] + [VMEM] * 4,
        out_specs=[VMEM] * 2,
        out_shape=two_parts,
        compiler_params=PARAMS,
        cost_estimate=cost(6 * MB),
        name="stay",
    )(here, new_global_slot, *olds, final_got)
    back_rest_got = sent(after(back_rest, back_edge_got, stay_edge), back_route)
    far_late_got = sent(after(far_late, far_first_got), far_route)

    edges = pl.BlockSpec((FIELDS, CAP, 2 * CHUNK), lambda i: (0, 0, 0))
    faces = pl.BlockSpec((FIELDS, CAP, HALO * FACE), lambda i: (0, 0, 0))
    edge, low, high = pl.pallas_call(
        face_kernel,
        grid=(1,),
        in_specs=[edges] * 3,
        out_specs=[edges, faces, faces],
        out_shape=[shaped(2 * CHUNK_PLANES), shaped(HALO), shaped(HALO)],
        compiler_params=PARAMS,
        cost_estimate=cost(3 * MB),
        name="faces",
    )(stay_edge, far_first_got, back_edge_got)
    below = sent(high, [(p, p + 1) for p in devices])
    above = sent(low, [(p, p - 1) for p in devices])

    state = pltpu.VMEM((EXT, CAP, FACE), jnp.float32)
    whole = jax.ShapeDtypeStruct((CAP, CELLS), jnp.float32)

    def kept(fields, planes):
        return jax.ShapeDtypeStruct((fields, planes, CAP, FACE), jnp.float32)

    phase, solute, kept0, kept1, kept2 = pl.pallas_call(
        edge_kernel,
        in_specs=[SMEM] + [VMEM] * 4,
        out_specs=[VMEM] * 5,
        out_shape=[whole, whole, kept(3, 6), kept(2, 4), kept(2, 4)],
        scratch_shapes=[state] * 7,
        compiler_params=PARAMS,
        cost_estimate=cost(8 * MB),
        name="edge_steps",
    )(here, edge, below, above, neighbors)

    state = pltpu.VMEM((MAIN_PLANES, CAP, FACE), jnp.float32)
    rows_out = pltpu.VMEM((CAP, OUT_PLANES * FACE), jnp.float32)
    phase, solute = pl.pallas_call(
        main_kernel,
        in_specs=[SMEM] + [VMEM] * 8 + [HBM] * 2,
        out_specs=[HBM] * 2,
        out_shape=[whole, whole],
        scratch_shapes=[state] * 7 + [rows_out] * 2 + [pltpu.SemaphoreType.DMA((PIECES, 2))],
        input_output_aliases={9: 0, 10: 1},
        compiler_params=PARAMS,
        cost_estimate=cost(20 * MB),
        name="main_steps",
    )(here, stay_rest, far_first_got, far_late_got, back_rest_got, neighbors, kept0, kept1, kept2, phase, solute)
    return phase, solute


def solution(mesh):
    placed = (P("blk", None), P("blk", None), P("blk", None), P("blk"), P("blk", None))
    return jax.shard_map(
        on_device,
        mesh=mesh,
        in_specs=placed,
        out_specs=(P("blk", None), P("blk", None)),
        check_vma=False,
    )
```

```python
import functools

import jax
import jax.numpy as jnp
from jax import lax
from jax.experimental import pallas as pl
from jax.experimental.pallas import tpu as pltpu
from jax.sharding import PartitionSpec as P

EDGE = 32
FACE = EDGE * EDGE
CELLS = EDGE * FACE
CAP = 8
OLD = 16
FIELDS = 3
HALO = 3
CHUNK_PLANES = 4
CHUNK = CHUNK_PLANES * FACE
CHUNKS = EDGE // CHUNK_PLANES
LANES = 128
EXT = EDGE + 2 * HALO
REST = EDGE - 2 * CHUNK_PLANES
VREGS = FACE // LANES

time_step = 0.15
coupling = 1.5


def windows(slot_ref, here):
    first = slot_ref[0]
    count = jnp.int32(0)
    for i in range(OLD):
        count += (slot_ref[i] >= 0).astype(jnp.int32)
    amount = jnp.bitwise_and(first, CAP - 1)
    row = lax.broadcasted_iota(jnp.int32, (CAP, LANES), 0)

    def masks(k):
        index = row + ((here + k) * CAP - first)
        low = (index >= 0) & (index < CAP) & (index < count)
        high = (index >= CAP) & (index < count)
        return low, high

    return amount, masks


def picked(masks, low_rows, high_rows):
    low, high = masks
    return jnp.where(low, low_rows, jnp.where(high, high_rows, 0.0))


def side_of(here):
    return jnp.where(jnp.bitwise_and(here, 1) == 0, -1, 1)


def aligned(ref, lanes, amount):
    return pltpu.roll(ref[0:CAP, lanes], amount, 0), pltpu.roll(ref[CAP:OLD, lanes], amount, 0)


def chunk_at(i):
    return jnp.where(i == 0, 0, jnp.where(i == 1, CHUNKS - 1, i - 1))


def lanes_at(start, v):
    return pl.ds(pl.multiple_of(start + v * LANES, LANES), LANES)


def pack_kernel(
    here_ref, slot_hbm, phi_hbm, conc_hbm, mob_hbm,
    phi_ref, conc_ref, mob_ref, merge_ref, final_ref, far_ref,
    slot_ref, slot_sem, sems,
):
    olds = tuple(zip((phi_hbm, conc_hbm, mob_hbm), (phi_ref, conc_ref, mob_ref)))

    def copies(i):
        lanes = pl.ds(pl.multiple_of(chunk_at(i) * CHUNK, CHUNK), CHUNK)
        return [pltpu.make_async_copy(hbm.at[:, lanes], ref.at[:, lanes], sems.at[i, f]) for f, (hbm, ref) in enumerate(olds)]

    slot_copy = pltpu.make_async_copy(slot_hbm, slot_ref, slot_sem)
    slot_copy.start()

    @pl.loop(0, CHUNKS)
    def _(i):
        for copy in copies(i):
            copy.start()

    slot_copy.wait()
    here = here_ref[0]
    side = side_of(here)
    amount, masks = windows(slot_ref, here)
    far, merge, final = masks(2 * side), masks(side), masks(-side)

    def fill(i):
        start = chunk_at(i) * CHUNK
        for f, (_, ref) in enumerate(olds):
            for v in range(CHUNK // LANES):
                lanes = lanes_at(start, v)
                rows = aligned(ref, lanes, amount)
                merge_ref[f, :, lanes] = picked(merge, *rows)
                final_ref[f, :, lanes] = picked(final, *rows)
                far_ref[f, :, lanes_at(i * CHUNK, v)] = picked(far, *rows)

    @pl.loop(0, CHUNKS)
    def _(i):
        for copy in copies(i):
            copy.wait()
        fill(i)


def add_rows(masks, amount, old_refs, add_ref, edge_ref, rest_ref):
    for out_ref, out_plane, plane, count in (
        (edge_ref, 0, 0, CHUNK_PLANES),
        (edge_ref, CHUNK_PLANES, CHUNK_PLANES + REST, CHUNK_PLANES),
        (rest_ref, 0, CHUNK_PLANES, REST),
    ):

        @pl.loop(0, count // 2)
        def _(i):
            for f, ref in enumerate(old_refs):
                for v in range(2 * VREGS):
                    lanes = lanes_at((plane + 2 * i) * FACE, v)
                    value = picked(masks, *aligned(ref, lanes, amount)) + add_ref[f, :, lanes]
                    out_ref[f, :, lanes_at((out_plane + 2 * i) * FACE, v)] = value


def relay_kernel(here_ref, slot_ref, phi_ref, conc_ref, mob_ref, merge_ref, *part_refs):
    here = here_ref[0]
    amount, masks = windows(slot_ref, here)
    add_rows(masks(-2 * side_of(here)), amount, (phi_ref, conc_ref, mob_ref), merge_ref, *part_refs)


def stay_kernel(here_ref, slot_ref, phi_ref, conc_ref, mob_ref, final_ref, *part_refs):
    here = here_ref[0]
    amount, masks = windows(slot_ref, here)
    add_rows(masks(0), amount, (phi_ref, conc_ref, mob_ref), final_ref, *part_refs)


def face_kernel(stay_ref, far_ref, back_ref, edge_ref, low_ref, high_ref):
    first_high = (2 * CHUNK_PLANES - HALO) * FACE
    for f in range(FIELDS):
        for v in range(2 * CHUNK_PLANES * VREGS):
            lanes = pl.ds(v * LANES, LANES)
            value = stay_ref[f, :, lanes] + far_ref[f, :, lanes] + back_ref[f, :, lanes]
            edge_ref[f, :, lanes] = value
            at = v * LANES
            if at < HALO * FACE:
                low_ref[f, :, lanes] = value
            if at >= first_high:
                high_ref[f, :, pl.ds(at - first_high, LANES)] = value


class Stencil:
    def __init__(self, here, nbr):
        base = here * CAP
        self.nbr = nbr
        lane = lax.broadcasted_iota(jnp.int32, (CAP, LANES), 1)
        z = jnp.bitwise_and(lane, EDGE - 1)
        self.z_first, self.z_last = z == 0, z == EDGE - 1
        self.y_first, self.y_last = lane < EDGE, lane >= LANES - EDGE
        self.below_x, self.has_below_x = self.column(0, base - CAP)
        self.above_x, self.has_above_x = self.column(1, base + CAP)
        self.below_y, self.has_below_y = self.column(2, base)
        self.above_y, self.has_above_y = self.column(3, base)
        self.below_z, _ = self.column(4, base)
        self.above_z, _ = self.column(5, base)

    def column(self, c, start):
        wide = jnp.broadcast_to(self.nbr[:, c : c + 1], (CAP, LANES))
        valid = wide >= 0
        return jnp.where(valid, wide - start, 0), valid

    @staticmethod
    def rows(x, index):
        return jnp.take_along_axis(x, index, axis=0, mode="promise_in_bounds")

    def across_y(self, centre):
        lower = [pltpu.roll(c, EDGE, 1) for c in centre]
        upper = [pltpu.roll(c, LANES - EDGE, 1) for c in centre]
        out = []
        for v, c in enumerate(centre):
            if v:
                from_lower = lower[v - 1]
            else:
                from_lower = jnp.where(self.has_below_y, self.rows(lower[-1], self.below_y), c)
            if v < VREGS - 1:
                from_upper = upper[v + 1]
            else:
                from_upper = jnp.where(self.has_above_y, self.rows(upper[0], self.above_y), c)
            out.append(jnp.where(self.y_first, from_lower, lower[v]) + jnp.where(self.y_last, from_upper, upper[v]))
        return out

    def across_z(self, phi, conc):
        phi_prev, conc_prev = pltpu.roll(phi, 1, 1), pltpu.roll(conc, 1, 1)
        phi_next, conc_next = pltpu.roll(phi, LANES - 1, 1), pltpu.roll(conc, LANES - 1, 1)
        below = self.rows(jnp.where(self.z_first, conc_prev, phi), self.below_z)
        above = self.rows(jnp.where(self.z_last, conc_next, phi), self.above_z)
        phi_prev = jnp.where(self.z_first, pltpu.roll(below, LANES - EDGE + 1, 1), phi_prev)
        conc_prev = jnp.where(self.z_first, pltpu.roll(below, LANES - EDGE, 1), conc_prev)
        phi_next = jnp.where(self.z_last, pltpu.roll(above, EDGE - 1, 1), phi_next)
        conc_next = jnp.where(self.z_last, pltpu.roll(above, EDGE, 1), conc_next)
        return phi_prev + phi_next, conc_prev + conc_next

    def advance(self, phi_ref, conc_ref, mob_ref, x, store):
        lanes = [pl.ds(v * LANES, LANES) for v in range(VREGS)]
        phis, concs = ([ref[x, :, part] for part in lanes] for ref in (phi_ref, conc_ref))
        phi_y, conc_y = self.across_y(phis), self.across_y(concs)
        lapl_phi, lapl_conc = [], []
        for v in range(VREGS):
            phi_z, conc_z = self.across_z(phis[v], concs[v])
            for out, ref, c, in_y, in_z in (
                (lapl_phi, phi_ref, phis[v], phi_y[v], phi_z),
                (lapl_conc, conc_ref, concs[v], conc_y[v], conc_z),
            ):
                total = (ref[x - 1, :, lanes[v]] + ref[x + 1, :, lanes[v]]) + in_y + in_z
                out.append(total - 6.0 * c)
        for v in range(VREGS):
            phi, conc = phis[v], concs[v]
            square = phi * phi
            wetting = 1.0 - square
            drive = lapl_phi[v] + phi - square * phi - coupling * conc * wetting * wetting
            change = time_step * mob_ref[x, :, pl.ds(v * LANES, LANES)] * drive
            store(v, phi + change, conc + time_step * lapl_conc[v] + 0.5 * change)

    def sweep(self, first, last, unroll, source, mob_ref, target, shift=None):
        phi_ref, conc_ref = source
        phi_out, conc_out = target

        def one(x):
            def store(v, phi, conc):
                if shift is None:
                    where = (x, slice(None), pl.ds(v * LANES, LANES))
                else:
                    where = (slice(None), pl.ds(pl.multiple_of((x - shift) * FACE + v * LANES, LANES), LANES))
                phi_out[where] = phi
                conc_out[where] = conc

            self.advance(phi_ref, conc_ref, mob_ref, x, store)

        whole = first + (last - first) // unroll * unroll
        if whole > first:

            @pl.loop(0, (whole - first) // unroll)
            def _(i):
                for u in range(unroll):
                    one(first + i * unroll + u)

        for x in range(whole, last):
            one(x)


def place(states, planes, at, *parts):
    for f, ref in enumerate(states):

        @pl.loop(0, planes // 2)
        def _(i):
            for u in range(2):
                x = 2 * i + u
                for v in range(VREGS):
                    value = sum(part[f, :, lanes_at((x + first) * FACE, v)] for part, first in parts)
                    ref[x + at, :, pl.ds(v * LANES, LANES)] = value


REST_AT = HALO + CHUNK_PLANES
TOP_AT = REST_AT + REST


def edge_kernel(
    here_ref, edge_ref, below_ref, above_ref, nbr_ref,
    phase_ref, solute_ref, kept0_ref, kept1_ref, kept2_ref,
    phi0, conc0, mob, phi1, conc1, phi2, conc2,
):
    st = Stencil(here_ref[0], nbr_ref[...])
    states = (phi0, conc0, mob)
    for f, ref in enumerate(states):
        for d in range(2 * CHUNK_PLANES):
            at = HALO + d if d < CHUNK_PLANES else TOP_AT + d - CHUNK_PLANES
            for v in range(VREGS):
                ref[at, :, pl.ds(v * LANES, LANES)] = edge_ref[f, :, pl.ds(d * FACE + v * LANES, LANES)]
        for d in range(HALO):
            for v in range(VREGS):
                lanes = pl.ds(v * LANES, LANES)
                part = pl.ds(d * FACE + v * LANES, LANES)
                mirror_low = ref[2 * HALO - 1 - d, :, lanes]
                ref[d, :, lanes] = jnp.where(st.has_below_x, st.rows(below_ref[f, :, part], st.below_x), mirror_low)
                mirror_high = ref[EDGE + HALO - 1 - d, :, lanes]
                ref[EDGE + HALO + d, :, lanes] = jnp.where(st.has_above_x, st.rows(above_ref[f, :, part], st.above_x), mirror_high)
    for first, last in ((1, REST_AT - 1), (TOP_AT + 1, EXT - 1)):
        st.sweep(first, last, 5, (phi0, conc0), mob, (phi1, conc1))
        st.sweep(first + 1, last - 1, 3, (phi1, conc1), mob, (phi2, conc2))
        st.sweep(first + 2, last - 2, 1, (phi2, conc2), mob, (phase_ref, solute_ref), HALO)
    for f, ref in enumerate(states):
        for n, x in enumerate((*range(REST_AT - 3, REST_AT), *range(TOP_AT, TOP_AT + 3))):
            kept0_ref[f, n] = ref[x]
    for f, ref in enumerate((phi1, conc1)):
        for n, x in enumerate((REST_AT - 3, REST_AT - 2, TOP_AT + 1, TOP_AT + 2)):
            kept1_ref[f, n] = ref[x]
    for f, ref in enumerate((phi2, conc2)):
        for n, x in enumerate((REST_AT - 4, REST_AT - 3, TOP_AT + 2, TOP_AT + 3)):
            kept2_ref[f, n] = ref[x]


BACK = REST_AT - 4
MAIN_PLANES = TOP_AT + 4 - BACK
OUT_FIRST = REST_AT - 3
OUT_PLANES = TOP_AT + 3 - OUT_FIRST
PIECE = 6
PIECES = OUT_PLANES // PIECE


def main_kernel(
    here_ref, stay_ref, far_ref, back_ref, nbr_ref, kept0_ref, kept1_ref, kept2_ref, _phase_in, _solute_in,
    phase_hbm, solute_hbm,
    phi0, conc0, mob, phi1, conc1, phi2, conc2, phase_ref, solute_ref, sems,
):
    st = Stencil(here_ref[0], nbr_ref[...])
    states = (phi0, conc0, mob)
    first, last = REST_AT - BACK, TOP_AT - BACK
    for f, ref in enumerate(states):
        for n, x in enumerate((*range(first - 3, first), *range(last, last + 3))):
            ref[x] = kept0_ref[f, n]
    for f, ref in enumerate((phi1, conc1)):
        for n, x in enumerate((first - 3, first - 2, last + 1, last + 2)):
            ref[x] = kept1_ref[f, n]
    for f, ref in enumerate((phi2, conc2)):
        for n, x in enumerate((first - 4, first - 3, last + 2, last + 3)):
            ref[x] = kept2_ref[f, n]
    place(states, REST, first, (stay_ref, 0), (far_ref, 2 * CHUNK_PLANES), (back_ref, 0))
    st.sweep(first - 1, last + 1, 5, (phi0, conc0), mob, (phi1, conc1))
    st.sweep(first - 2, last + 2, 4, (phi1, conc1), mob, (phi2, conc2))
    start = first - 3
    copies = []
    for piece in range(PIECES):
        at = start + piece * PIECE
        st.sweep(at, at + PIECE, PIECE, (phi2, conc2), mob, (phase_ref, solute_ref), start)
        source = pl.ds(piece * PIECE * FACE, PIECE * FACE)
        target = pl.ds((OUT_FIRST - HALO + piece * PIECE) * FACE, PIECE * FACE)
        for n, (ref, hbm) in enumerate(((phase_ref, phase_hbm), (solute_ref, solute_hbm))):
            copies.append(pltpu.make_async_copy(ref.at[:, source], hbm.at[:, target], sems.at[piece, n]))
            copies[-1].start()
    for copy in copies:
        copy.wait()


SMEM = pl.BlockSpec(memory_space=pltpu.SMEM)
VMEM = pl.BlockSpec(memory_space=pltpu.VMEM)
HBM = pl.BlockSpec(memory_space=pltpu.HBM)
ANY = pl.BlockSpec(memory_space=pl.ANY)
PARAMS = pltpu.CompilerParams(vmem_limit_bytes=32 * 2**20)


def shaped(planes, fields=FIELDS):
    return jax.ShapeDtypeStruct((fields, CAP, planes * FACE), jnp.float32)


def cost(moved, flops=10**6):
    return pl.CostEstimate(flops=flops, bytes_accessed=moved, transcendentals=0)


MB = 2**20


def on_device(old_phase, old_solute, old_mobility, new_global_slot, neighbors):
    count = lax.axis_size("blk")
    here = lax.axis_index("blk").astype(jnp.int32).reshape(1)
    olds = tuple(pltpu.with_memory_space_constraint(x, pltpu.HBM) for x in (old_phase, old_solute, old_mobility))
    devices = range(count)

    def sent(block, route):
        return lax.ppermute(block, "blk", [(p, q) for p, q in route if 0 <= q < count])

    def outward(p):
        return -2 if p % 2 == 0 else 2

    partner = [(p, p ^ 1) for p in devices]
    far_route = [(p, p + outward(p)) for p in devices]
    back_route = [(p, p - outward(p)) for p in devices]

    def after(block, *others):
        return lax.optimization_barrier((block, *others))[0]

    slots_hbm = pltpu.with_memory_space_constraint(new_global_slot, pltpu.HBM)
    old_shape = jax.ShapeDtypeStruct((OLD, CELLS), jnp.float32)
    *olds, merge, final, far_all = pl.pallas_call(
        pack_kernel,
        in_specs=[SMEM, HBM, HBM, HBM, HBM],
        out_specs=[VMEM] * 6,
        out_shape=[old_shape] * 3 + [shaped(EDGE)] * 3,
        scratch_shapes=[pltpu.SMEM((OLD,), jnp.int32), pltpu.SemaphoreType.DMA, pltpu.SemaphoreType.DMA((CHUNKS, FIELDS))],
        compiler_params=PARAMS,
        cost_estimate=cost(6 * MB),
        name="pack",
    )(here, slots_hbm, *olds)
    far_got = sent(far_all, far_route)
    merge_got = sent(merge, partner)
    final_got = sent(final, partner)

    two_parts = [shaped(2 * CHUNK_PLANES), shaped(REST)]
    back_edge, back_rest = pl.pallas_call(
        relay_kernel,
        in_specs=[SMEM, SMEM] + [VMEM] * 4,
        out_specs=[VMEM] * 2,
        out_shape=two_parts,
        compiler_params=PARAMS,
        cost_estimate=cost(6 * MB),
        name="relay",
    )(here, new_global_slot, *olds, merge_got)
    back_edge_got = sent(back_edge, back_route)

    stay_edge, stay_rest = pl.pallas_call(
        stay_kernel,
        in_specs=[SMEM, SMEM] + [VMEM] * 4,
        out_specs=[VMEM] * 2,
        out_shape=two_parts,
        compiler_params=PARAMS,
        cost_estimate=cost(6 * MB),
        name="stay",
    )(here, new_global_slot, *olds, final_got)
    back_rest_got = sent(after(back_rest, back_edge_got, stay_edge), back_route)

    edges = pl.BlockSpec((FIELDS, CAP, 2 * CHUNK), lambda i: (0, 0, 0))
    faces = pl.BlockSpec((FIELDS, CAP, HALO * FACE), lambda i: (0, 0, 0))
    edge, low, high = pl.pallas_call(
        face_kernel,
        grid=(1,),
        in_specs=[edges] * 3,
        out_specs=[edges, faces, faces],
        out_shape=[shaped(2 * CHUNK_PLANES), shaped(HALO), shaped(HALO)],
        compiler_params=PARAMS,
        cost_estimate=cost(3 * MB),
        name="faces",
    )(stay_edge, far_got, back_edge_got)
    below = sent(high, [(p, p + 1) for p in devices])
    above = sent(low, [(p, p - 1) for p in devices])

    state = pltpu.VMEM((EXT, CAP, FACE), jnp.float32)
    whole = jax.ShapeDtypeStruct((CAP, CELLS), jnp.float32)

    def kept(fields, planes):
        return jax.ShapeDtypeStruct((fields, planes, CAP, FACE), jnp.float32)

    phase, solute, kept0, kept1, kept2 = pl.pallas_call(
        edge_kernel,
        in_specs=[SMEM] + [VMEM] * 4,
        out_specs=[VMEM] * 5,
        out_shape=[whole, whole, kept(3, 6), kept(2, 4), kept(2, 4)],
        scratch_shapes=[state] * 7,
        compiler_params=PARAMS,
        cost_estimate=cost(8 * MB),
        name="edge_steps",
    )(here, edge, below, above, neighbors)

    state = pltpu.VMEM((MAIN_PLANES, CAP, FACE), jnp.float32)
    rows_out = pltpu.VMEM((CAP, OUT_PLANES * FACE), jnp.float32)
    phase, solute = pl.pallas_call(
        main_kernel,
        in_specs=[SMEM] + [VMEM] * 7 + [HBM] * 2,
        out_specs=[HBM] * 2,
        out_shape=[whole, whole],
        scratch_shapes=[state] * 7 + [rows_out] * 2 + [pltpu.SemaphoreType.DMA((PIECES, 2))],
        input_output_aliases={8: 0, 9: 1},
        compiler_params=PARAMS,
        cost_estimate=cost(20 * MB),
        name="main_steps",
    )(here, stay_rest, far_got, back_rest_got, neighbors, kept0, kept1, kept2, phase, solute)
    return phase, solute


def solution(mesh):
    placed = (P("blk", None), P("blk", None), P("blk", None), P("blk"), P("blk", None))
    return jax.shard_map(
        on_device,
        mesh=mesh,
        in_specs=placed,
        out_specs=(P("blk", None), P("blk", None)),
        check_vma=False,
    )
```

```python
import functools

import jax
import jax.numpy as jnp
from jax import lax
from jax.experimental import pallas as pl
from jax.experimental.pallas import tpu as pltpu
from jax.sharding import PartitionSpec as P

EDGE = 32
FACE = EDGE * EDGE
CELLS = EDGE * FACE
CAP = 8
OLD = 16
FIELDS = 3
HALO = 3
CHUNK_PLANES = 4
CHUNK = CHUNK_PLANES * FACE
CHUNKS = EDGE // CHUNK_PLANES
LANES = 128
EXT = EDGE + 2 * HALO
REST = EDGE - 2 * CHUNK_PLANES
AHEAD = 20
FIRST_STEPS = 2 + AHEAD // CHUNK_PLANES
VREGS = FACE // LANES

time_step = 0.15
coupling = 1.5


def windows(slot_ref, here):
    first = slot_ref[0]
    count = jnp.int32(0)
    for i in range(OLD):
        count += (slot_ref[i] >= 0).astype(jnp.int32)
    amount = jnp.bitwise_and(first, CAP - 1)
    row = lax.broadcasted_iota(jnp.int32, (CAP, LANES), 0)

    def masks(k):
        index = row + ((here + k) * CAP - first)
        low = (index >= 0) & (index < CAP) & (index < count)
        high = (index >= CAP) & (index < count)
        return low, high

    return amount, masks


def picked(masks, low_rows, high_rows):
    low, high = masks
    return jnp.where(low, low_rows, jnp.where(high, high_rows, 0.0))


def side_of(here):
    return jnp.where(jnp.bitwise_and(here, 1) == 0, -1, 1)


def aligned(ref, lanes, amount):
    return pltpu.roll(ref[0:CAP, lanes], amount, 0), pltpu.roll(ref[CAP:OLD, lanes], amount, 0)


def chunk_at(i):
    return jnp.where(i == 0, 0, jnp.where(i == 1, CHUNKS - 1, i - 1))


def lanes_at(start, v):
    return pl.ds(pl.multiple_of(start + v * LANES, LANES), LANES)


def pack_kernel(
    here_ref, slot_hbm, phi_hbm, conc_hbm, mob_hbm,
    phi_ref, conc_ref, mob_ref, merge_ref, final_ref, far_ref, late_ref,
    slot_ref, slot_sem, sems,
):
    olds = tuple(zip((phi_hbm, conc_hbm, mob_hbm), (phi_ref, conc_ref, mob_ref)))

    def copies(i):
        lanes = pl.ds(pl.multiple_of(chunk_at(i) * CHUNK, CHUNK), CHUNK)
        return [pltpu.make_async_copy(hbm.at[:, lanes], ref.at[:, lanes], sems.at[i, f]) for f, (hbm, ref) in enumerate(olds)]

    slot_copy = pltpu.make_async_copy(slot_hbm, slot_ref, slot_sem)
    slot_copy.start()

    @pl.loop(0, CHUNKS)
    def _(i):
        for copy in copies(i):
            copy.start()

    slot_copy.wait()
    here = here_ref[0]
    side = side_of(here)
    amount, masks = windows(slot_ref, here)
    far, merge, final = masks(2 * side), masks(side), masks(-side)

    def fill(i, out_ref, out_start):
        start = chunk_at(i) * CHUNK
        for f, (_, ref) in enumerate(olds):
            for v in range(CHUNK // LANES):
                lanes = lanes_at(start, v)
                rows = aligned(ref, lanes, amount)
                merge_ref[f, :, lanes] = picked(merge, *rows)
                final_ref[f, :, lanes] = picked(final, *rows)
                out_ref[f, :, lanes_at(out_start, v)] = picked(far, *rows)

    @pl.loop(0, FIRST_STEPS)
    def _(i):
        for copy in copies(i):
            copy.wait()
        fill(i, far_ref, i * CHUNK)

    @pl.loop(FIRST_STEPS, CHUNKS)
    def _(i):
        for copy in copies(i):
            copy.wait()
        fill(i, late_ref, (i - FIRST_STEPS) * CHUNK)


def add_rows(masks, amount, old_refs, add_ref, edge_ref, rest_ref):
    for out_ref, out_plane, plane, count in (
        (edge_ref, 0, 0, CHUNK_PLANES),
        (edge_ref, CHUNK_PLANES, CHUNK_PLANES + REST, CHUNK_PLANES),
        (rest_ref, 0, CHUNK_PLANES, REST),
    ):

        @pl.loop(0, count // 2)
        def _(i):
            for f, ref in enumerate(old_refs):
                for v in range(2 * VREGS):
                    lanes = lanes_at((plane + 2 * i) * FACE, v)
                    value = picked(masks, *aligned(ref, lanes, amount)) + add_ref[f, :, lanes]
                    out_ref[f, :, lanes_at((out_plane + 2 * i) * FACE, v)] = value


def relay_kernel(here_ref, slot_ref, phi_ref, conc_ref, mob_ref, merge_ref, *part_refs):
    here = here_ref[0]
    amount, masks = windows(slot_ref, here)
    add_rows(masks(-2 * side_of(here)), amount, (phi_ref, conc_ref, mob_ref), merge_ref, *part_refs)


def stay_kernel(here_ref, slot_ref, phi_ref, conc_ref, mob_ref, final_ref, *part_refs):
    here = here_ref[0]
    amount, masks = windows(slot_ref, here)
    add_rows(masks(0), amount, (phi_ref, conc_ref, mob_ref), final_ref, *part_refs)


def face_kernel(stay_ref, far_ref, back_ref, edge_ref, low_ref, high_ref):
    first_high = (2 * CHUNK_PLANES - HALO) * FACE
    for f in range(FIELDS):
        for v in range(2 * CHUNK_PLANES * VREGS):
            lanes = pl.ds(v * LANES, LANES)
            value = stay_ref[f, :, lanes] + far_ref[f, :, lanes] + back_ref[f, :, lanes]
            edge_ref[f, :, lanes] = value
            at = v * LANES
            if at < HALO * FACE:
                low_ref[f, :, lanes] = value
            if at >= first_high:
                high_ref[f, :, pl.ds(at - first_high, LANES)] = value


class Stencil:
    def __init__(self, here, nbr):
        base = here * CAP
        self.nbr = nbr
        lane = lax.broadcasted_iota(jnp.int32, (CAP, LANES), 1)
        z = jnp.bitwise_and(lane, EDGE - 1)
        self.z_first, self.z_last = z == 0, z == EDGE - 1
        self.y_first, self.y_last = lane < EDGE, lane >= LANES - EDGE
        self.below_x, self.has_below_x = self.column(0, base - CAP)
        self.above_x, self.has_above_x = self.column(1, base + CAP)
        self.below_y, self.has_below_y = self.column(2, base)
        self.above_y, self.has_above_y = self.column(3, base)
        self.below_z, _ = self.column(4, base)
        self.above_z, _ = self.column(5, base)

    def column(self, c, start):
        wide = jnp.broadcast_to(self.nbr[:, c : c + 1], (CAP, LANES))
        valid = wide >= 0
        return jnp.where(valid, wide - start, 0), valid

    @staticmethod
    def rows(x, index):
        return jnp.take_along_axis(x, index, axis=0, mode="promise_in_bounds")

    def laplacian(self, ref, x):
        centre = [ref[x, :, pl.ds(v * LANES, LANES)] for v in range(VREGS)]
        lower = [pltpu.roll(c, EDGE, 1) for c in centre]
        upper = [pltpu.roll(c, LANES - EDGE, 1) for c in centre]
        out = []
        for v in range(VREGS):
            c = centre[v]
            lanes = pl.ds(v * LANES, LANES)
            if v:
                from_lower = lower[v - 1]
            else:
                from_lower = jnp.where(self.has_below_y, self.rows(lower[-1], self.below_y), c)
            if v < VREGS - 1:
                from_upper = upper[v + 1]
            else:
                from_upper = jnp.where(self.has_above_y, self.rows(upper[0], self.above_y), c)
            prev_y = jnp.where(self.y_first, from_lower, lower[v])
            next_y = jnp.where(self.y_last, from_upper, upper[v])
            prev_z = jnp.where(self.z_first, pltpu.roll(self.rows(c, self.below_z), LANES - EDGE + 1, 1), pltpu.roll(c, 1, 1))
            next_z = jnp.where(self.z_last, pltpu.roll(self.rows(c, self.above_z), EDGE - 1, 1), pltpu.roll(c, LANES - 1, 1))
            total = (ref[x - 1, :, lanes] + ref[x + 1, :, lanes]) + (prev_y + next_y) + (prev_z + next_z)
            out.append(total - 6.0 * c)
        return out, centre

    def advance(self, phi_ref, conc_ref, mob_ref, x, store):
        lapl_phi, phis = self.laplacian(phi_ref, x)
        lapl_conc, concs = self.laplacian(conc_ref, x)
        for v in range(VREGS):
            phi, conc = phis[v], concs[v]
            square = phi * phi
            wetting = 1.0 - square
            drive = lapl_phi[v] + phi - square * phi - coupling * conc * wetting * wetting
            change = time_step * mob_ref[x, :, pl.ds(v * LANES, LANES)] * drive
            store(v, phi + change, conc + time_step * lapl_conc[v] + 0.5 * change)

    def sweep(self, first, last, unroll, source, mob_ref, target, shift=None):
        phi_ref, conc_ref = source
        phi_out, conc_out = target

        def one(x):
            def store(v, phi, conc):
                if shift is None:
                    where = (x, slice(None), pl.ds(v * LANES, LANES))
                else:
                    where = (slice(None), pl.ds(pl.multiple_of((x - shift) * FACE + v * LANES, LANES), LANES))
                phi_out[where] = phi
                conc_out[where] = conc

            self.advance(phi_ref, conc_ref, mob_ref, x, store)

        whole = first + (last - first) // unroll * unroll
        if whole > first:

            @pl.loop(0, (whole - first) // unroll)
            def _(i):
                for u in range(unroll):
                    one(first + i * unroll + u)

        for x in range(whole, last):
            one(x)


def place(states, planes, at, *parts):
    for f, ref in enumerate(states):

        @pl.loop(0, planes // 2)
        def _(i):
            for u in range(2):
                x = 2 * i + u
                for v in range(VREGS):
                    value = sum(part[f, :, lanes_at((x + first) * FACE, v)] for part, first in parts)
                    ref[x + at, :, pl.ds(v * LANES, LANES)] = value


REST_AT = HALO + CHUNK_PLANES
TOP_AT = REST_AT + REST


def edge_kernel(
    here_ref, edge_ref, below_ref, above_ref, nbr_ref,
    phase_ref, solute_ref, kept0_ref, kept1_ref, kept2_ref,
    phi0, conc0, mob, phi1, conc1, phi2, conc2,
):
    st = Stencil(here_ref[0], nbr_ref[...])
    states = (phi0, conc0, mob)
    for f, ref in enumerate(states):
        for d in range(2 * CHUNK_PLANES):
            at = HALO + d if d < CHUNK_PLANES else TOP_AT + d - CHUNK_PLANES
            for v in range(VREGS):
                ref[at, :, pl.ds(v * LANES, LANES)] = edge_ref[f, :, pl.ds(d * FACE + v * LANES, LANES)]
        for d in range(HALO):
            for v in range(VREGS):
                lanes = pl.ds(v * LANES, LANES)
                part = pl.ds(d * FACE + v * LANES, LANES)
                mirror_low = ref[2 * HALO - 1 - d, :, lanes]
                ref[d, :, lanes] = jnp.where(st.has_below_x, st.rows(below_ref[f, :, part], st.below_x), mirror_low)
                mirror_high = ref[EDGE + HALO - 1 - d, :, lanes]
                ref[EDGE + HALO + d, :, lanes] = jnp.where(st.has_above_x, st.rows(above_ref[f, :, part], st.above_x), mirror_high)
    for first, last in ((1, REST_AT - 1), (TOP_AT + 1, EXT - 1)):
        st.sweep(first, last, 5, (phi0, conc0), mob, (phi1, conc1))
        st.sweep(first + 1, last - 1, 3, (phi1, conc1), mob, (phi2, conc2))
        st.sweep(first + 2, last - 2, 1, (phi2, conc2), mob, (phase_ref, solute_ref), HALO)
    for f, ref in enumerate(states):
        for n, x in enumerate((*range(REST_AT - 3, REST_AT), *range(TOP_AT, TOP_AT + 3))):
            kept0_ref[f, n] = ref[x]
    for f, ref in enumerate((phi1, conc1)):
        for n, x in enumerate((REST_AT - 3, REST_AT - 2, TOP_AT + 1, TOP_AT + 2)):
            kept1_ref[f, n] = ref[x]
    for f, ref in enumerate((phi2, conc2)):
        for n, x in enumerate((REST_AT - 4, REST_AT - 3, TOP_AT + 2, TOP_AT + 3)):
            kept2_ref[f, n] = ref[x]


BACK = REST_AT - 4
MAIN_PLANES = TOP_AT + 4 - BACK
OUT_FIRST = REST_AT - 3
OUT_PLANES = TOP_AT + 3 - OUT_FIRST
PIECE = 10
PIECES = OUT_PLANES // PIECE


def main_kernel(
    here_ref, stay_ref, far_ref, far_late_ref, back_ref, nbr_ref, kept0_ref, kept1_ref, kept2_ref, _phase_in, _solute_in,
    phase_hbm, solute_hbm,
    phi0, conc0, mob, phi1, conc1, phi2, conc2, phase_ref, solute_ref, sems,
):
    st = Stencil(here_ref[0], nbr_ref[...])
    states = (phi0, conc0, mob)
    first, last = REST_AT - BACK, TOP_AT - BACK
    for f, ref in enumerate(states):
        for n, x in enumerate((*range(first - 3, first), *range(last, last + 3))):
            ref[x] = kept0_ref[f, n]
    for f, ref in enumerate((phi1, conc1)):
        for n, x in enumerate((first - 3, first - 2, last + 1, last + 2)):
            ref[x] = kept1_ref[f, n]
    for f, ref in enumerate((phi2, conc2)):
        for n, x in enumerate((first - 4, first - 3, last + 2, last + 3)):
            ref[x] = kept2_ref[f, n]
    place(states, AHEAD, first, (stay_ref, 0), (far_ref, 2 * CHUNK_PLANES), (back_ref, 0))
    place(states, REST - AHEAD, first + AHEAD, (stay_ref, AHEAD), (far_late_ref, 0), (back_ref, AHEAD))
    st.sweep(first - 1, last + 1, REST + 2, (phi0, conc0), mob, (phi1, conc1))
    st.sweep(first - 2, last + 2, REST + 4, (phi1, conc1), mob, (phi2, conc2))
    start = first - 3
    copies = []
    for piece in range(PIECES):
        at = start + piece * PIECE
        st.sweep(at, at + PIECE, PIECE, (phi2, conc2), mob, (phase_ref, solute_ref), start)
        source = pl.ds(piece * PIECE * FACE, PIECE * FACE)
        target = pl.ds((OUT_FIRST - HALO + piece * PIECE) * FACE, PIECE * FACE)
        for n, (ref, hbm) in enumerate(((phase_ref, phase_hbm), (solute_ref, solute_hbm))):
            copies.append(pltpu.make_async_copy(ref.at[:, source], hbm.at[:, target], sems.at[piece, n]))
            copies[-1].start()
    for copy in copies:
        copy.wait()


SMEM = pl.BlockSpec(memory_space=pltpu.SMEM)
VMEM = pl.BlockSpec(memory_space=pltpu.VMEM)
HBM = pl.BlockSpec(memory_space=pltpu.HBM)
ANY = pl.BlockSpec(memory_space=pl.ANY)
PARAMS = pltpu.CompilerParams(vmem_limit_bytes=32 * 2**20)


def shaped(planes, fields=FIELDS):
    return jax.ShapeDtypeStruct((fields, CAP, planes * FACE), jnp.float32)


def cost(moved, flops=10**6):
    return pl.CostEstimate(flops=flops, bytes_accessed=moved, transcendentals=0)


MB = 2**20


def on_device(old_phase, old_solute, old_mobility, new_global_slot, neighbors):
    count = lax.axis_size("blk")
    here = lax.axis_index("blk").astype(jnp.int32).reshape(1)
    olds = tuple(pltpu.with_memory_space_constraint(x, pltpu.HBM) for x in (old_phase, old_solute, old_mobility))
    devices = range(count)

    def sent(block, route):
        return lax.ppermute(block, "blk", [(p, q) for p, q in route if 0 <= q < count])

    def outward(p):
        return -2 if p % 2 == 0 else 2

    partner = [(p, p ^ 1) for p in devices]
    far_route = [(p, p + outward(p)) for p in devices]
    back_route = [(p, p - outward(p)) for p in devices]

    def after(block, *others):
        return lax.optimization_barrier((block, *others))[0]

    slots_hbm = pltpu.with_memory_space_constraint(new_global_slot, pltpu.HBM)
    old_shape = jax.ShapeDtypeStruct((OLD, CELLS), jnp.float32)
    *olds, merge, final, far_first, far_late = pl.pallas_call(
        pack_kernel,
        in_specs=[SMEM, HBM, HBM, HBM, HBM],
        out_specs=[VMEM] * 7,
        out_shape=[old_shape] * 3 + [shaped(EDGE)] * 2 + [shaped(2 * CHUNK_PLANES + AHEAD), shaped(REST - AHEAD)],
        scratch_shapes=[pltpu.SMEM((OLD,), jnp.int32), pltpu.SemaphoreType.DMA, pltpu.SemaphoreType.DMA((CHUNKS, FIELDS))],
        compiler_params=PARAMS,
        cost_estimate=cost(6 * MB),
        name="pack",
    )(here, slots_hbm, *olds)
    far_first_got = sent(far_first, far_route)
    merge_got = sent(merge, partner)
    final_got = sent(final, partner)

    two_parts = [shaped(2 * CHUNK_PLANES), shaped(REST)]
    back_edge, back_rest = pl.pallas_call(
        relay_kernel,
        in_specs=[SMEM, SMEM] + [VMEM] * 4,
        out_specs=[VMEM] * 2,
        out_shape=two_parts,
        compiler_params=PARAMS,
        cost_estimate=cost(6 * MB),
        name="relay",
    )(here, new_global_slot, *olds, merge_got)
    back_edge_got = sent(back_edge, back_route)

    stay_edge, stay_rest = pl.pallas_call(
        stay_kernel,
        in_specs=[SMEM, SMEM] + [VMEM] * 4,
        out_specs=[VMEM] * 2,
        out_shape=two_parts,
        compiler_params=PARAMS,
        cost_estimate=cost(6 * MB),
        name="stay",
    )(here, new_global_slot, *olds, final_got)
    back_rest_got = sent(after(back_rest, back_edge_got, stay_edge), back_route)

    edges = pl.BlockSpec((FIELDS, CAP, 2 * CHUNK), lambda i: (0, 0, 0))
    faces = pl.BlockSpec((FIELDS, CAP, HALO * FACE), lambda i: (0, 0, 0))
    edge, low, high = pl.pallas_call(
        face_kernel,
        grid=(1,),
        in_specs=[edges] * 3,
        out_specs=[edges, faces, faces],
        out_shape=[shaped(2 * CHUNK_PLANES), shaped(HALO), shaped(HALO)],
        compiler_params=PARAMS,
        cost_estimate=cost(3 * MB),
        name="faces",
    )(stay_edge, far_first_got, back_edge_got)
    below = sent(high, [(p, p + 1) for p in devices])
    above = sent(low, [(p, p - 1) for p in devices])
    far_late_got = sent(after(far_late, below, above), far_route)

    state = pltpu.VMEM((EXT, CAP, FACE), jnp.float32)
    whole = jax.ShapeDtypeStruct((CAP, CELLS), jnp.float32)

    def kept(fields, planes):
        return jax.ShapeDtypeStruct((fields, planes, CAP, FACE), jnp.float32)

    phase, solute, kept0, kept1, kept2 = pl.pallas_call(
        edge_kernel,
        in_specs=[SMEM] + [VMEM] * 4,
        out_specs=[VMEM] * 5,
        out_shape=[whole, whole, kept(3, 6), kept(2, 4), kept(2, 4)],
        scratch_shapes=[state] * 7,
        compiler_params=PARAMS,
        cost_estimate=cost(8 * MB),
        name="edge_steps",
    )(here, edge, below, above, neighbors)

    state = pltpu.VMEM((MAIN_PLANES, CAP, FACE), jnp.float32)
    rows_out = pltpu.VMEM((CAP, OUT_PLANES * FACE), jnp.float32)
    phase, solute = pl.pallas_call(
        main_kernel,
        in_specs=[SMEM] + [VMEM] * 8 + [HBM] * 2,
        out_specs=[HBM] * 2,
        out_shape=[whole, whole],
        scratch_shapes=[state] * 7 + [rows_out] * 2 + [pltpu.SemaphoreType.DMA((PIECES, 2))],
        input_output_aliases={9: 0, 10: 1},
        compiler_params=PARAMS,
        cost_estimate=cost(20 * MB),
        name="main_steps",
    )(here, stay_rest, far_first_got, far_late_got, back_rest_got, neighbors, kept0, kept1, kept2, phase, solute)
    return phase, solute


def solution(mesh):
    placed = (P("blk", None), P("blk", None), P("blk", None), P("blk"), P("blk", None))
    return jax.shard_map(
        on_device,
        mesh=mesh,
        in_specs=placed,
        out_specs=(P("blk", None), P("blk", None)),
        check_vma=False,
    )
```

```python
import functools

import jax
import jax.numpy as jnp
from jax import lax
from jax.experimental import pallas as pl
from jax.experimental.pallas import tpu as pltpu
from jax.sharding import PartitionSpec as P

EDGE = 32
FACE = EDGE * EDGE
CELLS = EDGE * FACE
CAP = 8
OLD = 16
FIELDS = 3
HALO = 3
CHUNK_PLANES = 4
CHUNK = CHUNK_PLANES * FACE
CHUNKS = EDGE // CHUNK_PLANES
LANES = 128
EXT = EDGE + 2 * HALO
REST = EDGE - 2 * CHUNK_PLANES
VREGS = FACE // LANES

time_step = 0.15
coupling = 1.5


def windows(slot_ref, here):
    first = slot_ref[0]
    count = jnp.int32(0)
    for i in range(OLD):
        count += (slot_ref[i] >= 0).astype(jnp.int32)
    amount = jnp.bitwise_and(first, CAP - 1)
    row = lax.broadcasted_iota(jnp.int32, (CAP, LANES), 0)

    def masks(k):
        index = row + ((here + k) * CAP - first)
        low = (index >= 0) & (index < CAP) & (index < count)
        high = (index >= CAP) & (index < count)
        return low, high

    return amount, masks


def picked(masks, low_rows, high_rows):
    low, high = masks
    return jnp.where(low, low_rows, jnp.where(high, high_rows, 0.0))


def side_of(here):
    return jnp.where(jnp.bitwise_and(here, 1) == 0, -1, 1)


def aligned(ref, lanes, amount):
    return pltpu.roll(ref[0:CAP, lanes], amount, 0), pltpu.roll(ref[CAP:OLD, lanes], amount, 0)


def chunk_at(i):
    return jnp.where(i == 0, 0, jnp.where(i == 1, CHUNKS - 1, i - 1))


def lanes_at(start, v):
    return pl.ds(pl.multiple_of(start + v * LANES, LANES), LANES)


def pack_kernel(
    here_ref, slot_hbm, phi_hbm, conc_hbm, mob_hbm,
    phi_ref, conc_ref, mob_ref, merge_ref, final_ref, far_ref,
    slot_ref, slot_sem, sems,
):
    olds = tuple(zip((phi_hbm, conc_hbm, mob_hbm), (phi_ref, conc_ref, mob_ref)))

    def copies(i):
        lanes = pl.ds(pl.multiple_of(chunk_at(i) * CHUNK, CHUNK), CHUNK)
        return [pltpu.make_async_copy(hbm.at[:, lanes], ref.at[:, lanes], sems.at[i, f]) for f, (hbm, ref) in enumerate(olds)]

    slot_copy = pltpu.make_async_copy(slot_hbm, slot_ref, slot_sem)
    slot_copy.start()

    @pl.loop(0, CHUNKS)
    def _(i):
        for copy in copies(i):
            copy.start()

    slot_copy.wait()
    here = here_ref[0]
    side = side_of(here)
    amount, masks = windows(slot_ref, here)
    far, merge, final = masks(2 * side), masks(side), masks(-side)

    def fill(i):
        start = chunk_at(i) * CHUNK
        for f, (_, ref) in enumerate(olds):
            for v in range(CHUNK // LANES):
                lanes = lanes_at(start, v)
                rows = aligned(ref, lanes, amount)
                merge_ref[f, :, lanes] = picked(merge, *rows)
                final_ref[f, :, lanes] = picked(final, *rows)
                far_ref[f, :, lanes_at(i * CHUNK, v)] = picked(far, *rows)

    @pl.loop(0, CHUNKS)
    def _(i):
        for copy in copies(i):
            copy.wait()
        fill(i)


def add_rows(masks, amount, old_refs, add_ref, edge_ref, rest_ref):
    for out_ref, out_plane, plane, count in (
        (edge_ref, 0, 0, CHUNK_PLANES),
        (edge_ref, CHUNK_PLANES, CHUNK_PLANES + REST, CHUNK_PLANES),
        (rest_ref, 0, CHUNK_PLANES, REST),
    ):

        @pl.loop(0, count // 2)
        def _(i):
            for f, ref in enumerate(old_refs):
                for v in range(2 * VREGS):
                    lanes = lanes_at((plane + 2 * i) * FACE, v)
                    value = picked(masks, *aligned(ref, lanes, amount)) + add_ref[f, :, lanes]
                    out_ref[f, :, lanes_at((out_plane + 2 * i) * FACE, v)] = value


def relay_kernel(here_ref, slot_ref, phi_ref, conc_ref, mob_ref, merge_ref, *part_refs):
    here = here_ref[0]
    amount, masks = windows(slot_ref, here)
    add_rows(masks(-2 * side_of(here)), amount, (phi_ref, conc_ref, mob_ref), merge_ref, *part_refs)


def stay_kernel(here_ref, slot_ref, phi_ref, conc_ref, mob_ref, final_ref, *part_refs):
    here = here_ref[0]
    amount, masks = windows(slot_ref, here)
    add_rows(masks(0), amount, (phi_ref, conc_ref, mob_ref), final_ref, *part_refs)


def face_kernel(stay_ref, far_ref, back_ref, edge_ref, low_ref, high_ref):
    first_high = (2 * CHUNK_PLANES - HALO) * FACE
    for f in range(FIELDS):
        for v in range(2 * CHUNK_PLANES * VREGS):
            lanes = pl.ds(v * LANES, LANES)
            value = stay_ref[f, :, lanes] + far_ref[f, :, lanes] + back_ref[f, :, lanes]
            edge_ref[f, :, lanes] = value
            at = v * LANES
            if at < HALO * FACE:
                low_ref[f, :, lanes] = value
            if at >= first_high:
                high_ref[f, :, pl.ds(at - first_high, LANES)] = value


class Stencil:
    def __init__(self, here, nbr):
        base = here * CAP
        self.nbr = nbr
        lane = lax.broadcasted_iota(jnp.int32, (CAP, LANES), 1)
        z = jnp.bitwise_and(lane, EDGE - 1)
        self.z_first, self.z_last = z == 0, z == EDGE - 1
        self.y_first, self.y_last = lane < EDGE, lane >= LANES - EDGE
        self.below_x, self.has_below_x = self.column(0, base - CAP)
        self.above_x, self.has_above_x = self.column(1, base + CAP)
        self.below_y, self.has_below_y = self.column(2, base)
        self.above_y, self.has_above_y = self.column(3, base)
        self.below_z, _ = self.column(4, base)
        self.above_z, _ = self.column(5, base)

    def column(self, c, start):
        wide = jnp.broadcast_to(self.nbr[:, c : c + 1], (CAP, LANES))
        valid = wide >= 0
        return jnp.where(valid, wide - start, 0), valid

    @staticmethod
    def rows(x, index):
        return jnp.take_along_axis(x, index, axis=0, mode="promise_in_bounds")

    def laplacian(self, ref, x):
        centre = [ref[x, :, pl.ds(v * LANES, LANES)] for v in range(VREGS)]
        lower = [pltpu.roll(c, EDGE, 1) for c in centre]
        upper = [pltpu.roll(c, LANES - EDGE, 1) for c in centre]
        out = []
        for v in range(VREGS):
            c = centre[v]
            lanes = pl.ds(v * LANES, LANES)
            if v:
                from_lower = lower[v - 1]
            else:
                from_lower = jnp.where(self.has_below_y, self.rows(lower[-1], self.below_y), c)
            if v < VREGS - 1:
                from_upper = upper[v + 1]
            else:
                from_upper = jnp.where(self.has_above_y, self.rows(upper[0], self.above_y), c)
            prev_y = jnp.where(self.y_first, from_lower, lower[v])
            next_y = jnp.where(self.y_last, from_upper, upper[v])
            prev_z = jnp.where(self.z_first, pltpu.roll(self.rows(c, self.below_z), LANES - EDGE + 1, 1), pltpu.roll(c, 1, 1))
            next_z = jnp.where(self.z_last, pltpu.roll(self.rows(c, self.above_z), EDGE - 1, 1), pltpu.roll(c, LANES - 1, 1))
            total = (ref[x - 1, :, lanes] + ref[x + 1, :, lanes]) + (prev_y + next_y) + (prev_z + next_z)
            out.append(total - 6.0 * c)
        return out, centre

    def advance(self, phi_ref, conc_ref, mob_ref, x, store):
        lapl_phi, phis = self.laplacian(phi_ref, x)
        lapl_conc, concs = self.laplacian(conc_ref, x)
        for v in range(VREGS):
            phi, conc = phis[v], concs[v]
            square = phi * phi
            wetting = 1.0 - square
            drive = lapl_phi[v] + phi - square * phi - coupling * conc * wetting * wetting
            change = time_step * mob_ref[x, :, pl.ds(v * LANES, LANES)] * drive
            store(v, phi + change, conc + time_step * lapl_conc[v] + 0.5 * change)

    def sweep(self, first, last, unroll, source, mob_ref, target, shift=None):
        phi_ref, conc_ref = source
        phi_out, conc_out = target

        def one(x):
            def store(v, phi, conc):
                if shift is None:
                    where = (x, slice(None), pl.ds(v * LANES, LANES))
                else:
                    where = (slice(None), pl.ds(pl.multiple_of((x - shift) * FACE + v * LANES, LANES), LANES))
                phi_out[where] = phi
                conc_out[where] = conc

            self.advance(phi_ref, conc_ref, mob_ref, x, store)

        whole = first + (last - first) // unroll * unroll
        if whole > first:

            @pl.loop(0, (whole - first) // unroll)
            def _(i):
                for u in range(unroll):
                    one(first + i * unroll + u)

        for x in range(whole, last):
            one(x)


def place(states, planes, at, *parts):
    for f, ref in enumerate(states):

        @pl.loop(0, planes // 2)
        def _(i):
            for u in range(2):
                x = 2 * i + u
                for v in range(VREGS):
                    value = sum(part[f, :, lanes_at((x + first) * FACE, v)] for part, first in parts)
                    ref[x + at, :, pl.ds(v * LANES, LANES)] = value


REST_AT = HALO + CHUNK_PLANES
TOP_AT = REST_AT + REST


def edge_kernel(
    here_ref, edge_ref, below_ref, above_ref, nbr_ref,
    phase_ref, solute_ref, kept0_ref, kept1_ref, kept2_ref,
    phi0, conc0, mob, phi1, conc1, phi2, conc2,
):
    st = Stencil(here_ref[0], nbr_ref[...])
    states = (phi0, conc0, mob)
    for f, ref in enumerate(states):
        for d in range(2 * CHUNK_PLANES):
            at = HALO + d if d < CHUNK_PLANES else TOP_AT + d - CHUNK_PLANES
            for v in range(VREGS):
                ref[at, :, pl.ds(v * LANES, LANES)] = edge_ref[f, :, pl.ds(d * FACE + v * LANES, LANES)]
        for d in range(HALO):
            for v in range(VREGS):
                lanes = pl.ds(v * LANES, LANES)
                part = pl.ds(d * FACE + v * LANES, LANES)
                mirror_low = ref[2 * HALO - 1 - d, :, lanes]
                ref[d, :, lanes] = jnp.where(st.has_below_x, st.rows(below_ref[f, :, part], st.below_x), mirror_low)
                mirror_high = ref[EDGE + HALO - 1 - d, :, lanes]
                ref[EDGE + HALO + d, :, lanes] = jnp.where(st.has_above_x, st.rows(above_ref[f, :, part], st.above_x), mirror_high)
    for first, last in ((1, REST_AT - 1), (TOP_AT + 1, EXT - 1)):
        st.sweep(first, last, 5, (phi0, conc0), mob, (phi1, conc1))
        st.sweep(first + 1, last - 1, 3, (phi1, conc1), mob, (phi2, conc2))
        st.sweep(first + 2, last - 2, 1, (phi2, conc2), mob, (phase_ref, solute_ref), HALO)
    for f, ref in enumerate(states):
        for n, x in enumerate((*range(REST_AT - 3, REST_AT), *range(TOP_AT, TOP_AT + 3))):
            kept0_ref[f, n] = ref[x]
    for f, ref in enumerate((phi1, conc1)):
        for n, x in enumerate((REST_AT - 3, REST_AT - 2, TOP_AT + 1, TOP_AT + 2)):
            kept1_ref[f, n] = ref[x]
    for f, ref in enumerate((phi2, conc2)):
        for n, x in enumerate((REST_AT - 4, REST_AT - 3, TOP_AT + 2, TOP_AT + 3)):
            kept2_ref[f, n] = ref[x]


BACK = REST_AT - 4
MAIN_PLANES = TOP_AT + 4 - BACK
OUT_FIRST = REST_AT - 3
OUT_PLANES = TOP_AT + 3 - OUT_FIRST
PIECE = 10
PIECES = OUT_PLANES // PIECE


def main_kernel(
    here_ref, stay_ref, far_ref, back_ref, nbr_ref, kept0_ref, kept1_ref, kept2_ref, _phase_in, _solute_in,
    phase_hbm, solute_hbm,
    phi0, conc0, mob, phi1, conc1, phi2, conc2, phase_ref, solute_ref, sems,
):
    st = Stencil(here_ref[0], nbr_ref[...])
    states = (phi0, conc0, mob)
    first, last = REST_AT - BACK, TOP_AT - BACK
    for f, ref in enumerate(states):
        for n, x in enumerate((*range(first - 3, first), *range(last, last + 3))):
            ref[x] = kept0_ref[f, n]
    for f, ref in enumerate((phi1, conc1)):
        for n, x in enumerate((first - 3, first - 2, last + 1, last + 2)):
            ref[x] = kept1_ref[f, n]
    for f, ref in enumerate((phi2, conc2)):
        for n, x in enumerate((first - 4, first - 3, last + 2, last + 3)):
            ref[x] = kept2_ref[f, n]
    place(states, REST, first, (stay_ref, 0), (far_ref, 2 * CHUNK_PLANES), (back_ref, 0))
    st.sweep(first - 1, last + 1, REST + 2, (phi0, conc0), mob, (phi1, conc1))
    st.sweep(first - 2, last + 2, REST + 4, (phi1, conc1), mob, (phi2, conc2))
    start = first - 3
    copies = []
    for piece in range(PIECES):
        at = start + piece * PIECE
        st.sweep(at, at + PIECE, PIECE, (phi2, conc2), mob, (phase_ref, solute_ref), start)
        source = pl.ds(piece * PIECE * FACE, PIECE * FACE)
        target = pl.ds((OUT_FIRST - HALO + piece * PIECE) * FACE, PIECE * FACE)
        for n, (ref, hbm) in enumerate(((phase_ref, phase_hbm), (solute_ref, solute_hbm))):
            copies.append(pltpu.make_async_copy(ref.at[:, source], hbm.at[:, target], sems.at[piece, n]))
            copies[-1].start()
    for copy in copies:
        copy.wait()


SMEM = pl.BlockSpec(memory_space=pltpu.SMEM)
VMEM = pl.BlockSpec(memory_space=pltpu.VMEM)
HBM = pl.BlockSpec(memory_space=pltpu.HBM)
ANY = pl.BlockSpec(memory_space=pl.ANY)
PARAMS = pltpu.CompilerParams(vmem_limit_bytes=32 * 2**20)


def shaped(planes, fields=FIELDS):
    return jax.ShapeDtypeStruct((fields, CAP, planes * FACE), jnp.float32)


def cost(moved, flops=10**6):
    return pl.CostEstimate(flops=flops, bytes_accessed=moved, transcendentals=0)


MB = 2**20


def on_device(old_phase, old_solute, old_mobility, new_global_slot, neighbors):
    count = lax.axis_size("blk")
    here = lax.axis_index("blk").astype(jnp.int32).reshape(1)
    olds = tuple(pltpu.with_memory_space_constraint(x, pltpu.HBM) for x in (old_phase, old_solute, old_mobility))
    devices = range(count)

    def sent(block, route):
        return lax.ppermute(block, "blk", [(p, q) for p, q in route if 0 <= q < count])

    def outward(p):
        return -2 if p % 2 == 0 else 2

    partner = [(p, p ^ 1) for p in devices]
    far_route = [(p, p + outward(p)) for p in devices]
    back_route = [(p, p - outward(p)) for p in devices]

    def after(block, *others):
        return lax.optimization_barrier((block, *others))[0]

    slots_hbm = pltpu.with_memory_space_constraint(new_global_slot, pltpu.HBM)
    old_shape = jax.ShapeDtypeStruct((OLD, CELLS), jnp.float32)
    *olds, merge, final, far_all = pl.pallas_call(
        pack_kernel,
        in_specs=[SMEM, HBM, HBM, HBM, HBM],
        out_specs=[VMEM] * 6,
        out_shape=[old_shape] * 3 + [shaped(EDGE)] * 3,
        scratch_shapes=[pltpu.SMEM((OLD,), jnp.int32), pltpu.SemaphoreType.DMA, pltpu.SemaphoreType.DMA((CHUNKS, FIELDS))],
        compiler_params=PARAMS,
        cost_estimate=cost(6 * MB),
        name="pack",
    )(here, slots_hbm, *olds)
    far_got = sent(far_all, far_route)
    merge_got = sent(merge, partner)
    final_got = sent(final, partner)

    two_parts = [shaped(2 * CHUNK_PLANES), shaped(REST)]
    back_edge, back_rest = pl.pallas_call(
        relay_kernel,
        in_specs=[SMEM, SMEM] + [VMEM] * 4,
        out_specs=[VMEM] * 2,
        out_shape=two_parts,
        compiler_params=PARAMS,
        cost_estimate=cost(6 * MB),
        name="relay",
    )(here, new_global_slot, *olds, merge_got)
    back_edge_got = sent(back_edge, back_route)

    stay_edge, stay_rest = pl.pallas_call(
        stay_kernel,
        in_specs=[SMEM, SMEM] + [VMEM] * 4,
        out_specs=[VMEM] * 2,
        out_shape=two_parts,
        compiler_params=PARAMS,
        cost_estimate=cost(6 * MB),
        name="stay",
    )(here, new_global_slot, *olds, final_got)
    back_rest_got = sent(after(back_rest, back_edge_got, stay_edge), back_route)

    edges = pl.BlockSpec((FIELDS, CAP, 2 * CHUNK), lambda i: (0, 0, 0))
    faces = pl.BlockSpec((FIELDS, CAP, HALO * FACE), lambda i: (0, 0, 0))
    edge, low, high = pl.pallas_call(
        face_kernel,
        grid=(1,),
        in_specs=[edges] * 3,
        out_specs=[edges, faces, faces],
        out_shape=[shaped(2 * CHUNK_PLANES), shaped(HALO), shaped(HALO)],
        compiler_params=PARAMS,
        cost_estimate=cost(3 * MB),
        name="faces",
    )(stay_edge, far_got, back_edge_got)
    below = sent(high, [(p, p + 1) for p in devices])
    above = sent(low, [(p, p - 1) for p in devices])

    state = pltpu.VMEM((EXT, CAP, FACE), jnp.float32)
    whole = jax.ShapeDtypeStruct((CAP, CELLS), jnp.float32)

    def kept(fields, planes):
        return jax.ShapeDtypeStruct((fields, planes, CAP, FACE), jnp.float32)

    phase, solute, kept0, kept1, kept2 = pl.pallas_call(
        edge_kernel,
        in_specs=[SMEM] + [VMEM] * 4,
        out_specs=[VMEM] * 5,
        out_shape=[whole, whole, kept(3, 6), kept(2, 4), kept(2, 4)],
        scratch_shapes=[state] * 7,
        compiler_params=PARAMS,
        cost_estimate=cost(8 * MB),
        name="edge_steps",
    )(here, edge, below, above, neighbors)

    state = pltpu.VMEM((MAIN_PLANES, CAP, FACE), jnp.float32)
    rows_out = pltpu.VMEM((CAP, OUT_PLANES * FACE), jnp.float32)
    phase, solute = pl.pallas_call(
        main_kernel,
        in_specs=[SMEM] + [VMEM] * 7 + [HBM] * 2,
        out_specs=[HBM] * 2,
        out_shape=[whole, whole],
        scratch_shapes=[state] * 7 + [rows_out] * 2 + [pltpu.SemaphoreType.DMA((PIECES, 2))],
        input_output_aliases={8: 0, 9: 1},
        compiler_params=PARAMS,
        cost_estimate=cost(20 * MB),
        name="main_steps",
    )(here, stay_rest, far_got, back_rest_got, neighbors, kept0, kept1, kept2, phase, solute)
    return phase, solute


def solution(mesh):
    placed = (P("blk", None), P("blk", None), P("blk", None), P("blk"), P("blk", None))
    return jax.shard_map(
        on_device,
        mesh=mesh,
        in_specs=placed,
        out_specs=(P("blk", None), P("blk", None)),
        check_vma=False,
    )
```

```python
import functools

import jax
import jax.numpy as jnp
from jax import lax
from jax.experimental import pallas as pl
from jax.experimental.pallas import tpu as pltpu
from jax.sharding import PartitionSpec as P

EDGE = 32
FACE = EDGE * EDGE
CELLS = EDGE * FACE
CAP = 8
OLD = 16
FIELDS = 3
HALO = 3
CHUNK_PLANES = 4
CHUNK = CHUNK_PLANES * FACE
CHUNKS = EDGE // CHUNK_PLANES
LANES = 128
EXT = EDGE + 2 * HALO
REST = EDGE - 2 * CHUNK_PLANES
AHEAD = 16
FIRST_STEPS = 2 + AHEAD // CHUNK_PLANES
VREGS = FACE // LANES

time_step = 0.15
coupling = 1.5


def windows(slot_ref, here):
    first = slot_ref[0]
    count = jnp.int32(0)
    for i in range(OLD):
        count += (slot_ref[i] >= 0).astype(jnp.int32)
    amount = jnp.bitwise_and(first, CAP - 1)
    row = lax.broadcasted_iota(jnp.int32, (CAP, LANES), 0)

    def masks(k):
        index = row + ((here + k) * CAP - first)
        low = (index >= 0) & (index < CAP) & (index < count)
        high = (index >= CAP) & (index < count)
        return low, high

    return amount, masks


def picked(masks, low_rows, high_rows):
    low, high = masks
    return jnp.where(low, low_rows, jnp.where(high, high_rows, 0.0))


def side_of(here):
    return jnp.where(jnp.bitwise_and(here, 1) == 0, -1, 1)


def aligned(ref, lanes, amount):
    return pltpu.roll(ref[0:CAP, lanes], amount, 0), pltpu.roll(ref[CAP:OLD, lanes], amount, 0)


def chunk_at(i):
    return jnp.where(i == 0, 0, jnp.where(i == 1, CHUNKS - 1, i - 1))


def lanes_at(start, v):
    return pl.ds(pl.multiple_of(start + v * LANES, LANES), LANES)


def pack_kernel(
    here_ref, slot_hbm, phi_hbm, conc_hbm, mob_hbm,
    phi_ref, conc_ref, mob_ref, merge_ref, final_ref, far_ref, late_ref,
    slot_ref, slot_sem, sems,
):
    olds = tuple(zip((phi_hbm, conc_hbm, mob_hbm), (phi_ref, conc_ref, mob_ref)))

    def copies(i):
        lanes = pl.ds(pl.multiple_of(chunk_at(i) * CHUNK, CHUNK), CHUNK)
        return [pltpu.make_async_copy(hbm.at[:, lanes], ref.at[:, lanes], sems.at[i, f]) for f, (hbm, ref) in enumerate(olds)]

    slot_copy = pltpu.make_async_copy(slot_hbm, slot_ref, slot_sem)
    slot_copy.start()

    @pl.loop(0, CHUNKS)
    def _(i):
        for copy in copies(i):
            copy.start()

    slot_copy.wait()
    here = here_ref[0]
    side = side_of(here)
    amount, masks = windows(slot_ref, here)
    far, merge, final = masks(2 * side), masks(side), masks(-side)

    def fill(i, out_ref, out_start):
        start = chunk_at(i) * CHUNK
        for f, (_, ref) in enumerate(olds):
            for v in range(CHUNK // LANES):
                lanes = lanes_at(start, v)
                rows = aligned(ref, lanes, amount)
                merge_ref[f, :, lanes] = picked(merge, *rows)
                final_ref[f, :, lanes] = picked(final, *rows)
                out_ref[f, :, lanes_at(out_start, v)] = picked(far, *rows)

    @pl.loop(0, FIRST_STEPS)
    def _(i):
        for copy in copies(i):
            copy.wait()
        fill(i, far_ref, i * CHUNK)

    @pl.loop(FIRST_STEPS, CHUNKS)
    def _(i):
        for copy in copies(i):
            copy.wait()
        fill(i, late_ref, (i - FIRST_STEPS) * CHUNK)


def add_rows(masks, amount, old_refs, add_ref, edge_ref, rest_ref):
    for out_ref, out_plane, plane, count in (
        (edge_ref, 0, 0, CHUNK_PLANES),
        (edge_ref, CHUNK_PLANES, CHUNK_PLANES + REST, CHUNK_PLANES),
        (rest_ref, 0, CHUNK_PLANES, REST),
    ):

        @pl.loop(0, count // 2)
        def _(i):
            for f, ref in enumerate(old_refs):
                for v in range(2 * VREGS):
                    lanes = lanes_at((plane + 2 * i) * FACE, v)
                    value = picked(masks, *aligned(ref, lanes, amount)) + add_ref[f, :, lanes]
                    out_ref[f, :, lanes_at((out_plane + 2 * i) * FACE, v)] = value


def relay_kernel(here_ref, slot_ref, phi_ref, conc_ref, mob_ref, merge_ref, *part_refs):
    here = here_ref[0]
    amount, masks = windows(slot_ref, here)
    add_rows(masks(-2 * side_of(here)), amount, (phi_ref, conc_ref, mob_ref), merge_ref, *part_refs)


def stay_kernel(here_ref, slot_ref, phi_ref, conc_ref, mob_ref, final_ref, *part_refs):
    here = here_ref[0]
    amount, masks = windows(slot_ref, here)
    add_rows(masks(0), amount, (phi_ref, conc_ref, mob_ref), final_ref, *part_refs)


def face_kernel(stay_ref, far_ref, back_ref, edge_ref, low_ref, high_ref):
    first_high = (2 * CHUNK_PLANES - HALO) * FACE
    for f in range(FIELDS):
        for v in range(2 * CHUNK_PLANES * VREGS):
            lanes = pl.ds(v * LANES, LANES)
            value = stay_ref[f, :, lanes] + far_ref[f, :, lanes] + back_ref[f, :, lanes]
            edge_ref[f, :, lanes] = value
            at = v * LANES
            if at < HALO * FACE:
                low_ref[f, :, lanes] = value
            if at >= first_high:
                high_ref[f, :, pl.ds(at - first_high, LANES)] = value


class Stencil:
    def __init__(self, here, nbr):
        base = here * CAP
        self.nbr = nbr
        lane = lax.broadcasted_iota(jnp.int32, (CAP, LANES), 1)
        z = jnp.bitwise_and(lane, EDGE - 1)
        self.z_first, self.z_last = z == 0, z == EDGE - 1
        self.y_first, self.y_last = lane < EDGE, lane >= LANES - EDGE
        self.below_x, self.has_below_x = self.column(0, base - CAP)
        self.above_x, self.has_above_x = self.column(1, base + CAP)
        self.below_y, self.has_below_y = self.column(2, base)
        self.above_y, self.has_above_y = self.column(3, base)
        self.below_z, _ = self.column(4, base)
        self.above_z, _ = self.column(5, base)

    def column(self, c, start):
        wide = jnp.broadcast_to(self.nbr[:, c : c + 1], (CAP, LANES))
        valid = wide >= 0
        return jnp.where(valid, wide - start, 0), valid

    @staticmethod
    def rows(x, index):
        return jnp.take_along_axis(x, index, axis=0, mode="promise_in_bounds")

    def laplacian(self, ref, x):
        centre = [ref[x, :, pl.ds(v * LANES, LANES)] for v in range(VREGS)]
        lower = [pltpu.roll(c, EDGE, 1) for c in centre]
        upper = [pltpu.roll(c, LANES - EDGE, 1) for c in centre]
        out = []
        for v in range(VREGS):
            c = centre[v]
            lanes = pl.ds(v * LANES, LANES)
            if v:
                from_lower = lower[v - 1]
            else:
                from_lower = jnp.where(self.has_below_y, self.rows(lower[-1], self.below_y), c)
            if v < VREGS - 1:
                from_upper = upper[v + 1]
            else:
                from_upper = jnp.where(self.has_above_y, self.rows(upper[0], self.above_y), c)
            prev_y = jnp.where(self.y_first, from_lower, lower[v])
            next_y = jnp.where(self.y_last, from_upper, upper[v])
            prev_z = jnp.where(self.z_first, pltpu.roll(self.rows(c, self.below_z), LANES - EDGE + 1, 1), pltpu.roll(c, 1, 1))
            next_z = jnp.where(self.z_last, pltpu.roll(self.rows(c, self.above_z), EDGE - 1, 1), pltpu.roll(c, LANES - 1, 1))
            total = (ref[x - 1, :, lanes] + ref[x + 1, :, lanes]) + (prev_y + next_y) + (prev_z + next_z)
            out.append(total - 6.0 * c)
        return out, centre

    def advance(self, phi_ref, conc_ref, mob_ref, x, store):
        lapl_phi, phis = self.laplacian(phi_ref, x)
        lapl_conc, concs = self.laplacian(conc_ref, x)
        for v in range(VREGS):
            phi, conc = phis[v], concs[v]
            square = phi * phi
            wetting = 1.0 - square
            drive = lapl_phi[v] + phi - square * phi - coupling * conc * wetting * wetting
            change = time_step * mob_ref[x, :, pl.ds(v * LANES, LANES)] * drive
            store(v, phi + change, conc + time_step * lapl_conc[v] + 0.5 * change)

    def sweep(self, first, last, unroll, source, mob_ref, target, shift=None):
        phi_ref, conc_ref = source
        phi_out, conc_out = target

        def one(x):
            def store(v, phi, conc):
                if shift is None:
                    where = (x, slice(None), pl.ds(v * LANES, LANES))
                else:
                    where = (slice(None), pl.ds(pl.multiple_of((x - shift) * FACE + v * LANES, LANES), LANES))
                phi_out[where] = phi
                conc_out[where] = conc

            self.advance(phi_ref, conc_ref, mob_ref, x, store)

        whole = first + (last - first) // unroll * unroll
        if whole > first:

            @pl.loop(0, (whole - first) // unroll)
            def _(i):
                for u in range(unroll):
                    one(first + i * unroll + u)

        for x in range(whole, last):
            one(x)


def place(states, planes, at, *parts):
    for f, ref in enumerate(states):

        @pl.loop(0, planes // 2)
        def _(i):
            for u in range(2):
                x = 2 * i + u
                for v in range(VREGS):
                    value = sum(part[f, :, lanes_at((x + first) * FACE, v)] for part, first in parts)
                    ref[x + at, :, pl.ds(v * LANES, LANES)] = value


REST_AT = HALO + CHUNK_PLANES
TOP_AT = REST_AT + REST


def edge_kernel(
    here_ref, edge_ref, below_ref, above_ref, nbr_ref,
    phase_ref, solute_ref, kept0_ref, kept1_ref, kept2_ref,
    phi0, conc0, mob, phi1, conc1, phi2, conc2,
):
    st = Stencil(here_ref[0], nbr_ref[...])
    states = (phi0, conc0, mob)
    for f, ref in enumerate(states):
        for d in range(2 * CHUNK_PLANES):
            at = HALO + d if d < CHUNK_PLANES else TOP_AT + d - CHUNK_PLANES
            for v in range(VREGS):
                ref[at, :, pl.ds(v * LANES, LANES)] = edge_ref[f, :, pl.ds(d * FACE + v * LANES, LANES)]
        for d in range(HALO):
            for v in range(VREGS):
                lanes = pl.ds(v * LANES, LANES)
                part = pl.ds(d * FACE + v * LANES, LANES)
                mirror_low = ref[2 * HALO - 1 - d, :, lanes]
                ref[d, :, lanes] = jnp.where(st.has_below_x, st.rows(below_ref[f, :, part], st.below_x), mirror_low)
                mirror_high = ref[EDGE + HALO - 1 - d, :, lanes]
                ref[EDGE + HALO + d, :, lanes] = jnp.where(st.has_above_x, st.rows(above_ref[f, :, part], st.above_x), mirror_high)
    for first, last in ((1, REST_AT - 1), (TOP_AT + 1, EXT - 1)):
        st.sweep(first, last, 5, (phi0, conc0), mob, (phi1, conc1))
        st.sweep(first + 1, last - 1, 3, (phi1, conc1), mob, (phi2, conc2))
        st.sweep(first + 2, last - 2, 1, (phi2, conc2), mob, (phase_ref, solute_ref), HALO)
    for f, ref in enumerate(states):
        for n, x in enumerate((*range(REST_AT - 3, REST_AT), *range(TOP_AT, TOP_AT + 3))):
            kept0_ref[f, n] = ref[x]
    for f, ref in enumerate((phi1, conc1)):
        for n, x in enumerate((REST_AT - 3, REST_AT - 2, TOP_AT + 1, TOP_AT + 2)):
            kept1_ref[f, n] = ref[x]
    for f, ref in enumerate((phi2, conc2)):
        for n, x in enumerate((REST_AT - 4, REST_AT - 3, TOP_AT + 2, TOP_AT + 3)):
            kept2_ref[f, n] = ref[x]


BACK = REST_AT - 4
MAIN_PLANES = TOP_AT + 4 - BACK
OUT_FIRST = REST_AT - 3
OUT_PLANES = TOP_AT + 3 - OUT_FIRST
PIECE = 10
PIECES = OUT_PLANES // PIECE


def main_kernel(
    here_ref, stay_ref, far_ref, far_late_ref, back_ref, nbr_ref, kept0_ref, kept1_ref, kept2_ref, _phase_in, _solute_in,
    phase_hbm, solute_hbm,
    phi0, conc0, mob, phi1, conc1, phi2, conc2, phase_ref, solute_ref, sems,
):
    st = Stencil(here_ref[0], nbr_ref[...])
    states = (phi0, conc0, mob)
    first, last = REST_AT - BACK, TOP_AT - BACK
    for f, ref in enumerate(states):
        for n, x in enumerate((*range(first - 3, first), *range(last, last + 3))):
            ref[x] = kept0_ref[f, n]
    for f, ref in enumerate((phi1, conc1)):
        for n, x in enumerate((first - 3, first - 2, last + 1, last + 2)):
            ref[x] = kept1_ref[f, n]
    for f, ref in enumerate((phi2, conc2)):
        for n, x in enumerate((first - 4, first - 3, last + 2, last + 3)):
            ref[x] = kept2_ref[f, n]
    place(states, AHEAD, first, (stay_ref, 0), (far_ref, 2 * CHUNK_PLANES), (back_ref, 0))
    place(states, REST - AHEAD, first + AHEAD, (stay_ref, AHEAD), (far_late_ref, 0), (back_ref, AHEAD))
    st.sweep(first - 1, last + 1, REST + 2, (phi0, conc0), mob, (phi1, conc1))
    st.sweep(first - 2, last + 2, REST + 4, (phi1, conc1), mob, (phi2, conc2))
    start = first - 3
    copies = []
    for piece in range(PIECES):
        at = start + piece * PIECE
        st.sweep(at, at + PIECE, PIECE, (phi2, conc2), mob, (phase_ref, solute_ref), start)
        source = pl.ds(piece * PIECE * FACE, PIECE * FACE)
        target = pl.ds((OUT_FIRST - HALO + piece * PIECE) * FACE, PIECE * FACE)
        for n, (ref, hbm) in enumerate(((phase_ref, phase_hbm), (solute_ref, solute_hbm))):
            copies.append(pltpu.make_async_copy(ref.at[:, source], hbm.at[:, target], sems.at[piece, n]))
            copies[-1].start()
    for copy in copies:
        copy.wait()


SMEM = pl.BlockSpec(memory_space=pltpu.SMEM)
VMEM = pl.BlockSpec(memory_space=pltpu.VMEM)
HBM = pl.BlockSpec(memory_space=pltpu.HBM)
ANY = pl.BlockSpec(memory_space=pl.ANY)
PARAMS = pltpu.CompilerParams(vmem_limit_bytes=32 * 2**20)


def shaped(planes, fields=FIELDS):
    return jax.ShapeDtypeStruct((fields, CAP, planes * FACE), jnp.float32)


def cost(moved, flops=10**6):
    return pl.CostEstimate(flops=flops, bytes_accessed=moved, transcendentals=0)


MB = 2**20


def on_device(old_phase, old_solute, old_mobility, new_global_slot, neighbors):
    count = lax.axis_size("blk")
    here = lax.axis_index("blk").astype(jnp.int32).reshape(1)
    olds = tuple(pltpu.with_memory_space_constraint(x, pltpu.HBM) for x in (old_phase, old_solute, old_mobility))
    devices = range(count)

    def sent(block, route):
        return lax.ppermute(block, "blk", [(p, q) for p, q in route if 0 <= q < count])

    def outward(p):
        return -2 if p % 2 == 0 else 2

    partner = [(p, p ^ 1) for p in devices]
    far_route = [(p, p + outward(p)) for p in devices]
    back_route = [(p, p - outward(p)) for p in devices]

    def after(block, *others):
        return lax.optimization_barrier((block, *others))[0]

    slots_hbm = pltpu.with_memory_space_constraint(new_global_slot, pltpu.HBM)
    old_shape = jax.ShapeDtypeStruct((OLD, CELLS), jnp.float32)
    *olds, merge, final, far_first, far_late = pl.pallas_call(
        pack_kernel,
        in_specs=[SMEM, HBM, HBM, HBM, HBM],
        out_specs=[VMEM] * 7,
        out_shape=[old_shape] * 3 + [shaped(EDGE)] * 2 + [shaped(2 * CHUNK_PLANES + AHEAD), shaped(REST - AHEAD)],
        scratch_shapes=[pltpu.SMEM((OLD,), jnp.int32), pltpu.SemaphoreType.DMA, pltpu.SemaphoreType.DMA((CHUNKS, FIELDS))],
        compiler_params=PARAMS,
        cost_estimate=cost(6 * MB),
        name="pack",
    )(here, slots_hbm, *olds)
    far_first_got = sent(far_first, far_route)
    far_late_got = sent(after(far_late, far_first_got), far_route)
    merge_got = sent(merge, partner)
    final_got = sent(final, partner)

    two_parts = [shaped(2 * CHUNK_PLANES), shaped(REST)]
    back_edge, back_rest = pl.pallas_call(
        relay_kernel,
        in_specs=[SMEM, SMEM] + [VMEM] * 4,
        out_specs=[VMEM] * 2,
        out_shape=two_parts,
        compiler_params=PARAMS,
        cost_estimate=cost(6 * MB),
        name="relay",
    )(here, new_global_slot, *olds, merge_got)
    back_edge_got = sent(back_edge, back_route)

    stay_edge, stay_rest = pl.pallas_call(
        stay_kernel,
        in_specs=[SMEM, SMEM] + [VMEM] * 4,
        out_specs=[VMEM] * 2,
        out_shape=two_parts,
        compiler_params=PARAMS,
        cost_estimate=cost(6 * MB),
        name="stay",
    )(here, new_global_slot, *olds, final_got)
    back_rest_got = sent(after(back_rest, back_edge_got, stay_edge), back_route)

    edges = pl.BlockSpec((FIELDS, CAP, 2 * CHUNK), lambda i: (0, 0, 0))
    faces = pl.BlockSpec((FIELDS, CAP, HALO * FACE), lambda i: (0, 0, 0))
    edge, low, high = pl.pallas_call(
        face_kernel,
        grid=(1,),
        in_specs=[edges] * 3,
        out_specs=[edges, faces, faces],
        out_shape=[shaped(2 * CHUNK_PLANES), shaped(HALO), shaped(HALO)],
        compiler_params=PARAMS,
        cost_estimate=cost(3 * MB),
        name="faces",
    )(stay_edge, far_first_got, back_edge_got)
    below = sent(high, [(p, p + 1) for p in devices])
    above = sent(low, [(p, p - 1) for p in devices])

    state = pltpu.VMEM((EXT, CAP, FACE), jnp.float32)
    whole = jax.ShapeDtypeStruct((CAP, CELLS), jnp.float32)

    def kept(fields, planes):
        return jax.ShapeDtypeStruct((fields, planes, CAP, FACE), jnp.float32)

    phase, solute, kept0, kept1, kept2 = pl.pallas_call(
        edge_kernel,
        in_specs=[SMEM] + [VMEM] * 4,
        out_specs=[VMEM] * 5,
        out_shape=[whole, whole, kept(3, 6), kept(2, 4), kept(2, 4)],
        scratch_shapes=[state] * 7,
        compiler_params=PARAMS,
        cost_estimate=cost(8 * MB),
        name="edge_steps",
    )(here, edge, below, above, neighbors)

    state = pltpu.VMEM((MAIN_PLANES, CAP, FACE), jnp.float32)
    rows_out = pltpu.VMEM((CAP, OUT_PLANES * FACE), jnp.float32)
    phase, solute = pl.pallas_call(
        main_kernel,
        in_specs=[SMEM] + [VMEM] * 8 + [HBM] * 2,
        out_specs=[HBM] * 2,
        out_shape=[whole, whole],
        scratch_shapes=[state] * 7 + [rows_out] * 2 + [pltpu.SemaphoreType.DMA((PIECES, 2))],
        input_output_aliases={9: 0, 10: 1},
        compiler_params=PARAMS,
        cost_estimate=cost(20 * MB),
        name="main_steps",
    )(here, stay_rest, far_first_got, far_late_got, back_rest_got, neighbors, kept0, kept1, kept2, phase, solute)
    return phase, solute


def solution(mesh):
    placed = (P("blk", None), P("blk", None), P("blk", None), P("blk"), P("blk", None))
    return jax.shard_map(
        on_device,
        mesh=mesh,
        in_specs=placed,
        out_specs=(P("blk", None), P("blk", None)),
        check_vma=False,
    )
```

```python
import functools

import jax
import jax.numpy as jnp
from jax import lax
from jax.experimental import pallas as pl
from jax.experimental.pallas import tpu as pltpu
from jax.sharding import PartitionSpec as P

EDGE = 32
FACE = EDGE * EDGE
CELLS = EDGE * FACE
CAP = 8
OLD = 16
FIELDS = 3
HALO = 3
CHUNK_PLANES = 4
CHUNK = CHUNK_PLANES * FACE
CHUNKS = EDGE // CHUNK_PLANES
LANES = 128
EXT = EDGE + 2 * HALO
REST = EDGE - 2 * CHUNK_PLANES
VREGS = FACE // LANES

time_step = 0.15
coupling = 1.5


def windows(slot_ref, here):
    first = slot_ref[0]
    count = jnp.int32(0)
    for i in range(OLD):
        count += (slot_ref[i] >= 0).astype(jnp.int32)
    amount = jnp.bitwise_and(first, CAP - 1)
    row = lax.broadcasted_iota(jnp.int32, (CAP, LANES), 0)

    def masks(k):
        index = row + ((here + k) * CAP - first)
        low = (index >= 0) & (index < CAP) & (index < count)
        high = (index >= CAP) & (index < count)
        return low, high

    return amount, masks


def picked(masks, low_rows, high_rows):
    low, high = masks
    return jnp.where(low, low_rows, jnp.where(high, high_rows, 0.0))


def side_of(here):
    return jnp.where(jnp.bitwise_and(here, 1) == 0, -1, 1)


def aligned(ref, lanes, amount):
    return pltpu.roll(ref[0:CAP, lanes], amount, 0), pltpu.roll(ref[CAP:OLD, lanes], amount, 0)


def chunk_at(i):
    return jnp.where(i == 0, 0, jnp.where(i == 1, CHUNKS - 1, i - 1))


def lanes_at(start, v):
    return pl.ds(pl.multiple_of(start + v * LANES, LANES), LANES)


def pack_kernel(
    here_ref, slot_hbm, phi_hbm, conc_hbm, mob_hbm,
    phi_ref, conc_ref, mob_ref, merge_ref, final_ref, far_ref,
    slot_ref, slot_sem, sems,
):
    olds = tuple(zip((phi_hbm, conc_hbm, mob_hbm), (phi_ref, conc_ref, mob_ref)))

    def copies(i):
        lanes = pl.ds(pl.multiple_of(chunk_at(i) * CHUNK, CHUNK), CHUNK)
        return [pltpu.make_async_copy(hbm.at[:, lanes], ref.at[:, lanes], sems.at[i, f]) for f, (hbm, ref) in enumerate(olds)]

    slot_copy = pltpu.make_async_copy(slot_hbm, slot_ref, slot_sem)
    slot_copy.start()

    @pl.loop(0, CHUNKS)
    def _(i):
        for copy in copies(i):
            copy.start()

    slot_copy.wait()
    here = here_ref[0]
    side = side_of(here)
    amount, masks = windows(slot_ref, here)
    far, merge, final = masks(2 * side), masks(side), masks(-side)

    def fill(i):
        start = chunk_at(i) * CHUNK
        for f, (_, ref) in enumerate(olds):
            for v in range(CHUNK // LANES):
                lanes = lanes_at(start, v)
                rows = aligned(ref, lanes, amount)
                merge_ref[f, :, lanes] = picked(merge, *rows)
                final_ref[f, :, lanes] = picked(final, *rows)
                far_ref[f, :, lanes_at(i * CHUNK, v)] = picked(far, *rows)

    @pl.loop(0, CHUNKS)
    def _(i):
        for copy in copies(i):
            copy.wait()
        fill(i)


def add_rows(masks, amount, old_refs, add_ref, edge_ref, rest_ref):
    for out_ref, out_plane, plane, count in (
        (edge_ref, 0, 0, CHUNK_PLANES),
        (edge_ref, CHUNK_PLANES, CHUNK_PLANES + REST, CHUNK_PLANES),
        (rest_ref, 0, CHUNK_PLANES, REST),
    ):

        @pl.loop(0, count // 2)
        def _(i):
            for f, ref in enumerate(old_refs):
                for v in range(2 * VREGS):
                    lanes = lanes_at((plane + 2 * i) * FACE, v)
                    value = picked(masks, *aligned(ref, lanes, amount)) + add_ref[f, :, lanes]
                    out_ref[f, :, lanes_at((out_plane + 2 * i) * FACE, v)] = value


def relay_kernel(here_ref, slot_ref, phi_ref, conc_ref, mob_ref, merge_ref, *part_refs):
    here = here_ref[0]
    amount, masks = windows(slot_ref, here)
    add_rows(masks(-2 * side_of(here)), amount, (phi_ref, conc_ref, mob_ref), merge_ref, *part_refs)


def stay_kernel(here_ref, slot_ref, phi_ref, conc_ref, mob_ref, final_ref, *part_refs):
    here = here_ref[0]
    amount, masks = windows(slot_ref, here)
    add_rows(masks(0), amount, (phi_ref, conc_ref, mob_ref), final_ref, *part_refs)


LOW_PLANES = {(f, d): n for n, (f, d) in enumerate((f, d) for f in range(FIELDS) for d in range(HALO) if f < 2 or d < HALO - 1)}
HIGH_PLANES = {(f, d): n for n, (f, d) in enumerate((f, d) for f in range(FIELDS) for d in range(HALO) if f < 2 or d > 0)}


def face_kernel(stay_ref, far_ref, back_ref, edge_ref, low_ref, high_ref):
    first_high = (2 * CHUNK_PLANES - HALO) * FACE
    for f in range(FIELDS):
        for v in range(2 * CHUNK_PLANES * VREGS):
            lanes = pl.ds(v * LANES, LANES)
            value = stay_ref[f, :, lanes] + far_ref[f, :, lanes] + back_ref[f, :, lanes]
            edge_ref[f, :, lanes] = value
            at = v * LANES
            part = pl.ds(at % FACE, LANES)
            if (f, at // FACE) in LOW_PLANES:
                low_ref[LOW_PLANES[f, at // FACE], :, part] = value
            if (f, (at - first_high) // FACE) in HIGH_PLANES:
                high_ref[HIGH_PLANES[f, (at - first_high) // FACE], :, part] = value


class Stencil:
    def __init__(self, here, nbr):
        base = here * CAP
        self.nbr = nbr
        lane = lax.broadcasted_iota(jnp.int32, (CAP, LANES), 1)
        z = jnp.bitwise_and(lane, EDGE - 1)
        self.z_first, self.z_last = z == 0, z == EDGE - 1
        self.y_first, self.y_last = lane < EDGE, lane >= LANES - EDGE
        self.below_x, self.has_below_x = self.column(0, base - CAP)
        self.above_x, self.has_above_x = self.column(1, base + CAP)
        self.below_y, self.has_below_y = self.column(2, base)
        self.above_y, self.has_above_y = self.column(3, base)
        self.below_z, _ = self.column(4, base)
        self.above_z, _ = self.column(5, base)

    def column(self, c, start):
        wide = jnp.broadcast_to(self.nbr[:, c : c + 1], (CAP, LANES))
        valid = wide >= 0
        return jnp.where(valid, wide - start, 0), valid

    @staticmethod
    def rows(x, index):
        return jnp.take_along_axis(x, index, axis=0, mode="promise_in_bounds")

    def laplacian(self, ref, x):
        centre = [ref[x, :, pl.ds(v * LANES, LANES)] for v in range(VREGS)]
        lower = [pltpu.roll(c, EDGE, 1) for c in centre]
        upper = [pltpu.roll(c, LANES - EDGE, 1) for c in centre]
        out = []
        for v in range(VREGS):
            c = centre[v]
            lanes = pl.ds(v * LANES, LANES)
            if v:
                from_lower = lower[v - 1]
            else:
                from_lower = jnp.where(self.has_below_y, self.rows(lower[-1], self.below_y), c)
            if v < VREGS - 1:
                from_upper = upper[v + 1]
            else:
                from_upper = jnp.where(self.has_above_y, self.rows(upper[0], self.above_y), c)
            prev_y = jnp.where(self.y_first, from_lower, lower[v])
            next_y = jnp.where(self.y_last, from_upper, upper[v])
            prev_z = jnp.where(self.z_first, pltpu.roll(self.rows(c, self.below_z), LANES - EDGE + 1, 1), pltpu.roll(c, 1, 1))
            next_z = jnp.where(self.z_last, pltpu.roll(self.rows(c, self.above_z), EDGE - 1, 1), pltpu.roll(c, LANES - 1, 1))
            total = (ref[x - 1, :, lanes] + ref[x + 1, :, lanes]) + (prev_y + next_y) + (prev_z + next_z)
            out.append(total - 6.0 * c)
        return out, centre

    def advance(self, phi_ref, conc_ref, mob_ref, x, store):
        lapl_phi, phis = self.laplacian(phi_ref, x)
        lapl_conc, concs = self.laplacian(conc_ref, x)
        for v in range(VREGS):
            phi, conc = phis[v], concs[v]
            square = phi * phi
            wetting = 1.0 - square
            drive = lapl_phi[v] + phi - square * phi - coupling * conc * wetting * wetting
            change = time_step * mob_ref[x, :, pl.ds(v * LANES, LANES)] * drive
            store(v, phi + change, conc + time_step * lapl_conc[v] + 0.5 * change)

    def sweep(self, first, last, unroll, source, mob_ref, target, shift=None):
        phi_ref, conc_ref = source
        phi_out, conc_out = target

        def one(x):
            def store(v, phi, conc):
                if shift is None:
                    where = (x, slice(None), pl.ds(v * LANES, LANES))
                else:
                    where = (slice(None), pl.ds(pl.multiple_of((x - shift) * FACE + v * LANES, LANES), LANES))
                phi_out[where] = phi
                conc_out[where] = conc

            self.advance(phi_ref, conc_ref, mob_ref, x, store)

        whole = first + (last - first) // unroll * unroll
        if whole > first:

            @pl.loop(0, (whole - first) // unroll)
            def _(i):
                for u in range(unroll):
                    one(first + i * unroll + u)

        for x in range(whole, last):
            one(x)


def place(states, planes, at, *parts):
    for f, ref in enumerate(states):

        @pl.loop(0, planes // 2)
        def _(i):
            for u in range(2):
                x = 2 * i + u
                for v in range(VREGS):
                    value = sum(part[f, :, lanes_at((x + first) * FACE, v)] for part, first in parts)
                    ref[x + at, :, pl.ds(v * LANES, LANES)] = value


REST_AT = HALO + CHUNK_PLANES
TOP_AT = REST_AT + REST


def edge_kernel(
    here_ref, edge_ref, below_ref, above_ref, nbr_ref,
    phase_ref, solute_ref, kept0_ref, kept1_ref, kept2_ref,
    phi0, conc0, mob, phi1, conc1, phi2, conc2,
):
    st = Stencil(here_ref[0], nbr_ref[...])
    states = (phi0, conc0, mob)
    for f, ref in enumerate(states):
        for d in range(2 * CHUNK_PLANES):
            at = HALO + d if d < CHUNK_PLANES else TOP_AT + d - CHUNK_PLANES
            for v in range(VREGS):
                ref[at, :, pl.ds(v * LANES, LANES)] = edge_ref[f, :, pl.ds(d * FACE + v * LANES, LANES)]
        for d in range(HALO):
            for v in range(VREGS):
                lanes = pl.ds(v * LANES, LANES)
                if (f, d) in HIGH_PLANES:
                    mirror = ref[2 * HALO - 1 - d, :, lanes]
                    taken = st.rows(below_ref[HIGH_PLANES[f, d], :, lanes], st.below_x)
                    ref[d, :, lanes] = jnp.where(st.has_below_x, taken, mirror)
                if (f, d) in LOW_PLANES:
                    mirror = ref[EDGE + HALO - 1 - d, :, lanes]
                    taken = st.rows(above_ref[LOW_PLANES[f, d], :, lanes], st.above_x)
                    ref[EDGE + HALO + d, :, lanes] = jnp.where(st.has_above_x, taken, mirror)
    for first, last in ((1, REST_AT - 1), (TOP_AT + 1, EXT - 1)):
        st.sweep(first, last, 5, (phi0, conc0), mob, (phi1, conc1))
        st.sweep(first + 1, last - 1, 3, (phi1, conc1), mob, (phi2, conc2))
        st.sweep(first + 2, last - 2, 1, (phi2, conc2), mob, (phase_ref, solute_ref), HALO)
    for f, ref in enumerate(states):
        for n, x in enumerate((*range(REST_AT - 3, REST_AT), *range(TOP_AT, TOP_AT + 3))):
            kept0_ref[f, n] = ref[x]
    for f, ref in enumerate((phi1, conc1)):
        for n, x in enumerate((REST_AT - 3, REST_AT - 2, TOP_AT + 1, TOP_AT + 2)):
            kept1_ref[f, n] = ref[x]
    for f, ref in enumerate((phi2, conc2)):
        for n, x in enumerate((REST_AT - 4, REST_AT - 3, TOP_AT + 2, TOP_AT + 3)):
            kept2_ref[f, n] = ref[x]


BACK = REST_AT - 4
MAIN_PLANES = TOP_AT + 4 - BACK
OUT_FIRST = REST_AT - 3
OUT_PLANES = TOP_AT + 3 - OUT_FIRST
PIECE = 10
PIECES = OUT_PLANES // PIECE


def main_kernel(
    here_ref, stay_ref, far_ref, back_ref, nbr_ref, kept0_ref, kept1_ref, kept2_ref, _phase_in, _solute_in,
    phase_hbm, solute_hbm,
    phi0, conc0, mob, phi1, conc1, phi2, conc2, phase_ref, solute_ref, sems,
):
    st = Stencil(here_ref[0], nbr_ref[...])
    states = (phi0, conc0, mob)
    first, last = REST_AT - BACK, TOP_AT - BACK
    for f, ref in enumerate(states):
        for n, x in enumerate((*range(first - 3, first), *range(last, last + 3))):
            ref[x] = kept0_ref[f, n]
    for f, ref in enumerate((phi1, conc1)):
        for n, x in enumerate((first - 3, first - 2, last + 1, last + 2)):
            ref[x] = kept1_ref[f, n]
    for f, ref in enumerate((phi2, conc2)):
        for n, x in enumerate((first - 4, first - 3, last + 2, last + 3)):
            ref[x] = kept2_ref[f, n]
    place(states, REST, first, (stay_ref, 0), (far_ref, 2 * CHUNK_PLANES), (back_ref, 0))
    st.sweep(first - 1, last + 1, REST + 2, (phi0, conc0), mob, (phi1, conc1))
    st.sweep(first - 2, last + 2, REST + 4, (phi1, conc1), mob, (phi2, conc2))
    start = first - 3
    copies = []
    for piece in range(PIECES):
        at = start + piece * PIECE
        st.sweep(at, at + PIECE, PIECE, (phi2, conc2), mob, (phase_ref, solute_ref), start)
        source = pl.ds(piece * PIECE * FACE, PIECE * FACE)
        target = pl.ds((OUT_FIRST - HALO + piece * PIECE) * FACE, PIECE * FACE)
        for n, (ref, hbm) in enumerate(((phase_ref, phase_hbm), (solute_ref, solute_hbm))):
            copies.append(pltpu.make_async_copy(ref.at[:, source], hbm.at[:, target], sems.at[piece, n]))
            copies[-1].start()
    for copy in copies:
        copy.wait()


SMEM = pl.BlockSpec(memory_space=pltpu.SMEM)
VMEM = pl.BlockSpec(memory_space=pltpu.VMEM)
HBM = pl.BlockSpec(memory_space=pltpu.HBM)
ANY = pl.BlockSpec(memory_space=pl.ANY)
PARAMS = pltpu.CompilerParams(vmem_limit_bytes=32 * 2**20)


def shaped(planes, fields=FIELDS):
    return jax.ShapeDtypeStruct((fields, CAP, planes * FACE), jnp.float32)


def cost(moved, flops=10**6):
    return pl.CostEstimate(flops=flops, bytes_accessed=moved, transcendentals=0)


MB = 2**20


def on_device(old_phase, old_solute, old_mobility, new_global_slot, neighbors):
    count = lax.axis_size("blk")
    here = lax.axis_index("blk").astype(jnp.int32).reshape(1)
    olds = tuple(pltpu.with_memory_space_constraint(x, pltpu.HBM) for x in (old_phase, old_solute, old_mobility))
    devices = range(count)

    def sent(block, route):
        return lax.ppermute(block, "blk", [(p, q) for p, q in route if 0 <= q < count])

    def outward(p):
        return -2 if p % 2 == 0 else 2

    partner = [(p, p ^ 1) for p in devices]
    far_route = [(p, p + outward(p)) for p in devices]
    back_route = [(p, p - outward(p)) for p in devices]

    def after(block, *others):
        return lax.optimization_barrier((block, *others))[0]

    slots_hbm = pltpu.with_memory_space_constraint(new_global_slot, pltpu.HBM)
    old_shape = jax.ShapeDtypeStruct((OLD, CELLS), jnp.float32)
    *olds, merge, final, far_all = pl.pallas_call(
        pack_kernel,
        in_specs=[SMEM, HBM, HBM, HBM, HBM],
        out_specs=[VMEM] * 6,
        out_shape=[old_shape] * 3 + [shaped(EDGE)] * 3,
        scratch_shapes=[pltpu.SMEM((OLD,), jnp.int32), pltpu.SemaphoreType.DMA, pltpu.SemaphoreType.DMA((CHUNKS, FIELDS))],
        compiler_params=PARAMS,
        cost_estimate=cost(6 * MB),
        name="pack",
    )(here, slots_hbm, *olds)
    far_got = sent(far_all, far_route)
    merge_got = sent(merge, partner)
    final_got = sent(final, partner)

    two_parts = [shaped(2 * CHUNK_PLANES), shaped(REST)]
    back_edge, back_rest = pl.pallas_call(
        relay_kernel,
        in_specs=[SMEM, SMEM] + [VMEM] * 4,
        out_specs=[VMEM] * 2,
        out_shape=two_parts,
        compiler_params=PARAMS,
        cost_estimate=cost(6 * MB),
        name="relay",
    )(here, new_global_slot, *olds, merge_got)
    back_edge_got = sent(back_edge, back_route)

    stay_edge, stay_rest = pl.pallas_call(
        stay_kernel,
        in_specs=[SMEM, SMEM] + [VMEM] * 4,
        out_specs=[VMEM] * 2,
        out_shape=two_parts,
        compiler_params=PARAMS,
        cost_estimate=cost(6 * MB),
        name="stay",
    )(here, new_global_slot, *olds, final_got)
    back_rest_got = sent(after(back_rest, back_edge_got, stay_edge), back_route)

    edges = pl.BlockSpec((FIELDS, CAP, 2 * CHUNK), lambda i: (0, 0, 0))
    faces = pl.BlockSpec((len(LOW_PLANES), CAP, FACE), lambda i: (0, 0, 0))
    edge, low, high = pl.pallas_call(
        face_kernel,
        grid=(1,),
        in_specs=[edges] * 3,
        out_specs=[edges, faces, faces],
        out_shape=[shaped(2 * CHUNK_PLANES)] + [shaped(1, len(LOW_PLANES))] * 2,
        compiler_params=PARAMS,
        cost_estimate=cost(3 * MB),
        name="faces",
    )(stay_edge, far_got, back_edge_got)
    below = sent(high, [(p, p + 1) for p in devices])
    above = sent(low, [(p, p - 1) for p in devices])

    state = pltpu.VMEM((EXT, CAP, FACE), jnp.float32)
    whole = jax.ShapeDtypeStruct((CAP, CELLS), jnp.float32)

    def kept(fields, planes):
        return jax.ShapeDtypeStruct((fields, planes, CAP, FACE), jnp.float32)

    phase, solute, kept0, kept1, kept2 = pl.pallas_call(
        edge_kernel,
        in_specs=[SMEM] + [VMEM] * 4,
        out_specs=[VMEM] * 5,
        out_shape=[whole, whole, kept(3, 6), kept(2, 4), kept(2, 4)],
        scratch_shapes=[state] * 7,
        compiler_params=PARAMS,
        cost_estimate=cost(8 * MB),
        name="edge_steps",
    )(here, edge, below, above, neighbors)

    state = pltpu.VMEM((MAIN_PLANES, CAP, FACE), jnp.float32)
    rows_out = pltpu.VMEM((CAP, OUT_PLANES * FACE), jnp.float32)
    phase, solute = pl.pallas_call(
        main_kernel,
        in_specs=[SMEM] + [VMEM] * 7 + [HBM] * 2,
        out_specs=[HBM] * 2,
        out_shape=[whole, whole],
        scratch_shapes=[state] * 7 + [rows_out] * 2 + [pltpu.SemaphoreType.DMA((PIECES, 2))],
        input_output_aliases={8: 0, 9: 1},
        compiler_params=PARAMS,
        cost_estimate=cost(20 * MB),
        name="main_steps",
    )(here, stay_rest, far_got, back_rest_got, neighbors, kept0, kept1, kept2, phase, solute)
    return phase, solute


def solution(mesh):
    placed = (P("blk", None), P("blk", None), P("blk", None), P("blk"), P("blk", None))
    return jax.shard_map(
        on_device,
        mesh=mesh,
        in_specs=placed,
        out_specs=(P("blk", None), P("blk", None)),
        check_vma=False,
    )
```

```python
import functools

import jax
import jax.numpy as jnp
from jax import lax
from jax.experimental import pallas as pl
from jax.experimental.pallas import tpu as pltpu
from jax.sharding import PartitionSpec as P

EDGE = 32
FACE = EDGE * EDGE
CELLS = EDGE * FACE
CAP = 8
OLD = 16
FIELDS = 3
HALO = 3
CHUNK_PLANES = 4
CHUNK = CHUNK_PLANES * FACE
CHUNKS = EDGE // CHUNK_PLANES
LANES = 128
EXT = EDGE + 2 * HALO
REST = EDGE - 2 * CHUNK_PLANES
VREGS = FACE // LANES

time_step = 0.15
coupling = 1.5


def windows(slot_ref, here):
    first = slot_ref[0]
    count = jnp.int32(0)
    for i in range(OLD):
        count += (slot_ref[i] >= 0).astype(jnp.int32)
    amount = jnp.bitwise_and(first, CAP - 1)
    row = lax.broadcasted_iota(jnp.int32, (CAP, LANES), 0)

    def masks(k):
        index = row + ((here + k) * CAP - first)
        low = (index >= 0) & (index < CAP) & (index < count)
        high = (index >= CAP) & (index < count)
        return low, high

    return amount, masks


def picked(masks, low_rows, high_rows):
    low, high = masks
    return jnp.where(low, low_rows, jnp.where(high, high_rows, 0.0))


def side_of(here):
    return jnp.where(jnp.bitwise_and(here, 1) == 0, -1, 1)


def aligned(ref, lanes, amount):
    return pltpu.roll(ref[0:CAP, lanes], amount, 0), pltpu.roll(ref[CAP:OLD, lanes], amount, 0)


def chunk_at(i):
    return jnp.where(i == 0, 0, jnp.where(i == 1, CHUNKS - 1, i - 1))


def lanes_at(start, v):
    return pl.ds(pl.multiple_of(start + v * LANES, LANES), LANES)


def pack_kernel(
    here_ref, slot_hbm, phi_hbm, conc_hbm, mob_hbm,
    phi_ref, conc_ref, mob_ref, merge_ref, final_ref, far_ref,
    slot_ref, slot_sem, sems,
):
    olds = tuple(zip((phi_hbm, conc_hbm, mob_hbm), (phi_ref, conc_ref, mob_ref)))

    def copies(i):
        lanes = pl.ds(pl.multiple_of(chunk_at(i) * CHUNK, CHUNK), CHUNK)
        return [pltpu.make_async_copy(hbm.at[:, lanes], ref.at[:, lanes], sems.at[i, f]) for f, (hbm, ref) in enumerate(olds)]

    slot_copy = pltpu.make_async_copy(slot_hbm, slot_ref, slot_sem)
    slot_copy.start()

    @pl.loop(0, CHUNKS)
    def _(i):
        for copy in copies(i):
            copy.start()

    slot_copy.wait()
    here = here_ref[0]
    side = side_of(here)
    amount, masks = windows(slot_ref, here)
    far, merge, final = masks(2 * side), masks(side), masks(-side)

    def fill(i):
        start = chunk_at(i) * CHUNK
        for f, (_, ref) in enumerate(olds):
            for v in range(CHUNK // LANES):
                lanes = lanes_at(start, v)
                rows = aligned(ref, lanes, amount)
                merge_ref[f, :, lanes] = picked(merge, *rows)
                final_ref[f, :, lanes] = picked(final, *rows)
                far_ref[f, :, lanes_at(i * CHUNK, v)] = picked(far, *rows)

    @pl.loop(0, CHUNKS)
    def _(i):
        for copy in copies(i):
            copy.wait()
        fill(i)


def add_rows(masks, amount, old_refs, add_ref, edge_ref, rest_ref):
    for out_ref, out_plane, plane, count in (
        (edge_ref, 0, 0, CHUNK_PLANES),
        (edge_ref, CHUNK_PLANES, CHUNK_PLANES + REST, CHUNK_PLANES),
        (rest_ref, 0, CHUNK_PLANES, REST),
    ):

        @pl.loop(0, count // 2)
        def _(i):
            for f, ref in enumerate(old_refs):
                for v in range(2 * VREGS):
                    lanes = lanes_at((plane + 2 * i) * FACE, v)
                    value = picked(masks, *aligned(ref, lanes, amount)) + add_ref[f, :, lanes]
                    out_ref[f, :, lanes_at((out_plane + 2 * i) * FACE, v)] = value


def relay_kernel(here_ref, slot_ref, phi_ref, conc_ref, mob_ref, merge_ref, *part_refs):
    here = here_ref[0]
    amount, masks = windows(slot_ref, here)
    add_rows(masks(-2 * side_of(here)), amount, (phi_ref, conc_ref, mob_ref), merge_ref, *part_refs)


def stay_kernel(here_ref, slot_ref, phi_ref, conc_ref, mob_ref, final_ref, *part_refs):
    here = here_ref[0]
    amount, masks = windows(slot_ref, here)
    add_rows(masks(0), amount, (phi_ref, conc_ref, mob_ref), final_ref, *part_refs)


LOW_PLANES = {(f, d): n for n, (f, d) in enumerate((f, d) for f in range(FIELDS) for d in range(HALO) if f < 2 or d < HALO - 1)}
HIGH_PLANES = {(f, d): n for n, (f, d) in enumerate((f, d) for f in range(FIELDS) for d in range(HALO) if f < 2 or d > 0)}


def face_kernel(stay_ref, far_ref, back_ref, edge_ref, low_ref, high_ref):
    first_high = (2 * CHUNK_PLANES - HALO) * FACE
    for f in range(FIELDS):
        for v in range(2 * CHUNK_PLANES * VREGS):
            lanes = pl.ds(v * LANES, LANES)
            value = stay_ref[f, :, lanes] + far_ref[f, :, lanes] + back_ref[f, :, lanes]
            edge_ref[f, :, lanes] = value
            at = v * LANES
            part = pl.ds(at % FACE, LANES)
            if (f, at // FACE) in LOW_PLANES:
                low_ref[LOW_PLANES[f, at // FACE], :, part] = value
            if (f, (at - first_high) // FACE) in HIGH_PLANES:
                high_ref[HIGH_PLANES[f, (at - first_high) // FACE], :, part] = value


class Stencil:
    def __init__(self, here, nbr):
        base = here * CAP
        self.nbr = nbr
        lane = lax.broadcasted_iota(jnp.int32, (CAP, LANES), 1)
        z = jnp.bitwise_and(lane, EDGE - 1)
        self.z_first, self.z_last = z == 0, z == EDGE - 1
        self.y_first, self.y_last = lane < EDGE, lane >= LANES - EDGE
        self.below_x, self.has_below_x = self.column(0, base - CAP)
        self.above_x, self.has_above_x = self.column(1, base + CAP)
        self.below_y, self.has_below_y = self.column(2, base)
        self.above_y, self.has_above_y = self.column(3, base)
        self.below_z, _ = self.column(4, base)
        self.above_z, _ = self.column(5, base)

    def column(self, c, start):
        wide = jnp.broadcast_to(self.nbr[:, c : c + 1], (CAP, LANES))
        valid = wide >= 0
        return jnp.where(valid, wide - start, 0), valid

    @staticmethod
    def rows(x, index):
        return jnp.take_along_axis(x, index, axis=0, mode="promise_in_bounds")

    def laplacian(self, ref, x):
        centre = [ref[x, :, pl.ds(v * LANES, LANES)] for v in range(VREGS)]
        lower = [pltpu.roll(c, EDGE, 1) for c in centre]
        upper = [pltpu.roll(c, LANES - EDGE, 1) for c in centre]
        out = []
        for v in range(VREGS):
            c = centre[v]
            lanes = pl.ds(v * LANES, LANES)
            if v:
                from_lower = lower[v - 1]
            else:
                from_lower = jnp.where(self.has_below_y, self.rows(lower[-1], self.below_y), c)
            if v < VREGS - 1:
                from_upper = upper[v + 1]
            else:
                from_upper = jnp.where(self.has_above_y, self.rows(upper[0], self.above_y), c)
            prev_y = jnp.where(self.y_first, from_lower, lower[v])
            next_y = jnp.where(self.y_last, from_upper, upper[v])
            prev_z = jnp.where(self.z_first, pltpu.roll(self.rows(c, self.below_z), LANES - EDGE + 1, 1), pltpu.roll(c, 1, 1))
            next_z = jnp.where(self.z_last, pltpu.roll(self.rows(c, self.above_z), EDGE - 1, 1), pltpu.roll(c, LANES - 1, 1))
            total = (ref[x - 1, :, lanes] + ref[x + 1, :, lanes]) + (prev_y + next_y) + (prev_z + next_z)
            out.append(total - 6.0 * c)
        return out, centre

    def advance(self, phi_ref, conc_ref, mob_ref, x, store):
        lapl_phi, phis = self.laplacian(phi_ref, x)
        lapl_conc, concs = self.laplacian(conc_ref, x)
        for v in range(VREGS):
            phi, conc = phis[v], concs[v]
            square = phi * phi
            wetting = 1.0 - square
            drive = lapl_phi[v] + phi - square * phi - coupling * conc * wetting * wetting
            change = time_step * mob_ref[x, :, pl.ds(v * LANES, LANES)] * drive
            store(v, phi + change, conc + time_step * lapl_conc[v] + 0.5 * change)

    def sweep(self, first, last, unroll, source, mob_ref, target, shift=None):
        phi_ref, conc_ref = source
        phi_out, conc_out = target

        def one(x):
            def store(v, phi, conc):
                if shift is None:
                    where = (x, slice(None), pl.ds(v * LANES, LANES))
                else:
                    where = (slice(None), pl.ds(pl.multiple_of((x - shift) * FACE + v * LANES, LANES), LANES))
                phi_out[where] = phi
                conc_out[where] = conc

            self.advance(phi_ref, conc_ref, mob_ref, x, store)

        whole = first + (last - first) // unroll * unroll
        if whole > first:

            @pl.loop(0, (whole - first) // unroll)
            def _(i):
                for u in range(unroll):
                    one(first + i * unroll + u)

        for x in range(whole, last):
            one(x)


def place(states, planes, at, *parts):
    for f, ref in enumerate(states):

        @pl.loop(0, planes // 2)
        def _(i):
            for u in range(2):
                x = 2 * i + u
                for v in range(VREGS):
                    value = sum(part[f, :, lanes_at((x + first) * FACE, v)] for part, first in parts)
                    ref[x + at, :, pl.ds(v * LANES, LANES)] = value


REST_AT = HALO + CHUNK_PLANES
TOP_AT = REST_AT + REST


def edge_kernel(
    here_ref, edge_ref, below_ref, above_ref, nbr_ref,
    phase_hbm, solute_hbm, kept0_ref, kept1_ref, kept2_ref,
    phi0, conc0, mob, phi1, conc1, phi2, conc2, phase_ref, solute_ref, sems,
):
    st = Stencil(here_ref[0], nbr_ref[...])
    states = (phi0, conc0, mob)
    for f, ref in enumerate(states):
        for d in range(2 * CHUNK_PLANES):
            at = HALO + d if d < CHUNK_PLANES else TOP_AT + d - CHUNK_PLANES
            for v in range(VREGS):
                ref[at, :, pl.ds(v * LANES, LANES)] = edge_ref[f, :, pl.ds(d * FACE + v * LANES, LANES)]
        for d in range(HALO):
            for v in range(VREGS):
                lanes = pl.ds(v * LANES, LANES)
                if (f, d) in HIGH_PLANES:
                    mirror = ref[2 * HALO - 1 - d, :, lanes]
                    taken = st.rows(below_ref[HIGH_PLANES[f, d], :, lanes], st.below_x)
                    ref[d, :, lanes] = jnp.where(st.has_below_x, taken, mirror)
                if (f, d) in LOW_PLANES:
                    mirror = ref[EDGE + HALO - 1 - d, :, lanes]
                    taken = st.rows(above_ref[LOW_PLANES[f, d], :, lanes], st.above_x)
                    ref[EDGE + HALO + d, :, lanes] = jnp.where(st.has_above_x, taken, mirror)
    copies = []
    for n, (first, last) in enumerate(((1, REST_AT - 1), (TOP_AT + 1, EXT - 1))):
        st.sweep(first, last, 5, (phi0, conc0), mob, (phi1, conc1))
        st.sweep(first + 1, last - 1, 3, (phi1, conc1), mob, (phi2, conc2))
        st.sweep(first + 2, last - 2, 1, (phi2, conc2), mob, (phase_ref, solute_ref), first + 2 - n)
        source, target = pl.ds(n * FACE, FACE), pl.ds(n * (EDGE - 1) * FACE, FACE)
        for k, (ref, hbm) in enumerate(((phase_ref, phase_hbm), (solute_ref, solute_hbm))):
            copies.append(pltpu.make_async_copy(ref.at[:, source], hbm.at[:, target], sems.at[n, k]))
            copies[-1].start()
    for f, ref in enumerate(states):
        for n, x in enumerate((*range(REST_AT - 3, REST_AT), *range(TOP_AT, TOP_AT + 3))):
            kept0_ref[f, n] = ref[x]
    for f, ref in enumerate((phi1, conc1)):
        for n, x in enumerate((REST_AT - 3, REST_AT - 2, TOP_AT + 1, TOP_AT + 2)):
            kept1_ref[f, n] = ref[x]
    for f, ref in enumerate((phi2, conc2)):
        for n, x in enumerate((REST_AT - 4, REST_AT - 3, TOP_AT + 2, TOP_AT + 3)):
            kept2_ref[f, n] = ref[x]
    for copy in copies:
        copy.wait()


BACK = REST_AT - 4
MAIN_PLANES = TOP_AT + 4 - BACK
OUT_FIRST = REST_AT - 3
OUT_PLANES = TOP_AT + 3 - OUT_FIRST
PIECE = 10
PIECES = OUT_PLANES // PIECE


def main_kernel(
    here_ref, stay_ref, far_ref, back_ref, nbr_ref, kept0_ref, kept1_ref, kept2_ref, _phase_in, _solute_in,
    phase_hbm, solute_hbm,
    phi0, conc0, mob, phi1, conc1, phi2, conc2, phase_ref, solute_ref, sems,
):
    st = Stencil(here_ref[0], nbr_ref[...])
    states = (phi0, conc0, mob)
    first, last = REST_AT - BACK, TOP_AT - BACK
    for f, ref in enumerate(states):
        for n, x in enumerate((*range(first - 3, first), *range(last, last + 3))):
            ref[x] = kept0_ref[f, n]
    for f, ref in enumerate((phi1, conc1)):
        for n, x in enumerate((first - 3, first - 2, last + 1, last + 2)):
            ref[x] = kept1_ref[f, n]
    for f, ref in enumerate((phi2, conc2)):
        for n, x in enumerate((first - 4, first - 3, last + 2, last + 3)):
            ref[x] = kept2_ref[f, n]
    place(states, REST, first, (stay_ref, 0), (far_ref, 2 * CHUNK_PLANES), (back_ref, 0))
    st.sweep(first - 1, last + 1, REST + 2, (phi0, conc0), mob, (phi1, conc1))
    st.sweep(first - 2, last + 2, REST + 4, (phi1, conc1), mob, (phi2, conc2))
    start = first - 3
    copies = []
    for piece in range(PIECES):
        at = start + piece * PIECE
        st.sweep(at, at + PIECE, PIECE, (phi2, conc2), mob, (phase_ref, solute_ref), start)
        source = pl.ds(piece * PIECE * FACE, PIECE * FACE)
        target = pl.ds((OUT_FIRST - HALO + piece * PIECE) * FACE, PIECE * FACE)
        for n, (ref, hbm) in enumerate(((phase_ref, phase_hbm), (solute_ref, solute_hbm))):
            copies.append(pltpu.make_async_copy(ref.at[:, source], hbm.at[:, target], sems.at[piece, n]))
            copies[-1].start()
    for copy in copies:
        copy.wait()


SMEM = pl.BlockSpec(memory_space=pltpu.SMEM)
VMEM = pl.BlockSpec(memory_space=pltpu.VMEM)
HBM = pl.BlockSpec(memory_space=pltpu.HBM)
ANY = pl.BlockSpec(memory_space=pl.ANY)
PARAMS = pltpu.CompilerParams(vmem_limit_bytes=32 * 2**20)


def shaped(planes, fields=FIELDS):
    return jax.ShapeDtypeStruct((fields, CAP, planes * FACE), jnp.float32)


def cost(moved, flops=10**6):
    return pl.CostEstimate(flops=flops, bytes_accessed=moved, transcendentals=0)


MB = 2**20


def on_device(old_phase, old_solute, old_mobility, new_global_slot, neighbors):
    count = lax.axis_size("blk")
    here = lax.axis_index("blk").astype(jnp.int32).reshape(1)
    olds = tuple(pltpu.with_memory_space_constraint(x, pltpu.HBM) for x in (old_phase, old_solute, old_mobility))
    devices = range(count)

    def sent(block, route):
        return lax.ppermute(block, "blk", [(p, q) for p, q in route if 0 <= q < count])

    def outward(p):
        return -2 if p % 2 == 0 else 2

    partner = [(p, p ^ 1) for p in devices]
    far_route = [(p, p + outward(p)) for p in devices]
    back_route = [(p, p - outward(p)) for p in devices]

    def after(block, *others):
        return lax.optimization_barrier((block, *others))[0]

    slots_hbm = pltpu.with_memory_space_constraint(new_global_slot, pltpu.HBM)
    old_shape = jax.ShapeDtypeStruct((OLD, CELLS), jnp.float32)
    *olds, merge, final, far_all = pl.pallas_call(
        pack_kernel,
        in_specs=[SMEM, HBM, HBM, HBM, HBM],
        out_specs=[VMEM] * 6,
        out_shape=[old_shape] * 3 + [shaped(EDGE)] * 3,
        scratch_shapes=[pltpu.SMEM((OLD,), jnp.int32), pltpu.SemaphoreType.DMA, pltpu.SemaphoreType.DMA((CHUNKS, FIELDS))],
        compiler_params=PARAMS,
        cost_estimate=cost(6 * MB),
        name="pack",
    )(here, slots_hbm, *olds)
    far_got = sent(far_all, far_route)
    merge_got = sent(merge, partner)
    final_got = sent(final, partner)

    two_parts = [shaped(2 * CHUNK_PLANES), shaped(REST)]
    back_edge, back_rest = pl.pallas_call(
        relay_kernel,
        in_specs=[SMEM, SMEM] + [VMEM] * 4,
        out_specs=[VMEM] * 2,
        out_shape=two_parts,
        compiler_params=PARAMS,
        cost_estimate=cost(6 * MB),
        name="relay",
    )(here, new_global_slot, *olds, merge_got)
    back_edge_got = sent(back_edge, back_route)

    stay_edge, stay_rest = pl.pallas_call(
        stay_kernel,
        in_specs=[SMEM, SMEM] + [VMEM] * 4,
        out_specs=[VMEM] * 2,
        out_shape=two_parts,
        compiler_params=PARAMS,
        cost_estimate=cost(6 * MB),
        name="stay",
    )(here, new_global_slot, *olds, final_got)
    back_rest_got = sent(after(back_rest, back_edge_got, stay_edge), back_route)

    edges = pl.BlockSpec((FIELDS, CAP, 2 * CHUNK), lambda i: (0, 0, 0))
    faces = pl.BlockSpec((len(LOW_PLANES), CAP, FACE), lambda i: (0, 0, 0))
    edge, low, high = pl.pallas_call(
        face_kernel,
        grid=(1,),
        in_specs=[edges] * 3,
        out_specs=[edges, faces, faces],
        out_shape=[shaped(2 * CHUNK_PLANES)] + [shaped(1, len(LOW_PLANES))] * 2,
        compiler_params=PARAMS,
        cost_estimate=cost(3 * MB),
        name="faces",
    )(stay_edge, far_got, back_edge_got)
    below = sent(high, [(p, p + 1) for p in devices])
    above = sent(low, [(p, p - 1) for p in devices])

    state = pltpu.VMEM((EXT, CAP, FACE), jnp.float32)
    whole = jax.ShapeDtypeStruct((CAP, CELLS), jnp.float32)

    def kept(fields, planes):
        return jax.ShapeDtypeStruct((fields, planes, CAP, FACE), jnp.float32)

    phase, solute, kept0, kept1, kept2 = pl.pallas_call(
        edge_kernel,
        in_specs=[SMEM] + [VMEM] * 4,
        out_specs=[HBM] * 2 + [VMEM] * 3,
        out_shape=[whole, whole, kept(3, 6), kept(2, 4), kept(2, 4)],
        scratch_shapes=[state] * 7 + [pltpu.VMEM((CAP, 2 * FACE), jnp.float32)] * 2 + [pltpu.SemaphoreType.DMA((2, 2))],
        compiler_params=PARAMS,
        cost_estimate=cost(8 * MB),
        name="edge_steps",
    )(here, edge, below, above, neighbors)

    state = pltpu.VMEM((MAIN_PLANES, CAP, FACE), jnp.float32)
    rows_out = pltpu.VMEM((CAP, OUT_PLANES * FACE), jnp.float32)
    phase, solute = pl.pallas_call(
        main_kernel,
        in_specs=[SMEM] + [VMEM] * 7 + [HBM] * 2,
        out_specs=[HBM] * 2,
        out_shape=[whole, whole],
        scratch_shapes=[state] * 7 + [rows_out] * 2 + [pltpu.SemaphoreType.DMA((PIECES, 2))],
        input_output_aliases={8: 0, 9: 1},
        compiler_params=PARAMS,
        cost_estimate=cost(20 * MB),
        name="main_steps",
    )(here, stay_rest, far_got, back_rest_got, neighbors, kept0, kept1, kept2, phase, solute)
    return phase, solute


def solution(mesh):
    placed = (P("blk", None), P("blk", None), P("blk", None), P("blk"), P("blk", None))
    return jax.shard_map(
        on_device,
        mesh=mesh,
        in_specs=placed,
        out_specs=(P("blk", None), P("blk", None)),
        check_vma=False,
    )
```
